32 devices in a mesh: dp: 8 (over z, x), seq: 4 (over y, core).
Axes of the slice: x: 2, y: 2, z: 4, core: 2. Of those that a mesh axis runs over, the one named last changes fastest.
Arguments:
- hidden_in: bfloat16 [8, 1024, 768], P('dp', 'seq'), may hold values from -6 to 6
- condition: bfloat16 [8, 256], P('dp'), may hold values from -6 to 6
- qkv_weight: bfloat16 [768, 2304], P('dp'), may hold values from -0.21875 to 0.21875
- out_weight: bfloat16 [768, 768], P('dp'), may hold values from -3.5 to 3.5
- gate_up_weight: bfloat16 [768, 6144], P('dp'), may hold values from -0.21875 to 0.21875
- down_weight: bfloat16 [3072, 768], P('dp'), may hold values from -0.109375 to 0.109375
- ada_weight: bfloat16 [256, 4608], P('dp'), may hold values from -0.375 to 0.375
- pair_embed: bfloat16 [66, 256], replicated, may hold values from -6 to 6
- pair_gain: bfloat16 [256], replicated, may hold values from 0.099609375 to 1.8984375
- pair_weight: bfloat16 [256, 12], replicated, may hold values from -0.375 to 0.375
- valid_len: int32 [8], P('dp'), may hold values from 512 to 1024, as said below
- chain_break: int32 [8], P('dp'), may hold values from 256 to 1535
- out_grad: bfloat16 [8, 1024, 768], P('dp', 'seq'), may hold values from -6 to 6
Outputs:
- result: bfloat16 [8, 1024, 768], P('dp', 'seq')
- input_grad: bfloat16 [8, 1024, 768], P('dp', 'seq')
- grad_qkv: float32 [768, 2304], P('dp')
- grad_out: float32 [768, 768], P('dp')
- grad_gate_up: float32 [768, 6144], P('dp')
- grad_down: float32 [3072, 768], P('dp')
- grad_ada: float32 [256, 4608], P('dp')
- grad_embed: float32 [66, 256], replicated
- grad_gain: float32 [256], replicated
- grad_pair: float32 [256, 12], replicated
The draws below stay inside these ranges and needn't reach their ends.
Inputs may be any that keep to these rules, and one draw needn't show every extreme that they name: Positions from valid_len on are padding keys; in each aligned group of 1 items one item has live residues in the last residue block of the seq axis; the first item has all 1024 residues. Positions from chain_break on form a second chain; a value of 1024 or more means one chain.
All inputs are finite; a program needn't handle non-finite values.
Results may differ from the reference program's by a relative error of at most 0.023.
Values may be sent and summed in bfloat16 or wider, within the bound.
A program may use at most 192 MiB of HBM per device.

```python
import jax
import jax.numpy as jnp
from jax import lax

D = 768
H = 12
DH = 64
FF = 3072
PW = 256
CD = 256
L = 1024
RR = 32
ITEMS_DEV = 1
ITEMS = 8
CLASSES = 66
N_SEQ = 4


def draw_valid_len(key, part):
    key = jax.random.fold_in(key, 11)
    first_key, second_key, third_key = jax.random.split(key, 3)
    groups = ITEMS // ITEMS_DEV
    lengths = jax.random.randint(first_key, (groups, ITEMS_DEV), L // 2, L + 1)
    reaching = jax.random.randint(third_key, (groups, ITEMS_DEV), L - L // N_SEQ + 1, L + 1)
    chosen = jax.random.randint(second_key, (groups, 1), 0, ITEMS_DEV)
    filled = jnp.arange(ITEMS_DEV)[None, :] == chosen
    flat = jnp.where(filled, reaching, lengths).reshape(ITEMS)
    first_item = jnp.arange(ITEMS) == 0
    return jnp.where(first_item, L, flat).astype(jnp.int32)


def place_ends(values, rng, low, top_value):
    index_at = [jax.random.randint(jax.random.fold_in(rng, axis), (), 0, length) for axis, length in enumerate(values.shape)]
    longest = values.shape.index(max(values.shape))
    next_to = index_at[:longest] + [(index_at[longest] + 1) % values.shape[longest]] + index_at[longest + 1:]
    return values.at[tuple(index_at)].set(low).at[tuple(next_to)].set(top_value)


def block_scale(stream_key, shape, shards, least, top_value):
    level = 1.0
    for dim, blocks in shards:
        draws = jax.random.uniform(jax.random.fold_in(jax.random.fold_in(stream_key, 6), dim), (blocks,), jnp.float32, least / len(shards), top_value / len(shards))
        level = level * jnp.repeat(jnp.exp(draws), shape[dim] // blocks).reshape((-1,) + (1,) * (len(shape) - 1 - dim))
    return level


def gaussian(stream_key, shape, deviation, limit, pieces=(), kind=jnp.bfloat16):
    factor_of = block_scale(stream_key, shape, pieces, -0.22, 0.18) if pieces else 1.0
    array = jax.random.normal(stream_key, shape, jnp.float32) * deviation * factor_of
    return jnp.minimum(jnp.maximum(array, -limit), limit).astype(kind)


def setup_inputs(seed: int = 0) -> dict:
    streams_of = jax.random.split(jax.random.key(seed), 14)
    return {
        "hidden_in": gaussian(streams_of[0], (ITEMS, L, D), 1.0, 6.0, ((0, 8), (1, 4))),
        "condition": gaussian(streams_of[1], (ITEMS, CD), 1.0, 6.0, ((0, 8),)),
        "qkv_weight": gaussian(streams_of[2], (D, 3 * D), D ** -0.5, 0.21875, ((0, 8),)),
        "out_weight": gaussian(streams_of[3], (D, D), (4 * D // L) ** -0.5, 3.5, ((0, 8),)),
        "gate_up_weight": gaussian(streams_of[4], (D, 2 * FF), D ** -0.5, 0.21875, ((0, 8),)),
        "down_weight": gaussian(streams_of[5], (FF, D), FF ** -0.5, 0.109375, ((0, 8),)),
        "ada_weight": gaussian(streams_of[6], (CD, 6 * D), CD ** -0.5, 0.375, ((0, 8),)),
        "pair_embed": gaussian(streams_of[7], (CLASSES, PW), 1.0, 6.0),
        "pair_gain": jnp.clip(1.0 + 0.18 * jax.random.normal(streams_of[8], (PW,), jnp.float32), 0.099609375, 1.8984375).astype(jnp.bfloat16),
        "pair_weight": gaussian(streams_of[9], (PW, H), PW ** -0.5, 0.375),
        "valid_len": draw_valid_len(jax.random.fold_in(streams_of[13], 71), 0),
        "chain_break": place_ends(jax.random.randint(streams_of[11], (ITEMS,), L // 4, 3 * L // 2), jax.random.fold_in(streams_of[11], 1), L // 4, (3 * L // 2) - 1).astype(jnp.int32),
        "out_grad": gaussian(streams_of[12], (ITEMS, L, D), 1.0, 6.0, ((0, 8), (1, 4))),
    }


HIGHEST = lax.Precision.HIGHEST

@jax.custom_vjp
def low(v):
    return lax.optimization_barrier(v.astype(jnp.bfloat16)).astype(jnp.float32)

@jax.custom_vjp
def low_back(v):
    return v

def low_keep(v):
    return (low(v), None)

def low_pass(kept, grad):
    return (grad,)

def back_keep(v):
    return (v, None)

def back_low(kept, grad):
    return (low(grad),)
low.defvjp(low_keep, low_pass)
low_back.defvjp(back_keep, back_low)

def normed(values, epsilon):
    average = lax.optimization_barrier(jnp.mean(values, axis=-1, keepdims=True))
    centered = values - average
    return centered * lax.rsqrt(lax.optimization_barrier(jnp.mean(centered * centered, axis=-1, keepdims=True)) + epsilon)

def pair_table(pair_embed, pair_gain, pair_weight):
    return jnp.dot(normed(pair_embed, 1e-05) * pair_gain, pair_weight, precision=HIGHEST)

def pair_classes(position, breaks):
    same_side = (position[:, None] >= breaks) == (position[None, :] >= breaks)
    offset = jnp.clip(position[:, None] - position[None, :], -RR, RR) + RR
    return jnp.where(same_side, offset, 2 * RR + 1).astype(jnp.int32)

def item_block(hidden, modulation, length, breaks, qkv_w, out_w, gate_up_w, down_w, table):
    shift_one, scale_one, gate_one, shift_two, scale_two, gate_two = jnp.split(modulation, 6)
    first = low(normed(hidden, 1e-06) * (1.0 + scale_one) + shift_one)
    merged = low_back(low(jnp.dot(first, qkv_w, precision=HIGHEST)))
    queries, keys, values = jnp.split(merged, 3, axis=-1)
    queries = queries.reshape(L, H, DH)
    keys = keys.reshape(L, H, DH)
    values = values.reshape(L, H, DH)
    position = jnp.arange(L, dtype=jnp.int32)
    classes = pair_classes(position, breaks)
    bias = jnp.transpose(jnp.take(table, classes, axis=0), (2, 0, 1))
    logits = jnp.einsum('qhd,khd->hqk', queries, keys, precision=HIGHEST) * 0.125 + bias
    logits = jnp.where((position < length)[None, None, :], logits, -1e+30)
    weights = jax.nn.softmax(low_back(logits), axis=-1)
    mixed = jnp.einsum('hqk,khd->qhd', low(weights), values, precision=HIGHEST).reshape(L, D)
    mixed = low_back(low(mixed))
    branch = low_back(jnp.dot(mixed, out_w, precision=HIGHEST))
    middle = hidden + gate_one * branch
    second = low(normed(middle, 1e-06) * (1.0 + scale_two) + shift_two)
    gate_up = low_back(jnp.dot(second, gate_up_w, precision=HIGHEST))
    gate_part, up_part = jnp.split(gate_up, 2, axis=-1)
    inner = low(jax.nn.silu(gate_part) * up_part)
    feed = low_back(jnp.dot(inner, down_w, precision=HIGHEST))
    return middle + gate_two * feed

def reference(hidden_in, condition, qkv_weight, out_weight, gate_up_weight, down_weight, ada_weight, pair_embed, pair_gain, pair_weight, valid_len, chain_break, out_grad):
    floats = tuple((a.astype(jnp.float32) for a in (hidden_in, condition, qkv_weight, out_weight, gate_up_weight, down_weight, ada_weight, pair_embed, pair_gain, pair_weight)))

    def forward(hidden, cond, qkv_w, out_w, gate_up_w, down_w, ada_w, embed, gain, proj):
        table = pair_table(embed, gain, proj)
        modulation = jnp.dot(low(jax.nn.silu(cond)), ada_w, precision=HIGHEST)

        def one_item(item):
            return item_block(item[0], item[1], item[2], item[3], qkv_w, out_w, gate_up_w, down_w, table)
        return lax.map(jax.checkpoint(one_item), (hidden, modulation, valid_len, chain_break))
    result, pullback = jax.vjp(forward, *floats)
    grads = pullback(out_grad.astype(jnp.float32))
    return (result.astype(jnp.bfloat16), grads[0].astype(jnp.bfloat16), grads[2], grads[3], grads[4], grads[5], grads[6], grads[7], grads[8], grads[9])
```

```python
import jax
import jax.numpy as jnp
from jax import lax
from jax.sharding import PartitionSpec as P

H = 12
DH = 64
RR = 32
CLASSES = 66

HIGHEST = lax.Precision.HIGHEST
F32 = jnp.float32
BF16 = jnp.bfloat16


def layer_norm(values):
    average = jnp.mean(values, axis=-1, keepdims=True)
    centered = values - average
    inv_std = lax.rsqrt(jnp.mean(centered * centered, axis=-1, keepdims=True) + 1e-06)
    return (centered * inv_std, inv_std)


def norm_back(upstream, normal, inv_std):
    return inv_std * (
        upstream
        - jnp.mean(upstream, axis=-1, keepdims=True)
        - normal * jnp.mean(upstream * normal, axis=-1, keepdims=True)
    )


def pair_table(pair_embed, pair_gain, pair_weight):
    average = jnp.mean(pair_embed, axis=-1, keepdims=True)
    centered = pair_embed - average
    normal = centered * lax.rsqrt(jnp.mean(centered * centered, axis=-1, keepdims=True) + 1e-05)
    return jnp.dot(normal * pair_gain, pair_weight, precision=HIGHEST)


def mm(spec, a, b):
    return jnp.einsum(spec, a, b, preferred_element_type=F32)


def body(
    hidden_in,
    condition,
    qkv_weight,
    out_weight,
    gate_up_weight,
    down_weight,
    ada_weight,
    pair_embed,
    pair_gain,
    pair_weight,
    valid_len,
    chain_break,
    out_grad,
):
    items, rows, width = hidden_in.shape
    seq = lax.axis_size("seq")
    dp = lax.axis_size("dp")
    me = lax.axis_index("seq")
    at = lax.axis_index("dp")
    length = rows * seq
    heads = H // seq
    part = heads * DH
    shard = qkv_weight.shape[0]
    strip = down_weight.shape[0] // seq
    hidden_units = dp * strip

    def pick(array, axis):
        return lax.dynamic_index_in_dim(array, me, axis, keepdims=False)

    def gather(array, name, axis):
        return lax.all_gather(array, name, axis=axis, tiled=True)

    def scatter(array, name, axis):
        return lax.psum_scatter(array, name, scatter_dimension=axis, tiled=True)

    conditions = gather(condition, "dp", 0)
    squashed = jax.nn.silu(conditions.astype(F32)).astype(BF16)
    ada_rows = ada_weight.shape[0]
    squashed_part = lax.dynamic_slice_in_dim(squashed, at * ada_rows, ada_rows, 1)
    modulation = scatter(mm("ic,ce->ie", squashed_part, ada_weight), "dp", 0)
    shift_one, scale_one, gate_one, shift_two, scale_two, gate_two = jnp.split(
        modulation[:, None, :], 6, axis=-1
    )
    qkv_w = gather(pick(qkv_weight.reshape(shard, 3, seq, part), 2).reshape(shard, 3 * part), "dp", 0)
    gate_up_w = gather(
        pick(gate_up_weight.reshape(shard, 2, dp, seq, strip), 3).reshape(shard, 2 * hidden_units), "dp", 0
    )
    down_w = gather(pick(down_weight.reshape(seq, strip, width), 0), "dp", 0)
    out_w = gather(gather(pick(out_weight.reshape(shard, seq, width // seq), 1), "dp", 0), "seq", 1)

    table, pair_pull = jax.vjp(
        pair_table, pair_embed.astype(F32), pair_gain.astype(F32), pair_weight.astype(F32)
    )
    my_table = lax.dynamic_slice_in_dim(table, me * heads, heads, 1)
    spread = jnp.arange(2 * length)
    distance = jnp.where(spread < length, -spread, 2 * length - spread)
    line = jnp.take(my_table, jnp.clip(distance, -RR, RR) + RR, axis=0).T
    toeplitz = jnp.tile(line, (1, length))[:, : length * (2 * length - 1)]
    toeplitz = toeplitz.reshape(heads, length, 2 * length - 1)[:, :, :length]
    positions = jnp.arange(length, dtype=jnp.int32)
    side = positions[None] >= chain_break[:, None]
    same = side[:, :, None] == side[:, None, :]
    alive = (positions[None] < valid_len[:, None])[:, None, None, :]

    hidden = gather(hidden_in, "seq", 1).astype(F32)
    upstream = out_grad.astype(F32)
    first_norm, first_inv = layer_norm(hidden)
    first = (first_norm * (1.0 + scale_one) + shift_one).astype(BF16)
    merged = mm("ird,de->ire", first, qkv_w).astype(BF16)
    queries, keys, values = (
        part_of.reshape(items, length, heads, DH) for part_of in jnp.split(merged, 3, axis=-1)
    )
    logits = mm("iqhd,ikhd->ihqk", queries, keys) * 0.125
    logits = logits + jnp.where(same[:, None], toeplitz[None], my_table[CLASSES - 1][None, :, None, None])
    logits = jnp.where(alive, logits, -1e30)
    powers = jnp.exp(logits - jnp.max(logits, axis=-1, keepdims=True))
    probs = powers / jnp.sum(powers, axis=-1, keepdims=True)
    probs_low = probs.astype(BF16)
    mixed_heads = mm("ihqk,ikhd->iqhd", probs_low, values)
    mixed_part = mixed_heads.reshape(items, length, part).astype(BF16)
    mixed_all = gather(mixed_part, "seq", 2)

    def mine(array):
        return lax.dynamic_slice_in_dim(array, me * rows, rows, 1)

    branch = mm("ire,ed->ird", mine(mixed_all), out_w)
    middle = hidden_in.astype(F32) + gate_one * branch
    second_norm, second_inv = layer_norm(middle)
    second = gather((second_norm * (1.0 + scale_two) + shift_two).astype(BF16), "seq", 1)
    gate_up = mm("ird,de->ire", second, gate_up_w)
    gate_part, up_part = jnp.split(gate_up, 2, axis=-1)
    sigmoid_gate = jax.nn.sigmoid(gate_part)
    inner = (gate_part * sigmoid_gate * up_part).astype(BF16)
    feed = scatter(mm("irf,fd->ird", inner, down_w).astype(BF16), "seq", 1).astype(F32)
    result = (middle + gate_two * feed).astype(BF16)

    feed_grad = (gate_two * gather(out_grad, "seq", 1).astype(F32)).astype(BF16)
    d_gate_two = jnp.sum(upstream * feed, axis=1)
    grad_down = mm("irf,ird->fd", inner, feed_grad)
    inner_grad = mm("ird,fd->irf", feed_grad, down_w)
    gate_grad = inner_grad * up_part * sigmoid_gate * (1.0 + gate_part * (1.0 - sigmoid_gate))
    up_grad = inner_grad * gate_part * sigmoid_gate
    gate_up_grad = jnp.concatenate([gate_grad, up_grad], axis=-1).astype(BF16)
    grad_gate_up = mm("ird,ire->de", second, gate_up_grad)
    second_grad = scatter(mm("ire,de->ird", gate_up_grad, gate_up_w).astype(BF16), "seq", 1).astype(F32)
    d_shift_two = jnp.sum(second_grad, axis=1)
    d_scale_two = jnp.sum(second_grad * second_norm, axis=1)
    middle_grad = upstream + norm_back(second_grad * (1.0 + scale_two), second_norm, second_inv)
    branch_grad = (gate_one * middle_grad).astype(BF16)
    d_gate_one = jnp.sum(middle_grad * branch, axis=1)
    branch_grad_all = gather(branch_grad, "seq", 1)
    my_columns = lax.dynamic_slice_in_dim(branch_grad_all, me * part, part, 2)
    grad_out = mm("ire,ird->ed", mixed_all, my_columns)
    out_w_rows = lax.dynamic_slice_in_dim(out_w, me * part, part, 0)
    mixed_grad = mm("ird,ed->ire", branch_grad_all, out_w_rows).astype(BF16).reshape(items, length, heads, DH)

    prob_grad = mm("iqhd,ikhd->ihqk", mixed_grad, values)
    delta = jnp.sum(probs * prob_grad, axis=-1, keepdims=True)
    score_grad = (probs * (prob_grad - delta)).astype(BF16)
    query_grad = mm("ihqk,ikhd->iqhd", score_grad, keys) * 0.125
    key_grad = mm("ihqk,iqhd->ikhd", score_grad, queries) * 0.125
    value_grad = mm("ihqk,iqhd->ikhd", probs_low, mixed_grad)
    merged_grad = jnp.concatenate(
        [term.reshape(items, length, part) for term in (query_grad, key_grad, value_grad)], axis=-1
    ).astype(BF16)
    wide = score_grad.astype(F32)
    kept = jnp.sum(jnp.where(same[:, None], wide, 0.0), axis=0)
    crossed = jnp.sum(jnp.where(same[:, None], 0.0, wide), axis=(0, 2, 3))
    skewed = jnp.pad(kept[:, :, ::-1], ((0, 0), (0, 0), (0, length))).reshape(heads, -1)
    skewed = skewed[:, : length * (2 * length - 1)].reshape(heads, length, 2 * length - 1)
    lines = jnp.sum(skewed, axis=1)
    middle_line = length - 1
    low_end = jnp.sum(lines[:, : middle_line - RR + 1], axis=1)
    high_end = jnp.sum(lines[:, middle_line + RR :], axis=1)
    near = lines[:, middle_line - RR + 1 : middle_line + RR]
    my_table_grad = jnp.concatenate([low_end[:, None], near, high_end[:, None], crossed[:, None]], axis=1).T
    table_grad = lax.psum(
        lax.dynamic_update_slice_in_dim(jnp.zeros((CLASSES, H), F32), my_table_grad, me * heads, 1), ("dp", "seq")
    )
    grad_embed, grad_gain, grad_pair = pair_pull(table_grad)

    grad_qkv = mm("ird,ire->de", first, merged_grad)
    first_grad = scatter(mm("ire,de->ird", merged_grad, qkv_w).astype(BF16), "seq", 1).astype(F32)
    my_norm, my_inv = mine(first_norm), mine(first_inv)
    d_shift_one = jnp.sum(first_grad, axis=1)
    d_scale_one = jnp.sum(first_grad * my_norm, axis=1)
    input_grad = middle_grad + norm_back(first_grad * (1.0 + scale_one), my_norm, my_inv)
    modulation_grad = jnp.concatenate(
        [d_shift_one, d_scale_one, d_gate_one, d_shift_two, d_scale_two, d_gate_two], axis=-1
    )
    modulation_grads = gather(lax.psum(modulation_grad, "seq"), "dp", 0)
    grad_ada = jnp.einsum("ic,ie->ce", squashed_part.astype(F32), modulation_grads, precision=HIGHEST)

    def owned(grad):
        return scatter(grad.astype(BF16), "dp", 0)

    def everyone(grad):
        return lax.all_gather(grad, "seq", axis=0)

    shares_qkv = everyone(owned(grad_qkv)).reshape(seq, shard, 3, part)
    shares_out = everyone(owned(grad_out))
    shares_gate_up = everyone(owned(grad_gate_up)).reshape(seq, shard, 2, dp, strip)
    shares_down = everyone(owned(grad_down))
    return (
        result,
        input_grad.astype(BF16),
        jnp.transpose(shares_qkv, (1, 2, 0, 3)).reshape(shard, -1).astype(F32),
        jnp.transpose(shares_out, (1, 0, 2)).reshape(shard, -1).astype(F32),
        jnp.transpose(shares_gate_up, (1, 2, 3, 0, 4)).reshape(shard, -1).astype(F32),
        shares_down.reshape(seq * strip, width).astype(F32),
        grad_ada,
        grad_embed,
        grad_gain,
        grad_pair,
    )


def solution(mesh):
    rows = P("dp", "seq", None)
    share = P("dp", None)
    return jax.shard_map(
        body,
        mesh=mesh,
        in_specs=(rows, share, share, share, share, share, share, P(), P(), P(), P("dp"), P("dp"), rows),
        out_specs=(rows, rows, share, share, share, share, share, P(), P(), P()),
        check_vma=False,
    )
```

```python
import functools
import types

import jax
import jax.numpy as jnp
from jax import lax
from jax.experimental import pallas as pl
from jax.experimental.pallas import tpu as pltpu
from jax.sharding import PartitionSpec as P

H = 12
DH = 64
RR = 32
CLASSES = 66

HIGHEST = lax.Precision.HIGHEST
F32 = jnp.float32
BF16 = jnp.bfloat16


VMEM_LIMIT = 65400 * 2**10


def layer_norm(values):
    average = jnp.mean(values, axis=-1, keepdims=True)
    centered = values - average
    inv_std = lax.rsqrt(jnp.mean(centered * centered, axis=-1, keepdims=True) + 1e-06)
    return (centered * inv_std, inv_std)


def norm_back(upstream, normal, inv_std):
    return inv_std * (
        upstream
        - jnp.mean(upstream, axis=-1, keepdims=True)
        - normal * jnp.mean(upstream * normal, axis=-1, keepdims=True)
    )


def pair_table(pair_embed, pair_gain, pair_weight):
    average = jnp.mean(pair_embed, axis=-1, keepdims=True)
    centered = pair_embed - average
    normal = centered * lax.rsqrt(jnp.mean(centered * centered, axis=-1, keepdims=True) + 1e-05)
    return jnp.dot(normal * pair_gain, pair_weight, precision=HIGHEST)


def mm(spec, a, b):
    return jnp.einsum(spec, a, b, preferred_element_type=F32)


def plain_body(
    hidden_in,
    condition,
    qkv_weight,
    out_weight,
    gate_up_weight,
    down_weight,
    ada_weight,
    pair_embed,
    pair_gain,
    pair_weight,
    valid_len,
    chain_break,
    out_grad,
):
    items, rows, width = hidden_in.shape
    seq = lax.axis_size("seq")
    dp = lax.axis_size("dp")
    me = lax.axis_index("seq")
    at = lax.axis_index("dp")
    length = rows * seq
    heads = H // seq
    part = heads * DH
    shard = qkv_weight.shape[0]
    strip = down_weight.shape[0] // seq
    hidden_units = dp * strip

    def pick(array, axis):
        return lax.dynamic_index_in_dim(array, me, axis, keepdims=False)

    def gather(array, name, axis):
        return lax.all_gather(array, name, axis=axis, tiled=True)

    def scatter(array, name, axis):
        return lax.psum_scatter(array, name, scatter_dimension=axis, tiled=True)

    conditions = gather(condition, "dp", 0)
    squashed = jax.nn.silu(conditions.astype(F32)).astype(BF16)
    ada_rows = ada_weight.shape[0]
    squashed_part = lax.dynamic_slice_in_dim(squashed, at * ada_rows, ada_rows, 1)
    modulation = scatter(mm("ic,ce->ie", squashed_part, ada_weight), "dp", 0)
    shift_one, scale_one, gate_one, shift_two, scale_two, gate_two = jnp.split(
        modulation[:, None, :], 6, axis=-1
    )
    qkv_w = gather(pick(qkv_weight.reshape(shard, 3, seq, part), 2).reshape(shard, 3 * part), "dp", 0)
    gate_up_w = gather(
        pick(gate_up_weight.reshape(shard, 2, dp, seq, strip), 3).reshape(shard, 2 * hidden_units), "dp", 0
    )
    down_w = gather(pick(down_weight.reshape(seq, strip, width), 0), "dp", 0)
    out_w = gather(gather(pick(out_weight.reshape(shard, seq, width // seq), 1), "dp", 0), "seq", 1)

    table, pair_pull = jax.vjp(
        pair_table, pair_embed.astype(F32), pair_gain.astype(F32), pair_weight.astype(F32)
    )
    my_table = lax.dynamic_slice_in_dim(table, me * heads, heads, 1)
    spread = jnp.arange(2 * length)
    distance = jnp.where(spread < length, -spread, 2 * length - spread)
    line = jnp.take(my_table, jnp.clip(distance, -RR, RR) + RR, axis=0).T
    toeplitz = jnp.tile(line, (1, length))[:, : length * (2 * length - 1)]
    toeplitz = toeplitz.reshape(heads, length, 2 * length - 1)[:, :, :length]
    positions = jnp.arange(length, dtype=jnp.int32)
    side = positions[None] >= chain_break[:, None]
    same = side[:, :, None] == side[:, None, :]
    alive = (positions[None] < valid_len[:, None])[:, None, None, :]

    hidden = gather(hidden_in, "seq", 1).astype(F32)
    upstream = out_grad.astype(F32)
    first_norm, first_inv = layer_norm(hidden)
    first = (first_norm * (1.0 + scale_one) + shift_one).astype(BF16)
    merged = mm("ird,de->ire", first, qkv_w).astype(BF16)
    queries, keys, values = (
        part_of.reshape(items, length, heads, DH) for part_of in jnp.split(merged, 3, axis=-1)
    )
    logits = mm("iqhd,ikhd->ihqk", queries, keys) * 0.125
    logits = logits + jnp.where(same[:, None], toeplitz[None], my_table[CLASSES - 1][None, :, None, None])
    logits = jnp.where(alive, logits, -1e30)
    powers = jnp.exp(logits - jnp.max(logits, axis=-1, keepdims=True))
    probs = powers / jnp.sum(powers, axis=-1, keepdims=True)
    probs_low = probs.astype(BF16)
    mixed_heads = mm("ihqk,ikhd->iqhd", probs_low, values)
    mixed_part = mixed_heads.reshape(items, length, part).astype(BF16)
    mixed_all = gather(mixed_part, "seq", 2)

    def mine(array):
        return lax.dynamic_slice_in_dim(array, me * rows, rows, 1)

    branch = mm("ire,ed->ird", mine(mixed_all), out_w)
    middle = hidden_in.astype(F32) + gate_one * branch
    second_norm, second_inv = layer_norm(middle)
    second = gather((second_norm * (1.0 + scale_two) + shift_two).astype(BF16), "seq", 1)
    gate_up = mm("ird,de->ire", second, gate_up_w)
    gate_part, up_part = jnp.split(gate_up, 2, axis=-1)
    sigmoid_gate = jax.nn.sigmoid(gate_part)
    inner = (gate_part * sigmoid_gate * up_part).astype(BF16)
    feed = scatter(mm("irf,fd->ird", inner, down_w).astype(BF16), "seq", 1).astype(F32)
    result = (middle + gate_two * feed).astype(BF16)

    feed_grad = (gate_two * gather(out_grad, "seq", 1).astype(F32)).astype(BF16)
    d_gate_two = jnp.sum(upstream * feed, axis=1)
    grad_down = mm("irf,ird->fd", inner, feed_grad)
    inner_grad = mm("ird,fd->irf", feed_grad, down_w)
    gate_grad = inner_grad * up_part * sigmoid_gate * (1.0 + gate_part * (1.0 - sigmoid_gate))
    up_grad = inner_grad * gate_part * sigmoid_gate
    gate_up_grad = jnp.concatenate([gate_grad, up_grad], axis=-1).astype(BF16)
    grad_gate_up = mm("ird,ire->de", second, gate_up_grad)
    second_grad = scatter(mm("ire,de->ird", gate_up_grad, gate_up_w).astype(BF16), "seq", 1).astype(F32)
    d_shift_two = jnp.sum(second_grad, axis=1)
    d_scale_two = jnp.sum(second_grad * second_norm, axis=1)
    middle_grad = upstream + norm_back(second_grad * (1.0 + scale_two), second_norm, second_inv)
    branch_grad = (gate_one * middle_grad).astype(BF16)
    d_gate_one = jnp.sum(middle_grad * branch, axis=1)
    branch_grad_all = gather(branch_grad, "seq", 1)
    my_columns = lax.dynamic_slice_in_dim(branch_grad_all, me * part, part, 2)
    grad_out = mm("ire,ird->ed", mixed_all, my_columns)
    out_w_rows = lax.dynamic_slice_in_dim(out_w, me * part, part, 0)
    mixed_grad = mm("ird,ed->ire", branch_grad_all, out_w_rows).astype(BF16).reshape(items, length, heads, DH)

    prob_grad = mm("iqhd,ikhd->ihqk", mixed_grad, values)
    delta = jnp.sum(probs * prob_grad, axis=-1, keepdims=True)
    score_grad = (probs * (prob_grad - delta)).astype(BF16)
    query_grad = mm("ihqk,ikhd->iqhd", score_grad, keys) * 0.125
    key_grad = mm("ihqk,iqhd->ikhd", score_grad, queries) * 0.125
    value_grad = mm("ihqk,iqhd->ikhd", probs_low, mixed_grad)
    merged_grad = jnp.concatenate(
        [term.reshape(items, length, part) for term in (query_grad, key_grad, value_grad)], axis=-1
    ).astype(BF16)
    wide = score_grad.astype(F32)
    kept = jnp.sum(jnp.where(same[:, None], wide, 0.0), axis=0)
    crossed = jnp.sum(jnp.where(same[:, None], 0.0, wide), axis=(0, 2, 3))
    skewed = jnp.pad(kept[:, :, ::-1], ((0, 0), (0, 0), (0, length))).reshape(heads, -1)
    skewed = skewed[:, : length * (2 * length - 1)].reshape(heads, length, 2 * length - 1)
    lines = jnp.sum(skewed, axis=1)
    middle_line = length - 1
    low_end = jnp.sum(lines[:, : middle_line - RR + 1], axis=1)
    high_end = jnp.sum(lines[:, middle_line + RR :], axis=1)
    near = lines[:, middle_line - RR + 1 : middle_line + RR]
    my_table_grad = jnp.concatenate([low_end[:, None], near, high_end[:, None], crossed[:, None]], axis=1).T
    table_grad = lax.psum(
        lax.dynamic_update_slice_in_dim(jnp.zeros((CLASSES, H), F32), my_table_grad, me * heads, 1), ("dp", "seq")
    )
    grad_embed, grad_gain, grad_pair = pair_pull(table_grad)

    grad_qkv = mm("ird,ire->de", first, merged_grad)
    first_grad = scatter(mm("ire,de->ird", merged_grad, qkv_w).astype(BF16), "seq", 1).astype(F32)
    my_norm, my_inv = mine(first_norm), mine(first_inv)
    d_shift_one = jnp.sum(first_grad, axis=1)
    d_scale_one = jnp.sum(first_grad * my_norm, axis=1)
    input_grad = middle_grad + norm_back(first_grad * (1.0 + scale_one), my_norm, my_inv)
    modulation_grad = jnp.concatenate(
        [d_shift_one, d_scale_one, d_gate_one, d_shift_two, d_scale_two, d_gate_two], axis=-1
    )
    modulation_grads = gather(lax.psum(modulation_grad, "seq"), "dp", 0)
    grad_ada = jnp.einsum("ic,ie->ce", squashed_part.astype(F32), modulation_grads, precision=HIGHEST)

    def owned(grad):
        return scatter(grad.astype(BF16), "dp", 0)

    def everyone(grad):
        return lax.all_gather(grad, "seq", axis=0)

    shares_qkv = everyone(owned(grad_qkv)).reshape(seq, shard, 3, part)
    shares_out = everyone(owned(grad_out))
    shares_gate_up = everyone(owned(grad_gate_up)).reshape(seq, shard, 2, dp, strip)
    shares_down = everyone(owned(grad_down))
    return (
        result,
        input_grad.astype(BF16),
        jnp.transpose(shares_qkv, (1, 2, 0, 3)).reshape(shard, -1).astype(F32),
        jnp.transpose(shares_out, (1, 0, 2)).reshape(shard, -1).astype(F32),
        jnp.transpose(shares_gate_up, (1, 2, 3, 0, 4)).reshape(shard, -1).astype(F32),
        shares_down.reshape(seq * strip, width).astype(F32),
        grad_ada,
        grad_embed,
        grad_gain,
        grad_pair,
    )


MESH = pl.DeviceIdType.MESH
LANES = 128


def nn(a, b):
    return jnp.dot(a, b, preferred_element_type=F32)


def nt(a, b):
    return lax.dot_general(a, b, (((1,), (1,)), ((), ())), preferred_element_type=F32)


def tn(a, b):
    return lax.dot_general(a, b, (((0,), (0,)), ((), ())), preferred_element_type=F32)


def skew(tile, back):
    row = lax.broadcasted_iota(jnp.int32, tile.shape, 0)
    for bit in range(7):
        turn = LANES - (1 << bit) if back else 1 << bit
        tile = jnp.where(((row >> bit) & 1) == 1, pltpu.roll(tile, turn, 1), tile)
    return tile


class Sizes:
    def __init__(self, rows, width, seq, dp, shard, down_shard, ada_rows, conditioning):
        self.rows, self.width, self.seq, self.dp = rows, width, seq, dp
        self.shard, self.ada_rows, self.conditioning = shard, ada_rows, conditioning
        self.strip = down_shard // seq
        self.length = rows * seq
        self.heads = H // seq
        self.part = self.heads * DH
        self.hidden = self.strip * dp
        self.far = dp // 2
        self.half = shard // 2
        self.blocks = self.length // LANES


class Wires:
    def __init__(self, send, recv):
        self.send, self.recv, self.count, self.started = send, recv, 0, []

    def reserve(self, count=1):
        first = self.count
        self.count += count
        return first

    def make(self, number, source, target, device):
        return pltpu.make_async_remote_copy(
            src_ref=source,
            dst_ref=target,
            send_sem=self.send.at[number],
            recv_sem=self.recv.at[number],
            device_id=device,
            device_id_type=MESH,
        )

    def go(self, number, source, target, device):
        copy = self.make(number, source, target, device)
        copy.start()
        self.started.append(copy)
        return copy

    def settle(self, copy):
        copy.wait_send()
        self.started = [other for other in self.started if other is not copy]

    def finish(self):
        for copy in self.started:
            copy.wait_send()
        self.started = []


def layer_kernel(sizes, names, *refs):
    r = types.SimpleNamespace(**dict(zip(names, refs, strict=True)))
    n = sizes
    rows, width, part, heads, length, hid = n.rows, n.width, n.part, n.heads, n.length, n.hidden
    half_rows = rows // 2
    d, s = lax.axis_index("dp"), lax.axis_index("seq")
    z, x = d // 2, lax.rem(d, 2)
    y, c = s // 2, lax.rem(s, 2)
    ox, oy, oc = 1 - x, 1 - y, 1 - c
    at_x = (z * 2 + ox, s)
    at_y = (d, oy * 2 + c)
    at_c = (d, y * 2 + oc)

    def z_plus(k):
        return lax.rem(z + k, n.far)

    def at_z(k):
        return (z_plus(k) * 2 + x, s)

    wires = Wires(r.send_sem, r.recv_sem)
    dp_peers = [(k, e) for k in range(n.far) for e in range(2) if k or e]
    seq_peers = [(1, 0), (0, 1), (1, 1)]

    def dp_peer(k, e):
        xx = lax.rem(x + e, 2)
        return z_plus(k) * 2 + xx, lax.rem(z + n.far - k, n.far) * 2 + xx

    def seq_peer(a, b):
        return lax.rem(y + a, 2) * 2 + lax.rem(c + b, 2)

    barrier = pltpu.get_barrier_semaphore()
    for k, e in dp_peers:
        pl.semaphore_signal(barrier, inc=1, device_id=(dp_peer(k, e)[0], s), device_id_type=MESH)
    for a, b in seq_peers:
        pl.semaphore_signal(barrier, inc=1, device_id=(d, seq_peer(a, b)), device_id_type=MESH)
    pl.semaphore_wait(barrier, len(dp_peers) + len(seq_peers))

    local_count = [0]

    def local(source, target):
        copy = pltpu.make_async_copy(source, target, r.local_sem.at[local_count[0]])
        local_count[0] += 1
        copy.start()
        return copy

    class SeqGather:
        def __init__(self, block):
            self.block, self.first = block, wires.reserve(3)
            self.mine, self.from_y, self.from_c, self.from_yc = s, at_y[1], at_c[1], oy * 2 + oc

        def start(self, source=None):
            mine = self.block(self.mine)
            source = mine if source is None else source
            self.sent = [wires.go(self.first, source, mine, at_y), wires.go(self.first + 1, source, mine, at_c)]

        def hand_on(self):
            place = self.block(self.from_y)
            wires.make(self.first, place, place, at_y).wait_recv()
            self.sent.append(wires.go(self.first + 2, place, place, at_c))

        def settle(self):
            for copy in self.sent:
                wires.settle(copy)

        def wait_core(self):
            place = self.block(self.from_c)
            wires.make(self.first + 1, place, place, at_c).wait_recv()

        def wait_last(self):
            place = self.block(self.from_yc)
            wires.make(self.first + 2, place, place, at_c).wait_recv()

        def wait(self):
            self.hand_on()
            self.wait_core()
            self.wait_last()

    class DpGather:
        def __init__(self, source, place):
            self.source, self.place, self.first = source, place, wires.reserve(2 * n.far - 1)

        def start(self):
            mine = self.place(d)
            self.own = local(self.source, mine)
            for k in range(1, n.far):
                wires.go(self.first + k - 1, self.source, mine, at_z(k))
            wires.go(self.first + n.far - 1, self.source, mine, at_x)

        def hand_on(self):
            for k in range(1, n.far):
                place = self.place(dp_peer(k, 0)[1])
                wires.make(self.first + k - 1, place, place, at_z(k)).wait_recv()
                wires.go(self.first + n.far - 1 + k, place, place, at_x)

        def wait(self):
            self.own.wait()
            for k in range(n.far):
                place = self.place(dp_peer(k, 1)[1])
                wires.make(self.first + n.far - 1 + k, place, place, at_x).wait_recv()

    class SeqReduce:
        def __init__(self, sib, got, over, come):
            self.sib, self.got, self.over, self.come = sib, got, over, come
            self.first, self.sent = wires.reserve(3), []

        def put_core(self, index):
            def put(lanes, block):
                self.sib[index, :, lanes] = block.astype(BF16)

            return put

        def to_core(self, index):
            self.sent.append(wires.go(self.first + index, self.sib.at[index], self.got.at[index], at_c))

        def wait_far(self):
            wires.make(self.first + 1, self.sib.at[1], self.got.at[1], at_c).wait_recv()

        def put_y(self):
            def put(lanes, block):
                self.over[:, lanes] = (block + self.got[1, :, lanes].astype(F32)).astype(BF16)

            return put

        def to_y(self):
            self.sent.append(wires.go(self.first + 2, self.over, self.come, at_y))

        def settle(self):
            for copy in self.sent:
                wires.settle(copy)

        def wait(self):
            wires.make(self.first, self.sib.at[0], self.got.at[0], at_c).wait_recv()
            wires.make(self.first + 2, self.over, self.come, at_y).wait_recv()

        def total(self, own, place):
            return own[place, :] + self.got[0, place, :].astype(F32) + self.come[place, :].astype(F32)

    class DpReduce:
        def __init__(self, grad, got, come, mine, share):
            self.grad, self.got, self.come, self.mine, self.share = grad, got, come, mine, share
            self.first, self.second = wires.reserve(n.far), wires.reserve(n.far)
            self.gather = SeqGather(lambda t: self.share.at[t])

        def start(self):
            for k in (*range(1, n.far), 0):
                to = z_plus(k)
                wires.go(self.first + k, self.grad.at[ox, to], self.got.at[to], at_x)

        def along_z(self, k):
            to = z_plus(k)
            wires.make(self.first + k, self.grad.at[ox, to], self.got.at[to], at_x).wait_recv()
            self.grad[x, to] = (self.grad[x, to].astype(F32) + self.got[to].astype(F32)).astype(BF16)
            if k:
                wires.go(self.second + k, self.grad.at[x, to], self.come.at[k - 1], at_z(k))

        def finish(self):
            total = self.grad[x, z].astype(F32)
            for k in range(1, n.far):
                wires.make(self.second + k, self.grad.at[x, z], self.come.at[k - 1], at_z(k)).wait_recv()
                total = total + self.come[k - 1].astype(F32)
            self.mine[...] = total.astype(BF16)
            self.own = local(self.mine, self.share.at[s])
            self.gather.start(self.mine)

        def hand_on(self):
            self.gather.hand_on()

        def wait(self):
            self.gather.wait_core()
            self.gather.wait_last()
            self.own.wait()

    step = 32

    def by_rows(count, work, start=0, unroll=2):
        def one(q, carry):
            return work(pl.ds(pl.multiple_of(q * step, step), step), carry)

        return lax.fori_loop(0, count // step, one, start, unroll=unroll)

    wide = 2 * LANES

    def by_lanes(count, work):
        def one(q, _):
            work(pl.ds(pl.multiple_of(q * wide, wide), wide))
            return 0

        lax.fori_loop(0, count // wide, one, 0)

    def fold_rows(array):
        return jnp.sum(array.reshape(step // 8, 8, width), axis=0)

    hidden_all, grads_all = r.hidden_all, r.grads_all

    def rows_of(ref):
        return lambda t: ref.at[pl.ds(pl.multiple_of(t * rows, rows), rows)]

    hidden_gather, up_gather = SeqGather(rows_of(hidden_all)), SeqGather(rows_of(grads_all))
    qkv_gather = DpGather(
        r.qkv, lambda t: r.w_qkv.at[pl.ds(pl.multiple_of(t * n.shard, n.shard), n.shard)]
    )
    pieces = [
        DpGather(
            r.gate_up.at[:, pl.ds(q * (hid // 2), hid // 2)],
            lambda t, q=q: r.w_gate_up.at[
                pl.ds(pl.multiple_of(t * n.shard, n.shard), n.shard), pl.ds(q * (hid // 2), hid // 2)
            ],
        )
        for q in range(4)
    ]
    pieces.append(
        DpGather(r.down, lambda t: r.w_down.at[pl.ds(pl.multiple_of(t * n.strip, n.strip), n.strip)])
    )
    lanes_y = pl.ds(pl.multiple_of(y * (width // 2), width // 2), width // 2)
    out_gather = DpGather(r.out, lambda t: r.w_out.at[t, c, :, lanes_y])
    pieces.insert(2, out_gather)

    def out_block(t):
        ty, tc = t // 2, lax.rem(t, 2)
        return r.w_out.at[:, tc, :, pl.ds(pl.multiple_of(ty * (width // 2), width // 2), width // 2)]

    out_share = SeqGather(out_block)

    cond_first, mod_first = wires.reserve(len(dp_peers)), wires.reserve(len(dp_peers))
    cond_all, mod_send, mod_recv = r.cond_all, r.mod_send, r.mod_recv
    own_cond = local(r.condition, cond_all.at[d])
    for i, (k, e) in enumerate(dp_peers):
        wires.go(cond_first + i, r.condition, cond_all.at[d], (dp_peer(k, e)[0], s))
    own_hidden = local(r.hidden, hidden_gather.block(s))
    keep_hidden = local(r.hidden, r.hidden_own)
    keep_grads = local(r.out_grad, r.upstream)
    hidden_gather.start(r.hidden)
    qkv_gather.start()
    own_grads = local(r.out_grad, up_gather.block(s))

    own_cond.wait()
    for i, (k, e) in enumerate(dp_peers):
        place = cond_all.at[dp_peer(k, e)[1]]
        wires.make(cond_first + i, place, place, (dp_peer(k, e)[0], s)).wait_recv()
    item_of = lax.broadcasted_iota(jnp.int32, (n.dp, n.conditioning), 0)
    conditions = jnp.where(item_of == 0, cond_all[0], 0.0)
    for i in range(1, n.dp):
        conditions = jnp.where(item_of == i, cond_all[i], conditions)
    squashed = (conditions * (1.0 / (1.0 + jnp.exp(-conditions)))).astype(BF16).astype(F32)
    r.squashed[...] = squashed.T
    squashed_rows = r.squashed[pl.ds(pl.multiple_of(d * n.ada_rows, n.ada_rows), n.ada_rows), :]
    ada_part = tn(squashed_rows.astype(BF16), r.ada[...])
    for i in range(n.dp):
        mod_send[i] = ada_part[i : i + 1]
    mod_recv[d] = mod_send[d]
    for i, (k, e) in enumerate(dp_peers):
        wires.go(mod_first + i, mod_send.at[dp_peer(k, e)[0]], mod_recv.at[d], (dp_peer(k, e)[0], s))
    pieces[0].start()
    hidden_gather.hand_on()
    up_gather.start(r.out_grad)
    qkv_gather.hand_on()
    pieces[1].start()

    bias, lines = r.bias, r.lines
    key_in = lax.broadcasted_iota(jnp.int32, (LANES, LANES), 0)
    query_in = lax.broadcasted_iota(jnp.int32, (LANES, LANES), 1)
    middle_tile = n.blocks - 1

    def build_bias(h, _):
        line = lines[h]
        near = skew(jnp.broadcast_to(line[:, :LANES], (LANES, LANES)), False)
        low_end = jnp.broadcast_to(line[:, LANES : LANES + 1], (LANES, LANES))
        high_end = jnp.broadcast_to(line[:, LANES + 1 : LANES + 2], (LANES, LANES))
        for tile in range(2 * n.blocks - 1):
            away = tile - middle_tile
            apart = query_in - key_in - away * LANES
            if away < -1:
                value = high_end
            elif away > 1:
                value = low_end
            else:
                value = jnp.where(apart >= RR, high_end, jnp.where(apart <= -RR, low_end, near))
            bias[h, tile * LANES : (tile + 1) * LANES] = value
        return 0

    lax.fori_loop(0, heads, build_bias, 0)

    own_hidden.wait()
    hidden_gather.wait_core()
    hidden_gather.wait_last()
    for i, (k, e) in enumerate(dp_peers):
        place = mod_recv.at[dp_peer(k, e)[1]]
        wires.make(mod_first + i, mod_send.at[d], place, (dp_peer(k, e)[0], s)).wait_recv()
    modulation = mod_recv[0]
    for i in range(1, n.dp):
        modulation = modulation + mod_recv[i]
    r.modulation[...] = modulation

    def vector(index):
        return r.modulation[:, index * width : (index + 1) * width]

    shift_one, scale_one, gate_one, shift_two, scale_two, gate_two = range(6)
    first = hidden_all
    hidden_gather.settle()

    def make_first(place, _):
        normal, _ = layer_norm(hidden_all[place, :].astype(F32))
        first[place, :] = (normal * (1.0 + vector(scale_one)) + vector(shift_one)).astype(BF16)
        return 0

    by_rows(length, make_first)

    qkv_gather.wait()
    w_qkv = r.w_qkv
    keys, values, queries = r.keys, r.values, r.queries
    keys_t, values_t, queries_t = r.keys_t, r.values_t, r.queries_t
    w_qkv_t = r.inner_t

    def turn_weight(q, _):
        place = pl.ds(pl.multiple_of(q * 2 * LANES, 2 * LANES), 2 * LANES)
        w_qkv_t[0 : 3 * part, place] = w_qkv[place, :].T
        return 0

    lax.fori_loop(0, width // (2 * LANES), turn_weight, 0)

    def project(t, _):
        place = pl.ds(pl.multiple_of(t * rows, rows), rows)
        block = first[place, :]
        for low in range(0, 3 * part, wide):
            merged = nn(block, w_qkv[:, low : min(low + wide, 3 * part)]).astype(BF16)
            for q in range(merged.shape[1] // DH):
                kind, h = divmod(low // DH + q, heads)
                column = merged[:, q * DH : (q + 1) * DH]
                if kind == 0:
                    column = (column.astype(F32) * 0.125).astype(BF16)
                (queries, keys, values)[kind][h, place, :] = column
        for kind, target in enumerate((queries_t, keys_t, values_t)):
            merged_t = nt(w_qkv_t[kind * part : (kind + 1) * part, 0:width], block).astype(BF16)
            if kind == 0:
                merged_t = (merged_t.astype(F32) * 0.125).astype(BF16)
            for h in range(heads):
                target[h, t] = merged_t[h * DH : (h + 1) * DH]
        return 0

    lax.fori_loop(0, n.seq, project, 0)

    valid, broken = r.valid_len[0], r.chain_break[0]
    exps, outs_t, inverse = r.exps, r.outs_t, r.inverse
    tiles = rows // LANES
    order = [oy * 2 + c, oy * 2 + oc, y * 2 + oc, s]

    raw = r.raw

    def tile_parts(t, tile):
        number = t * tiles + tile
        query_side = number * LANES + lax.broadcasted_iota(jnp.int32, (1, LANES), 1) >= broken
        for q in range(n.blocks):
            key_pos = q * LANES + lax.broadcasted_iota(jnp.int32, (LANES, LANES), 0)
            strip = pl.ds(pl.multiple_of((n.blocks - 1 + q - number) * LANES, LANES), LANES)
            yield slice(q * LANES, (q + 1) * LANES), strip, key_pos, (key_pos >= broken) == query_side

    def eights(array):
        return array.reshape(LANES // 8, 8, LANES)

    def attend(t):
        def one_head(h, _):
            for q in range(n.seq):
                place = slice(q * rows, (q + 1) * rows)
                raw[place, :] = nn(keys[h, place, :], queries_t[h, t])
            for tile in range(tiles):
                lanes = slice(tile * LANES, (tile + 1) * LANES)
                far_side = jnp.broadcast_to(lines[h][:, LANES + 2 : LANES + 3], (1, LANES))
                top = jnp.full((8, LANES), -1e30, F32)
                for place, strip, key_pos, same in tile_parts(t, tile):
                    logits = raw[place, lanes] + jnp.where(same, bias[h, strip, :], far_side)
                    logits = jnp.where(key_pos < valid, logits, -1e30)
                    raw[place, lanes] = logits
                    top = jnp.maximum(top, jnp.max(eights(logits), axis=0))
                top = jnp.max(top, axis=0, keepdims=True)
                total = jnp.zeros((8, LANES), F32)
                for q in range(n.blocks):
                    place = slice(q * LANES, (q + 1) * LANES)
                    powers = jnp.exp(raw[place, lanes] - top)
                    total = total + jnp.sum(eights(powers), axis=0)
                    exps[h, t, place, lanes] = powers.astype(BF16)
                inverse[h, t, :, lanes] = 1.0 / jnp.sum(total, axis=0, keepdims=True)
            values_wide = jnp.concatenate([values_t[h, q] for q in range(n.seq)], axis=1)
            outs_t[h, t] = nn(values_wide, exps[h, t]) * inverse[h, t]
            return 0

        lax.fori_loop(0, heads, one_head, 0)

    mixed_first = wires.reserve(3)
    mixed_send, mixed_recv = r.mixed_send, r.mixed_recv
    mixed_sent = []
    to_send = [at_y, (d, oy * 2 + oc), at_c]
    for i, t in enumerate(order):
        attend(t)
        block = jnp.concatenate([outs_t[h, t] for h in range(heads)], axis=0).T.astype(BF16)
        if i < 3:
            mixed_send[i] = block
            mixed_sent.append(wires.go(mixed_first + i, mixed_send.at[i], mixed_recv.at[s], to_send[i]))
        else:
            mixed_recv[s] = block
        pieces[i].hand_on()
        pieces[i + 2].start()
    up_gather.hand_on()

    out_gather.wait()
    out_share.start()
    out_share.wait()

    def w_out(q, lanes=slice(None)):
        shards = part // n.shard
        block = r.w_out[q * shards : (q + 1) * shards, :, :, lanes]
        return block.reshape(part, block.shape[-1])

    for i in range(3):
        place = mixed_recv.at[order[i]]
        wires.make(mixed_first + i, mixed_send.at[i], place, to_send[i]).wait_recv()
    keep_hidden.wait()

    def make_branch(lanes):
        branch = nn(mixed_recv[0], w_out(0, lanes))
        for q in range(1, n.seq):
            branch = branch + nn(mixed_recv[q], w_out(q, lanes))
        r.branch[:, lanes] = branch

    by_lanes(width, make_branch)
    second_all = r.second_all
    second_gather = SeqGather(rows_of(second_all))

    def make_second(place, _):
        middle = r.hidden_own[place, :].astype(F32) + vector(gate_one) * r.branch[place, :]
        r.middle[place, :] = middle
        normal, _ = layer_norm(middle)
        r.branch_grad[place, :] = (normal * (1.0 + vector(scale_two)) + vector(shift_two)).astype(BF16)
        return 0

    by_rows(rows, make_second)
    second_all[pl.ds(pl.multiple_of(s * rows, rows), rows), :] = r.branch_grad[...]
    second_gather.start()
    pieces[4].hand_on()

    own_grads.wait()
    up_gather.wait_core()
    up_gather.wait_last()
    up_gather.settle()
    feed_grads = grads_all

    def make_feed_grads(place, _):
        feed_grads[place, :] = (vector(gate_two) * grads_all[place, :].astype(F32)).astype(BF16)
        return 0

    by_rows(length, make_feed_grads)
    pieces[5].hand_on()
    for piece in pieces:
        if piece is not out_gather:
            piece.wait()
    second_gather.hand_on()
    w_gate_up, w_down = r.w_gate_up, r.w_down
    inner, inner_t, gate_up_grads, second_t = r.inner, r.inner_t, r.gate_up_grads, r.second_t
    feed_places = (r.feed_sib, r.feed_got, r.feed_over, r.feed_come)
    feed_reduce = SeqReduce(*feed_places)
    second_reduce = SeqReduce(r.second_sib, r.second_got, r.second_over, r.second_come)

    def feed_forward(t, put_second, put_feed):
        place = pl.ds(pl.multiple_of(t * rows, rows), rows)
        lanes_t = pl.ds(pl.multiple_of(t * rows, rows), rows)
        block = second_all[place, :]
        second_t[:, lanes_t] = block.T
        given = feed_grads[place, :]

        def units(q, _):
            low = pl.multiple_of(q * wide, wide)
            gates, ups, inner_grads = raw.at[0:rows], raw.at[rows : 2 * rows], raw.at[2 * rows : 3 * rows]
            gates[...] = nn(block, w_gate_up[:, pl.ds(low, wide)])
            ups[...] = nn(block, w_gate_up[:, pl.ds(low + hid, wide)])
            inner_grads[...] = nt(given, w_down[pl.ds(low, wide), :])
            for part_of in range(rows // step):
                few = slice(part_of * step, (part_of + 1) * step)
                gate, up, inner_grad = gates[few, :], ups[few, :], inner_grads[few, :]
                sigmoid = 1.0 / (1.0 + jnp.exp(-gate))
                silu = gate * sigmoid
                inner[few, pl.ds(low, wide)] = (silu * up).astype(BF16)
                to = pl.ds(pl.multiple_of(t * rows + part_of * step, step), step)
                gate_up_grads[to, pl.ds(low, wide)] = (
                    inner_grad * up * sigmoid * (1.0 + gate * (1.0 - sigmoid))
                ).astype(BF16)
                gate_up_grads[to, pl.ds(low + hid, wide)] = (inner_grad * silu).astype(BF16)
            inner_t[pl.ds(low, wide), lanes_t] = inner[:, pl.ds(low, wide)].T
            return 0

        lax.fori_loop(0, hid // wide, units, 0)
        by_lanes(width, lambda lanes: put_second(lanes, nt(gate_up_grads[place, :], w_gate_up[lanes, :])))
        by_lanes(width, lambda lanes: put_feed(lanes, nn(inner[...], w_down[:, lanes])))

    def put_in(ref):
        def put(lanes, block):
            ref[:, lanes] = block.astype(ref.dtype)

        return put

    feed_forward(s, put_in(r.second_own), put_in(r.feed_own))
    second_gather.wait_core()
    feed_forward(y * 2 + oc, second_reduce.put_core(0), feed_reduce.put_core(0))
    second_reduce.to_core(0)
    feed_reduce.to_core(0)
    second_gather.wait_last()
    feed_forward(oy * 2 + oc, second_reduce.put_core(1), feed_reduce.put_core(1))
    second_reduce.to_core(1)
    feed_reduce.to_core(1)
    second_reduce.wait_far()
    feed_reduce.wait_far()
    feed_forward(oy * 2 + c, second_reduce.put_y(), feed_reduce.put_y())
    second_reduce.to_y()
    feed_reduce.to_y()

    gate_up_reduce = DpReduce(r.gate_up_grad, r.gate_up_got, r.gate_up_come, r.gate_up_mine, r.gate_up_share)
    down_reduce = DpReduce(r.down_grad, r.down_got, r.down_come, r.down_mine, r.down_share)
    out_reduce = DpReduce(r.proj_grad, r.proj_got, r.proj_come, r.proj_mine, r.proj_share)
    qkv_reduce = DpReduce(r.qkv_grad, r.qkv_got, r.qkv_come, r.qkv_mine, r.qkv_share)

    def weight_grad(left_t, right, reduce, columns, step):
        def block(q, _):
            low = pl.multiple_of(q * step, step)
            height = reduce.grad.shape[2]
            few = n.dp // 2
            for first_of in range(0, n.dp, few):
                grad = nn(left_t[first_of * height : (first_of + few) * height, :], right[:, pl.ds(low, step)]).astype(BF16)
                for i in range(few):
                    to = first_of + i
                    reduce.grad[to % 2, to // 2, :, pl.ds(low, step)] = grad[i * height : (i + 1) * height]
            return 0

        lax.fori_loop(0, columns // step, block, 0)

    weight_grad(second_t, gate_up_grads, gate_up_reduce, 2 * hid, wide)
    gate_up_reduce.start()
    weight_grad(inner_t, feed_grads, down_reduce, width, wide)
    down_reduce.start()
    lax.fori_loop(0, width // (2 * LANES), turn_weight, 0)

    sums = r.mod_sums

    upstream = r.upstream
    keep_grads.wait()
    second_reduce.wait()
    kept_middle_grad, branch_grad = r.second_own, r.branch_grad
    empty = jnp.zeros((8, width), F32)

    def put_sum(index, array):
        sums[s, :, index * width : (index + 1) * width] = jnp.sum(array, axis=0, keepdims=True)

    def second_back(place, carry):
        second_grad = second_reduce.total(r.second_own, place)
        normal, inverted = layer_norm(r.middle[place, :])
        middle_grad = upstream[place, :].astype(F32) + norm_back(
            second_grad * (1.0 + vector(scale_two)), normal, inverted
        )
        kept_middle_grad[place, :] = middle_grad
        branch_grad[place, :] = (vector(gate_one) * middle_grad).astype(BF16)
        terms = (second_grad, second_grad * normal, middle_grad * r.branch[place, :])
        return tuple(total + fold_rows(term) for total, term in zip(carry, terms))

    for index, total in zip(
        (shift_two, scale_two, gate_one), by_rows(rows, second_back, (empty, empty, empty))
    ):
        put_sum(index, total)
    back_first = wires.reserve(3)
    for copy in mixed_sent:
        wires.settle(copy)
    back_all, back_recv = mixed_send, r.back_recv
    for q in range(n.seq):
        back_all[q] = nt(branch_grad[...], w_out(q)).astype(BF16)
    for i in range(3):
        wires.go(back_first + i, back_all.at[order[i]], back_recv.at[s], to_send[i])
    back_recv[s] = back_all[s]

    out_first = wires.reserve(2)
    second_gather.settle()
    out_parts, quarter = second_all, n.dp * n.half

    def make_out_grad(lanes):
        for q in range(n.seq):
            grad = tn(mixed_recv[q], branch_grad[:, lanes]).astype(BF16)
            for i in range(part // n.half):
                number = q * (part // n.half) + i
                low = (number % 2) * quarter + (number // 2) * n.half
                out_parts[low : low + n.half, lanes] = grad[i * n.half : (i + 1) * n.half]

    by_lanes(width, make_out_grad)

    feed_reduce.wait()

    def make_result(place, total):
        feed = feed_reduce.total(r.feed_own, place)
        r.result[place, :] = (r.middle[place, :] + vector(gate_two) * feed).astype(BF16)
        return total + fold_rows(upstream[place, :].astype(F32) * feed)

    put_sum(gate_two, by_rows(rows, make_result, empty))

    def out_rows(core):
        return out_parts.at[pl.ds(pl.multiple_of(core * quarter, quarter), quarter)]

    wires.go(out_first, out_rows(oc), r.out_near, at_c)
    lanes_oy = pl.ds(pl.multiple_of(oy * (width // 2), width // 2), width // 2)

    def out_cores():
        wires.make(out_first, out_rows(oc), r.out_near, at_c).wait_recv()
        mine = out_parts[pl.ds(pl.multiple_of(c * quarter, quarter), quarter), :]
        r.out_near[...] = (r.out_near[...].astype(F32) + mine.astype(F32)).astype(BF16)
        wires.go(out_first + 1, r.out_near.at[:, lanes_oy], r.out_far, at_y)

    def out_sum():
        wires.make(out_first + 1, r.out_near.at[:, lanes_oy], r.out_far, at_y).wait_recv()
        total = (r.out_near[:, lanes_y].astype(F32) + r.out_far[...].astype(F32)).astype(BF16)
        for to in range(n.dp):
            r.proj_grad[to % 2, to // 2] = total[to * n.half : (to + 1) * n.half]
        out_reduce.start()

    dots, dots_t, delta = r.dots, r.dots_t, r.delta
    pair_grads, query_grads = r.pair_grads, r.query_grads
    bias[...] = jnp.zeros_like(bias)
    pair_grads[...] = jnp.zeros_like(pair_grads)
    crossed, score_grad = r.crossed, r.score_grad
    crossed[...] = jnp.zeros_like(crossed)

    def attend_back(t):
        given_t = back_recv[t].T.astype(F32)
        for h in range(heads):
            scaled = (given_t[h * DH : (h + 1) * DH] * inverse[h, t]).astype(BF16)
            dots_t[h] = scaled
            dots[h] = scaled.T
            delta[h] = jnp.sum(scaled.astype(F32) * outs_t[h, t], axis=0, keepdims=True)
        place = pl.ds(pl.multiple_of(t * rows, rows), rows)

        def one_head(h, _):
            for q in range(n.seq):
                some = slice(q * rows, (q + 1) * rows)
                raw[some, :] = nn(values[h, some, :], dots_t[h])
            for tile in range(tiles):
                lanes = slice(tile * LANES, (tile + 1) * LANES)
                across = jnp.zeros((8, LANES), F32)
                for keys_of, strip, _, same in tile_parts(t, tile):
                    grad = exps[h, t, keys_of, lanes].astype(F32) * (raw[keys_of, lanes] - delta[h, :, lanes])
                    kept = jnp.where(same, grad, 0.0)
                    bias[h, strip, :] = bias[h, strip, :] + kept
                    across = across + jnp.sum(eights(grad - kept), axis=0)
                    score_grad[keys_of, lanes] = grad.astype(BF16)
                crossed[h] = crossed[h] + jnp.sum(across, axis=0, keepdims=True)
            keys_wide = jnp.concatenate([keys_t[h, q] for q in range(n.seq)], axis=1)
            query_grads[h, place, :] = (nn(keys_wide, score_grad[...]) * 0.125).T.astype(BF16)
            for q in range(n.seq):
                some = slice(q * rows, (q + 1) * rows)
                pair_grads[h, some, :] = pair_grads[h, some, :] + jnp.concatenate(
                    [nn(score_grad[some, :], queries[h, place, :]), nn(exps[h, t, some, :], dots[h])], axis=1
                )
            return 0

        lax.fori_loop(0, heads, one_head, 0)

    gate_up_reduce.along_z(1)
    attend_back(order[3])
    gate_up_reduce.along_z(2)
    out_cores()
    wires.make(back_first + 2, back_recv.at[order[2]], back_recv.at[order[2]], to_send[2]).wait_recv()
    attend_back(order[2])
    gate_up_reduce.along_z(3)
    out_sum()
    wires.make(back_first, back_recv.at[order[0]], back_recv.at[order[0]], to_send[0]).wait_recv()
    attend_back(order[0])
    gate_up_reduce.along_z(0)
    down_reduce.along_z(1)
    wires.make(back_first + 1, back_recv.at[order[1]], back_recv.at[order[1]], to_send[1]).wait_recv()
    attend_back(order[1])
    down_reduce.along_z(2)

    feed_reduce.settle()
    first_reduce = SeqReduce(*feed_places)
    merged_grads = gate_up_grads

    def first_part(t, put):
        place = pl.ds(pl.multiple_of(t * rows, rows), rows)
        merged = jnp.concatenate(
            [query_grads[h, place, :] for h in range(heads)]
            + [pair_grads[h, place, 0:DH].astype(BF16) for h in range(heads)]
            + [pair_grads[h, place, DH : 2 * DH].astype(BF16) for h in range(heads)],
            axis=1,
        )
        merged_grads[place, 0 : 3 * part] = merged
        by_lanes(width, lambda lanes: put(lanes, nn(merged_grads[place, 0 : 3 * part], w_qkv_t[0 : 3 * part, lanes])))

    first_part(oy * 2 + oc, first_reduce.put_core(1))
    first_reduce.to_core(1)
    first_part(y * 2 + oc, first_reduce.put_core(0))
    first_reduce.to_core(0)
    first_reduce.wait_far()
    first_part(oy * 2 + c, first_reduce.put_y())
    first_reduce.to_y()
    first_part(s, put_in(r.feed_own))

    def turn_first(t, _):
        place = pl.ds(pl.multiple_of(t * rows, rows), rows)
        second_t[:, place] = first[place, :].T
        return 0

    lax.fori_loop(0, n.seq, turn_first, 0)

    def qkv_grad(q, _):
        low = pl.multiple_of(q * 2 * n.shard, 2 * n.shard)
        grad = nn(second_t[pl.ds(low, 2 * n.shard), :], merged_grads[:, 0 : 3 * part]).astype(BF16)
        qkv_reduce.grad[0, q] = grad[: n.shard]
        qkv_reduce.grad[1, q] = grad[n.shard :]
        return 0

    lax.fori_loop(0, n.far, qkv_grad, 0)
    qkv_reduce.start()
    for k in (3, 0):
        down_reduce.along_z(k)

    table_sums, table_all = r.table_sums, r.table_all

    def fold(h, _):
        lane = lax.broadcasted_iota(jnp.int32, (1, LANES), 1)
        near = jnp.zeros((LANES, LANES), F32)
        low_end = jnp.zeros((LANES, LANES), F32)
        high_end = jnp.zeros((LANES, LANES), F32)
        for tile in range(2 * n.blocks - 1):
            away = tile - middle_tile
            apart = query_in - key_in - away * LANES
            value = bias[h, tile * LANES : (tile + 1) * LANES]
            if away < -1:
                high_end = high_end + value
            elif away > 1:
                low_end = low_end + value
            else:
                high_end = high_end + jnp.where(apart >= RR, value, 0.0)
                low_end = low_end + jnp.where(apart <= -RR, value, 0.0)
                near = near + jnp.where((apart < RR) & (apart > -RR), value, 0.0)
        line = jnp.sum(skew(near, True), axis=0, keepdims=True)
        for where, array in ((40, low_end), (41, high_end), (42, crossed[h])):
            line = jnp.where(lane == where, jnp.sum(array), line)
        table_sums[d, h] = line
        return 0

    lax.fori_loop(0, heads, fold, 0)
    table_first = wires.reserve(len(dp_peers))
    for i, (k, e) in enumerate(dp_peers):
        wires.go(table_first + i, table_sums.at[d], table_sums.at[d], (dp_peer(k, e)[0], s))

    first_reduce.wait()

    def first_back(place, carry):
        first_grad = first_reduce.total(r.feed_own, place)
        normal, inverted = layer_norm(r.hidden_own[place, :].astype(F32))
        r.input_grad[place, :] = (
            kept_middle_grad[place, :] + norm_back(first_grad * (1.0 + vector(scale_one)), normal, inverted)
        ).astype(BF16)
        return tuple(total + fold_rows(term) for total, term in zip(carry, (first_grad, first_grad * normal)))

    for index, total in zip((shift_one, scale_one), by_rows(rows, first_back, (empty, empty))):
        put_sum(index, total)
    sums_first = wires.reserve(3)
    for i, (a, b) in enumerate(seq_peers):
        wires.go(sums_first + i, sums.at[s], sums.at[s], (d, seq_peer(a, b)))
    for k in (1, 2, 3, 0):
        out_reduce.along_z(k)
    gate_up_reduce.finish()
    for k in (1, 2, 3, 0):
        qkv_reduce.along_z(k)
    down_reduce.finish()
    out_reduce.finish()
    for i, (k, e) in enumerate(dp_peers):
        place = table_sums.at[dp_peer(k, e)[1]]
        wires.make(table_first + i, place, place, (dp_peer(k, e)[0], s)).wait_recv()
    total = table_sums[0]
    for i in range(1, n.dp):
        total = total + table_sums[i]
    table_all[s] = total
    table_second = wires.reserve(3)
    for i, (a, b) in enumerate(seq_peers):
        wires.go(table_second + i, table_all.at[s], table_all.at[s], (d, seq_peer(a, b)))
    for i, (a, b) in enumerate(seq_peers):
        place = sums.at[seq_peer(a, b)]
        wires.make(sums_first + i, place, place, (d, seq_peer(a, b))).wait_recv()
    mod_total = sums[0]
    for i in range(1, n.seq):
        mod_total = mod_total + sums[i]
    mod_totals = r.mod_totals
    mod_totals[d] = mod_total
    totals_first = wires.reserve(len(dp_peers))
    for i, (k, e) in enumerate(dp_peers):
        wires.go(totals_first + i, mod_totals.at[d], mod_totals.at[d], (dp_peer(k, e)[0], s))
    qkv_reduce.finish()
    for i, (k, e) in enumerate(dp_peers):
        place = mod_totals.at[dp_peer(k, e)[1]]
        wires.make(totals_first + i, place, place, (dp_peer(k, e)[0], s)).wait_recv()
    squashed_rows = r.squashed[pl.ds(pl.multiple_of(d * n.ada_rows, n.ada_rows), n.ada_rows), :]
    ada = squashed_rows[:, 0:1] * mod_totals[0]
    for i in range(1, n.dp):
        ada = ada + squashed_rows[:, i : i + 1] * mod_totals[i]
    r.grad_ada[...] = ada
    for i, (a, b) in enumerate(seq_peers):
        place = table_all.at[seq_peer(a, b)]
        wires.make(table_second + i, place, place, (d, seq_peer(a, b))).wait_recv()
    r.table[...] = table_all[...]
    for reduce in (gate_up_reduce, down_reduce, out_reduce, qkv_reduce):
        reduce.hand_on()
    for reduce in (gate_up_reduce, down_reduce, out_reduce, qkv_reduce):
        reduce.wait()
    wires.finish()


def fused_layer(sizes, valid_len, chain_break, hidden, out_grad, condition, qkv, out, gate_up, down, ada, lines):
    n = sizes
    rows, width, length, heads, part, hid = n.rows, n.width, n.length, n.heads, n.part, n.hidden
    any_space, vmem, smem = pl.ANY, pltpu.VMEM, pltpu.SMEM
    inputs = dict(
        valid_len=(valid_len, smem),
        chain_break=(chain_break, smem),
        hidden=(hidden, any_space),
        out_grad=(out_grad, any_space),
        condition=(condition, any_space),
        qkv=(qkv, any_space),
        out=(out, any_space),
        gate_up=(gate_up, any_space),
        down=(down, any_space),
        ada=(ada, vmem),
        lines=(lines, vmem),
    )
    modulations = 6 * width

    def reduced(height, columns):
        return (
            ((2, n.far, height, columns), BF16),
            ((n.far, height, columns), BF16),
            ((n.far - 1, height, columns), BF16),
            ((height, columns), BF16),
        )

    def shares(height, columns):
        return (n.seq, height, columns), BF16, any_space

    sums = ((2, rows, width), BF16), ((2, rows, width), BF16), ((rows, width), BF16), ((rows, width), BF16)
    gate_up_sizes, down_sizes = (n.shard, 2 * hid), (n.strip, width)
    proj_sizes, qkv_sizes = (n.half, width // 2), (n.shard, 3 * part)
    outputs = dict(
        result=((rows, width), BF16, vmem),
        input_grad=((rows, width), BF16, vmem),
        grad_ada=((n.ada_rows, modulations), F32, vmem),
        table=((n.seq, heads, 1, LANES), F32, vmem),
        gate_up_share=shares(*gate_up_sizes),
        down_share=shares(*down_sizes),
        proj_share=shares(*proj_sizes),
        qkv_share=shares(*qkv_sizes),
    )
    scratch = dict(
        w_qkv=((width, 3 * part), BF16),
        w_out=((n.dp, 2, n.half, width), BF16),
        w_gate_up=((width, 2 * hid), BF16),
        w_down=((hid, width), BF16),
        hidden_all=((length, width), BF16),
        grads_all=((length, width), BF16),
        hidden_own=((rows, width), BF16),
        upstream=((rows, width), BF16),
        cond_all=((n.dp, 8, n.conditioning), F32),
        squashed=((n.conditioning, n.dp), F32),
        mod_send=((n.dp, 1, modulations), F32),
        mod_recv=((n.dp, 1, modulations), F32),
        modulation=((1, modulations), F32),
        mod_sums=((n.seq, 1, modulations), F32),
        mod_totals=((n.dp, 1, modulations), F32),
        bias=((heads, (2 * n.blocks - 1) * LANES, LANES), F32),
        crossed=((heads, 1, LANES), F32),
        table_sums=((n.dp, heads, 1, LANES), F32),
        table_all=((n.seq, heads, 1, LANES), F32),
        keys=((heads, length, DH), BF16),
        values=((heads, length, DH), BF16),
        queries=((heads, length, DH), BF16),
        keys_t=((heads, n.seq, DH, rows), BF16),
        values_t=((heads, n.seq, DH, rows), BF16),
        queries_t=((heads, n.seq, DH, rows), BF16),
        exps=((heads, n.seq, length, rows), BF16),
        outs_t=((heads, n.seq, DH, rows), F32),
        inverse=((heads, n.seq, 1, rows), F32),
        mixed_send=((n.seq, rows, part), BF16),
        mixed_recv=((n.seq, rows, part), BF16),
        back_recv=((n.seq, rows, part), BF16),
        branch=((rows, width), F32),
        middle=((rows, width), F32),
        feed_own=((rows, width), F32),
        second_own=((rows, width), F32),
        branch_grad=((rows, width), BF16),
        second_all=((length, width), BF16),
        second_t=((width, length), BF16),
        inner=((rows, hid), BF16),
        inner_t=((hid, length), BF16),
        gate_up_grads=((length, 2 * hid), BF16),
        out_near=((n.dp * n.half, width), BF16),
        out_far=((n.dp * n.half, width // 2), BF16),
        raw=((length, rows), F32),
        score_grad=((length, rows), BF16),
        dots=((heads, rows, DH), BF16),
        dots_t=((heads, DH, rows), BF16),
        delta=((heads, 1, rows), F32),
        pair_grads=((heads, length, 2 * DH), F32),
        query_grads=((heads, length, DH), BF16),
        feed_sib=sums[0],
        feed_got=sums[1],
        feed_over=sums[2],
        feed_come=sums[3],
        second_sib=sums[0],
        second_got=sums[1],
        second_over=sums[2],
        second_come=sums[3],
        gate_up_grad=reduced(*gate_up_sizes)[0],
        gate_up_got=reduced(*gate_up_sizes)[1],
        gate_up_come=reduced(*gate_up_sizes)[2],
        gate_up_mine=reduced(*gate_up_sizes)[3],
        down_grad=reduced(*down_sizes)[0],
        down_got=reduced(*down_sizes)[1],
        down_come=reduced(*down_sizes)[2],
        down_mine=reduced(*down_sizes)[3],
        proj_grad=reduced(*proj_sizes)[0],
        proj_got=reduced(*proj_sizes)[1],
        proj_come=reduced(*proj_sizes)[2],
        proj_mine=reduced(*proj_sizes)[3],
        qkv_grad=reduced(*qkv_sizes)[0],
        qkv_got=reduced(*qkv_sizes)[1],
        qkv_come=reduced(*qkv_sizes)[2],
        qkv_mine=reduced(*qkv_sizes)[3],
    )
    semaphores = dict(send_sem=256, recv_sem=256, local_sem=32)
    names = [*inputs, *outputs, *scratch, *semaphores]
    return pl.pallas_call(
        functools.partial(layer_kernel, n, names),
        out_shape=[jax.ShapeDtypeStruct(shape, kind) for shape, kind, _ in outputs.values()],
        in_specs=[pl.BlockSpec(memory_space=space) for _, space in inputs.values()],
        out_specs=[pl.BlockSpec(memory_space=space) for _, _, space in outputs.values()],
        scratch_shapes=[pltpu.VMEM(shape, kind) for shape, kind in scratch.values()]
        + [pltpu.SemaphoreType.DMA((count,)) for count in semaphores.values()],
        compiler_params=pltpu.CompilerParams(
            collective_id=0, has_side_effects=True, vmem_limit_bytes=VMEM_LIMIT
        ),
    )(*[array for array, _ in inputs.values()])


def fused_body(
    hidden_in,
    condition,
    qkv_weight,
    out_weight,
    gate_up_weight,
    down_weight,
    ada_weight,
    pair_embed,
    pair_gain,
    pair_weight,
    valid_len,
    chain_break,
    out_grad,
):
    _, rows, width = hidden_in.shape
    seq = lax.axis_size("seq")
    dp = lax.axis_size("dp")
    me = lax.axis_index("seq")
    shard = qkv_weight.shape[0]
    sizes = Sizes(
        rows, width, seq, dp, shard, down_weight.shape[0], ada_weight.shape[0], condition.shape[1]
    )
    heads, part, strip = sizes.heads, sizes.part, sizes.strip

    def pick(array, axis):
        return lax.dynamic_index_in_dim(array, me, axis, keepdims=False)

    table, pair_pull = jax.vjp(
        pair_table, pair_embed.astype(F32), pair_gain.astype(F32), pair_weight.astype(F32)
    )
    lines = jnp.concatenate(
        [
            table[RR : 2 * RR],
            jnp.zeros((LANES - 2 * RR + 1, H), F32),
            table[1:RR],
            table[:1],
            table[2 * RR :],
            jnp.zeros((LANES - 3, H), F32),
        ],
        axis=0,
    )
    lines = lax.dynamic_slice_in_dim(lines.T, me * heads, heads, 0)[:, None, :]
    y, c = me // 2, lax.rem(me, 2)
    outs = fused_layer(
        sizes,
        valid_len,
        chain_break,
        hidden_in[0],
        out_grad[0],
        jnp.broadcast_to(condition.astype(F32), (8, condition.shape[1])),
        pick(qkv_weight.reshape(shard, 3, seq, part), 2).reshape(shard, 3 * part),
        lax.dynamic_slice(out_weight, (c * sizes.half, y * (width // 2)), (sizes.half, width // 2)),
        pick(gate_up_weight.reshape(shard, 2, dp, seq, strip), 3).reshape(shard, 2 * sizes.hidden),
        pick(down_weight.reshape(seq, strip, width), 0),
        ada_weight,
        lines,
    )
    result, input_grad, grad_ada, table_lines, gate_up_share, down_share, proj_share, qkv_share = outs
    table_lines = table_lines.reshape(H, LANES)
    table_grad = jnp.concatenate(
        [
            table_lines[:, 40:41],
            table_lines[:, LANES - RR + 1 :],
            table_lines[:, :RR],
            table_lines[:, 41:43],
        ],
        axis=1,
    ).T
    grad_embed, grad_gain, grad_pair = pair_pull(table_grad)
    qkv_share = jnp.transpose(qkv_share.reshape(seq, shard, 3, part), (1, 2, 0, 3))
    proj_share = jnp.transpose(proj_share.reshape(seq // 2, 2, sizes.half, width // 2), (1, 2, 0, 3))
    gate_up_share = jnp.transpose(gate_up_share.reshape(seq, shard, 2, dp, strip), (1, 2, 3, 0, 4))
    return (
        result[None],
        input_grad[None],
        qkv_share.reshape(shard, -1).astype(F32),
        proj_share.reshape(shard, -1).astype(F32),
        gate_up_share.reshape(shard, -1).astype(F32),
        down_share.reshape(seq * strip, width).astype(F32),
        grad_ada,
        grad_embed,
        grad_gain,
        grad_pair,
    )


def body(*arguments):
    hidden_in, _, qkv_weight, _, _, down_weight = arguments[:6]
    seq, dp = lax.axis_size("seq"), lax.axis_size("dp")
    whole_tiles = qkv_weight.shape[0] % 32 == 0 and down_weight.shape[0] % (16 * seq) == 0
    if whole_tiles and hidden_in.shape[0] == 1 and seq == 4 and dp % 2 == 0:
        return fused_body(*arguments)
    return plain_body(*arguments)


def solution(mesh):
    rows = P("dp", "seq", None)
    share = P("dp", None)
    return jax.shard_map(
        body,
        mesh=mesh,
        in_specs=(rows, share, share, share, share, share, share, P(), P(), P(), P("dp"), P("dp"), rows),
        out_specs=(rows, rows, share, share, share, share, share, P(), P(), P()),
        check_vma=False,
    )
```

```python
import functools
import types

import jax
import jax.numpy as jnp
from jax import lax
from jax.experimental import pallas as pl
from jax.experimental.pallas import tpu as pltpu
from jax.sharding import PartitionSpec as P

H = 12
DH = 64
RR = 32
CLASSES = 66

HIGHEST = lax.Precision.HIGHEST
F32 = jnp.float32
BF16 = jnp.bfloat16


VMEM_LIMIT = 65400 * 2**10


def layer_norm(values, epsilon=1e-06):
    average = jnp.mean(values, axis=-1, keepdims=True)
    centered = values - average
    inv_std = lax.rsqrt(jnp.mean(centered * centered, axis=-1, keepdims=True) + epsilon)
    return (centered * inv_std, inv_std)


def norm_back(upstream, normal, inv_std):
    return inv_std * (
        upstream
        - jnp.mean(upstream, axis=-1, keepdims=True)
        - normal * jnp.mean(upstream * normal, axis=-1, keepdims=True)
    )


def pair_table(pair_embed, pair_gain, pair_weight):
    average = jnp.mean(pair_embed, axis=-1, keepdims=True)
    centered = pair_embed - average
    normal = centered * lax.rsqrt(jnp.mean(centered * centered, axis=-1, keepdims=True) + 1e-05)
    return jnp.dot(normal * pair_gain, pair_weight, precision=HIGHEST)


def mm(spec, a, b):
    return jnp.einsum(spec, a, b, preferred_element_type=F32)


def plain_body(
    hidden_in,
    condition,
    qkv_weight,
    out_weight,
    gate_up_weight,
    down_weight,
    ada_weight,
    pair_embed,
    pair_gain,
    pair_weight,
    valid_len,
    chain_break,
    out_grad,
):
    items, rows, width = hidden_in.shape
    seq = lax.axis_size("seq")
    dp = lax.axis_size("dp")
    me = lax.axis_index("seq")
    at = lax.axis_index("dp")
    length = rows * seq
    heads = H // seq
    part = heads * DH
    shard = qkv_weight.shape[0]
    strip = down_weight.shape[0] // seq
    hidden_units = dp * strip

    def pick(array, axis):
        return lax.dynamic_index_in_dim(array, me, axis, keepdims=False)

    def gather(array, name, axis):
        return lax.all_gather(array, name, axis=axis, tiled=True)

    def scatter(array, name, axis):
        return lax.psum_scatter(array, name, scatter_dimension=axis, tiled=True)

    conditions = gather(condition, "dp", 0)
    squashed = jax.nn.silu(conditions.astype(F32)).astype(BF16)
    ada_rows = ada_weight.shape[0]
    squashed_part = lax.dynamic_slice_in_dim(squashed, at * ada_rows, ada_rows, 1)
    modulation = scatter(mm("ic,ce->ie", squashed_part, ada_weight), "dp", 0)
    shift_one, scale_one, gate_one, shift_two, scale_two, gate_two = jnp.split(
        modulation[:, None, :], 6, axis=-1
    )
    qkv_w = gather(pick(qkv_weight.reshape(shard, 3, seq, part), 2).reshape(shard, 3 * part), "dp", 0)
    gate_up_w = gather(
        pick(gate_up_weight.reshape(shard, 2, dp, seq, strip), 3).reshape(shard, 2 * hidden_units), "dp", 0
    )
    down_w = gather(pick(down_weight.reshape(seq, strip, width), 0), "dp", 0)
    out_w = gather(gather(pick(out_weight.reshape(shard, seq, width // seq), 1), "dp", 0), "seq", 1)

    table, pair_pull = jax.vjp(
        pair_table, pair_embed.astype(F32), pair_gain.astype(F32), pair_weight.astype(F32)
    )
    my_table = lax.dynamic_slice_in_dim(table, me * heads, heads, 1)
    spread = jnp.arange(2 * length)
    distance = jnp.where(spread < length, -spread, 2 * length - spread)
    line = jnp.take(my_table, jnp.clip(distance, -RR, RR) + RR, axis=0).T
    toeplitz = jnp.tile(line, (1, length))[:, : length * (2 * length - 1)]
    toeplitz = toeplitz.reshape(heads, length, 2 * length - 1)[:, :, :length]
    positions = jnp.arange(length, dtype=jnp.int32)
    side = positions[None] >= chain_break[:, None]
    same = side[:, :, None] == side[:, None, :]
    alive = (positions[None] < valid_len[:, None])[:, None, None, :]

    hidden = gather(hidden_in, "seq", 1).astype(F32)
    upstream = out_grad.astype(F32)
    first_norm, first_inv = layer_norm(hidden)
    first = (first_norm * (1.0 + scale_one) + shift_one).astype(BF16)
    merged = mm("ird,de->ire", first, qkv_w).astype(BF16)
    queries, keys, values = (
        part_of.reshape(items, length, heads, DH) for part_of in jnp.split(merged, 3, axis=-1)
    )
    logits = mm("iqhd,ikhd->ihqk", queries, keys) * 0.125
    logits = logits + jnp.where(same[:, None], toeplitz[None], my_table[CLASSES - 1][None, :, None, None])
    logits = jnp.where(alive, logits, -1e30)
    powers = jnp.exp(logits - jnp.max(logits, axis=-1, keepdims=True))
    probs = powers / jnp.sum(powers, axis=-1, keepdims=True)
    probs_low = probs.astype(BF16)
    mixed_heads = mm("ihqk,ikhd->iqhd", probs_low, values)
    mixed_part = mixed_heads.reshape(items, length, part).astype(BF16)
    mixed_all = gather(mixed_part, "seq", 2)

    def mine(array):
        return lax.dynamic_slice_in_dim(array, me * rows, rows, 1)

    branch = mm("ire,ed->ird", mine(mixed_all), out_w)
    middle = hidden_in.astype(F32) + gate_one * branch
    second_norm, second_inv = layer_norm(middle)
    second = gather((second_norm * (1.0 + scale_two) + shift_two).astype(BF16), "seq", 1)
    gate_up = mm("ird,de->ire", second, gate_up_w)
    gate_part, up_part = jnp.split(gate_up, 2, axis=-1)
    sigmoid_gate = jax.nn.sigmoid(gate_part)
    inner = (gate_part * sigmoid_gate * up_part).astype(BF16)
    feed = scatter(mm("irf,fd->ird", inner, down_w).astype(BF16), "seq", 1).astype(F32)
    result = (middle + gate_two * feed).astype(BF16)

    feed_grad = (gate_two * gather(out_grad, "seq", 1).astype(F32)).astype(BF16)
    d_gate_two = jnp.sum(upstream * feed, axis=1)
    grad_down = mm("irf,ird->fd", inner, feed_grad)
    inner_grad = mm("ird,fd->irf", feed_grad, down_w)
    gate_grad = inner_grad * up_part * sigmoid_gate * (1.0 + gate_part * (1.0 - sigmoid_gate))
    up_grad = inner_grad * gate_part * sigmoid_gate
    gate_up_grad = jnp.concatenate([gate_grad, up_grad], axis=-1).astype(BF16)
    grad_gate_up = mm("ird,ire->de", second, gate_up_grad)
    second_grad = scatter(mm("ire,de->ird", gate_up_grad, gate_up_w).astype(BF16), "seq", 1).astype(F32)
    d_shift_two = jnp.sum(second_grad, axis=1)
    d_scale_two = jnp.sum(second_grad * second_norm, axis=1)
    middle_grad = upstream + norm_back(second_grad * (1.0 + scale_two), second_norm, second_inv)
    branch_grad = (gate_one * middle_grad).astype(BF16)
    d_gate_one = jnp.sum(middle_grad * branch, axis=1)
    branch_grad_all = gather(branch_grad, "seq", 1)
    my_columns = lax.dynamic_slice_in_dim(branch_grad_all, me * part, part, 2)
    grad_out = mm("ire,ird->ed", mixed_all, my_columns)
    out_w_rows = lax.dynamic_slice_in_dim(out_w, me * part, part, 0)
    mixed_grad = mm("ird,ed->ire", branch_grad_all, out_w_rows).astype(BF16).reshape(items, length, heads, DH)

    prob_grad = mm("iqhd,ikhd->ihqk", mixed_grad, values)
    delta = jnp.sum(probs * prob_grad, axis=-1, keepdims=True)
    score_grad = (probs * (prob_grad - delta)).astype(BF16)
    query_grad = mm("ihqk,ikhd->iqhd", score_grad, keys) * 0.125
    key_grad = mm("ihqk,iqhd->ikhd", score_grad, queries) * 0.125
    value_grad = mm("ihqk,iqhd->ikhd", probs_low, mixed_grad)
    merged_grad = jnp.concatenate(
        [term.reshape(items, length, part) for term in (query_grad, key_grad, value_grad)], axis=-1
    ).astype(BF16)
    wide = score_grad.astype(F32)
    kept = jnp.sum(jnp.where(same[:, None], wide, 0.0), axis=0)
    crossed = jnp.sum(jnp.where(same[:, None], 0.0, wide), axis=(0, 2, 3))
    skewed = jnp.pad(kept[:, :, ::-1], ((0, 0), (0, 0), (0, length))).reshape(heads, -1)
    skewed = skewed[:, : length * (2 * length - 1)].reshape(heads, length, 2 * length - 1)
    lines = jnp.sum(skewed, axis=1)
    middle_line = length - 1
    low_end = jnp.sum(lines[:, : middle_line - RR + 1], axis=1)
    high_end = jnp.sum(lines[:, middle_line + RR :], axis=1)
    near = lines[:, middle_line - RR + 1 : middle_line + RR]
    my_table_grad = jnp.concatenate([low_end[:, None], near, high_end[:, None], crossed[:, None]], axis=1).T
    table_grad = lax.psum(
        lax.dynamic_update_slice_in_dim(jnp.zeros((CLASSES, H), F32), my_table_grad, me * heads, 1), ("dp", "seq")
    )
    grad_embed, grad_gain, grad_pair = pair_pull(table_grad)

    grad_qkv = mm("ird,ire->de", first, merged_grad)
    first_grad = scatter(mm("ire,de->ird", merged_grad, qkv_w).astype(BF16), "seq", 1).astype(F32)
    my_norm, my_inv = mine(first_norm), mine(first_inv)
    d_shift_one = jnp.sum(first_grad, axis=1)
    d_scale_one = jnp.sum(first_grad * my_norm, axis=1)
    input_grad = middle_grad + norm_back(first_grad * (1.0 + scale_one), my_norm, my_inv)
    modulation_grad = jnp.concatenate(
        [d_shift_one, d_scale_one, d_gate_one, d_shift_two, d_scale_two, d_gate_two], axis=-1
    )
    modulation_grads = gather(lax.psum(modulation_grad, "seq"), "dp", 0)
    grad_ada = jnp.einsum("ic,ie->ce", squashed_part.astype(F32), modulation_grads, precision=HIGHEST)

    def owned(grad):
        return scatter(grad.astype(BF16), "dp", 0)

    def everyone(grad):
        return lax.all_gather(grad, "seq", axis=0)

    shares_qkv = everyone(owned(grad_qkv)).reshape(seq, shard, 3, part)
    shares_out = everyone(owned(grad_out))
    shares_gate_up = everyone(owned(grad_gate_up)).reshape(seq, shard, 2, dp, strip)
    shares_down = everyone(owned(grad_down))
    return (
        result,
        input_grad.astype(BF16),
        jnp.transpose(shares_qkv, (1, 2, 0, 3)).reshape(shard, -1).astype(F32),
        jnp.transpose(shares_out, (1, 0, 2)).reshape(shard, -1).astype(F32),
        jnp.transpose(shares_gate_up, (1, 2, 3, 0, 4)).reshape(shard, -1).astype(F32),
        shares_down.reshape(seq * strip, width).astype(F32),
        grad_ada,
        grad_embed,
        grad_gain,
        grad_pair,
    )


MESH = pl.DeviceIdType.MESH
LANES = 128


def nn(a, b):
    return jnp.dot(a, b, preferred_element_type=F32)


def nt(a, b):
    return lax.dot_general(a, b, (((1,), (1,)), ((), ())), preferred_element_type=F32)


def tn(a, b):
    return lax.dot_general(a, b, (((0,), (0,)), ((), ())), preferred_element_type=F32)


def skew(tile, back):
    row = lax.broadcasted_iota(jnp.int32, tile.shape, 0)
    for bit in range(7):
        turn = LANES - (1 << bit) if back else 1 << bit
        tile = jnp.where(((row >> bit) & 1) == 1, pltpu.roll(tile, turn, 1), tile)
    return tile


class Sizes:
    def __init__(self, rows, width, seq, dp, shard, down_shard, ada_rows, conditioning):
        self.rows, self.width, self.seq, self.dp = rows, width, seq, dp
        self.shard, self.ada_rows, self.conditioning = shard, ada_rows, conditioning
        self.strip = down_shard // seq
        self.length = rows * seq
        self.heads = H // seq
        self.part = self.heads * DH
        self.hidden = self.strip * dp
        self.far = dp // 2
        self.half = shard // 2
        self.blocks = self.length // LANES


def under(where, work):
    if where is None:
        work()
    else:
        pl.when(where)(work)


class Wires:
    def __init__(self, send, recv):
        self.send, self.recv, self.count, self.started = send, recv, 0, []

    def reserve(self, count=1):
        first = self.count
        self.count += count
        return first

    def make(self, number, source, target, device):
        return pltpu.make_async_remote_copy(
            src_ref=source,
            dst_ref=target,
            send_sem=self.send.at[number],
            recv_sem=self.recv.at[number],
            device_id=device,
            device_id_type=MESH,
        )

    def go(self, number, source, target, device, where=None):
        copy = self.make(number, source, target, device)
        under(where, copy.start)
        self.started.append((copy, where))
        return copy

    def settle(self, copy):
        copy.wait_send()
        self.started = [other for other in self.started if other[0] is not copy]

    def finish(self):
        for copy, where in self.started:
            under(where, copy.wait_send)
        self.started = []


def layer_kernel(sizes, names, *refs):
    r = types.SimpleNamespace(**dict(zip(names, refs, strict=True)))
    n = sizes
    rows, width, part, heads, length, hid = n.rows, n.width, n.part, n.heads, n.length, n.hidden
    half_rows = rows // 2
    d, s = lax.axis_index("dp"), lax.axis_index("seq")
    z, x = d // 2, lax.rem(d, 2)
    y, c = s // 2, lax.rem(s, 2)
    ox, oy, oc = 1 - x, 1 - y, 1 - c
    at_x = (z * 2 + ox, s)
    at_y = (d, oy * 2 + c)
    at_c = (d, y * 2 + oc)

    def z_plus(k):
        return lax.rem(z + k, n.far)

    def at_z(k):
        return (z_plus(k) * 2 + x, s)

    wires = Wires(r.send_sem, r.recv_sem)
    dp_peers = [(k, e) for k in range(n.far) for e in range(2) if k or e]
    seq_peers = [(1, 0), (0, 1), (1, 1)]

    def dp_peer(k, e):
        xx = lax.rem(x + e, 2)
        return z_plus(k) * 2 + xx, lax.rem(z + n.far - k, n.far) * 2 + xx

    def seq_peer(a, b):
        return lax.rem(y + a, 2) * 2 + lax.rem(c + b, 2)

    local_count = [0]

    def local(source, target):
        copy = pltpu.make_async_copy(source, target, r.local_sem.at[local_count[0]])
        local_count[0] += 1
        copy.start()
        return copy

    qkv_stage, gate_up_stage = r.second_t, r.gate_up_grads
    staged = [
        local(r.qkv.at[:, q * width : (q + 1) * width], qkv_stage.at[q * n.shard : (q + 1) * n.shard, 0:width])
        for q in range(3)
    ]
    staged_gate_up = [
        local(r.gate_up.at[:, q * 2 * hid : (q + 1) * 2 * hid], gate_up_stage.at[q * n.shard : (q + 1) * n.shard])
        for q in range(n.seq)
    ]
    own_shard = pl.ds(pl.multiple_of(d * n.shard, n.shard), n.shard)
    r.cond_all[d] = jnp.broadcast_to(r.condition[...].astype(F32), (8, n.conditioning))
    barrier = pltpu.get_barrier_semaphore()
    for k, e in dp_peers:
        pl.semaphore_signal(barrier, inc=1, device_id=(dp_peer(k, e)[0], s), device_id_type=MESH)
    for a, b in seq_peers:
        pl.semaphore_signal(barrier, inc=1, device_id=(d, seq_peer(a, b)), device_id_type=MESH)
    for copy in staged:
        copy.wait()
    for side in range(n.seq):

        @pl.when(s == side)
        def _():
            r.w_qkv[own_shard, :] = jnp.concatenate(
                [
                    qkv_stage[q * n.shard : (q + 1) * n.shard, side * part : (side + 1) * part]
                    for q in range(3)
                ],
                axis=1,
            )

    pl.semaphore_wait(barrier, len(dp_peers) + len(seq_peers))

    class SeqGather:
        def __init__(self, block):
            self.block, self.first = block, wires.reserve(3)
            self.mine, self.from_y, self.from_c, self.from_yc = s, at_y[1], at_c[1], oy * 2 + oc

        def start(self, source=None):
            mine = self.block(self.mine)
            source = mine if source is None else source
            self.sent = [wires.go(self.first, source, mine, at_y), wires.go(self.first + 1, source, mine, at_c)]

        def hand_on(self):
            place = self.block(self.from_y)
            wires.make(self.first, place, place, at_y).wait_recv()
            self.sent.append(wires.go(self.first + 2, place, place, at_c))

        def settle(self):
            for copy in self.sent:
                wires.settle(copy)

        def wait_core(self):
            place = self.block(self.from_c)
            wires.make(self.first + 1, place, place, at_c).wait_recv()

        def wait_last(self):
            place = self.block(self.from_yc)
            wires.make(self.first + 2, place, place, at_c).wait_recv()

        def wait(self):
            self.hand_on()
            self.wait_core()
            self.wait_last()

    last_z = n.far - 1

    class Wave:
        def __init__(self, block, direct=False):
            self.block, self.first, self.direct = block, wires.reserve(4), direct

        def send(self, source=None):
            mine = self.block(z)
            source = mine if source is None else source
            wires.go(self.first + 1, source, mine, at_z(1), None if self.direct else z != last_z)
            wires.go(self.first + 3, source, mine, at_z(3), None if self.direct else z != 0)
            wires.go(self.first + 2, source, mine, at_z(2))

        def relay(self):
            place = self.block(z_plus(2))
            wires.make(self.first + 2, place, place, at_z(2)).wait_recv()
            if not self.direct:
                wires.go(self.first, place, place, at_z(1), z == last_z - 1)
                wires.go(self.first, place, place, at_z(3), z == 1)

        def arrive(self, k):
            place = self.block(z_plus(n.far - k))
            far_end = z == (0 if k == 1 else last_z)
            near = wires.make(self.first + k, place, place, at_z(k))
            if self.direct:
                near.wait_recv()
                return
            far = wires.make(self.first, place, place, at_z(k))
            under(far_end, far.wait_recv)
            under(jnp.logical_not(far_end), near.wait_recv)

    class DpGather:
        def __init__(self, source, place, direct=False):
            self.source, self.place, self.first = source, place, wires.reserve(n.far)
            self.wave = Wave(lambda zz: place(zz * 2 + x), direct)

        def start(self):
            mine = self.place(d)
            self.own = None if self.source is None else local(self.source, mine)
            wires.go(self.first, mine if self.source is None else self.source, mine, at_x)

        def along_z(self):
            self.wave.send(self.source)

        def across(self, k):
            place = self.place(z_plus(n.far - k) * 2 + x)
            wires.go(self.first + k, place, place, at_x)

        def relay(self):
            self.wave.relay()
            self.across(2)

        def hand_on(self):
            for k in (1, 3):
                self.wave.arrive(k)
                self.across(k)

        def wait(self):
            if self.own is not None:
                self.own.wait()
            for k in range(n.far):
                place = self.place(z_plus(n.far - k) * 2 + ox)
                wires.make(self.first + k, place, place, at_x).wait_recv()

    class DpGatherX:
        def __init__(self, source, place):
            self.source, self.place, self.first = source, place, wires.reserve()
            self.waves = Wave(lambda zz: place(zz * 2 + x)), Wave(lambda zz: place(zz * 2 + ox))

        def start(self):
            self.own = local(self.source, self.place(d))
            wires.go(self.first, self.source, self.place(d), at_x)

        def along_z(self):
            self.waves[0].send(self.source)

        def cross(self):
            place = self.place(z * 2 + ox)
            wires.make(self.first, place, place, at_x).wait_recv()
            self.waves[1].send()

        def relay(self, which):
            self.waves[which].relay()

        def wait(self):
            self.own.wait()
            for wave in self.waves:
                wave.arrive(1)
                wave.arrive(3)

    class SeqReduce:
        def __init__(self, sib, got, over, come):
            self.sib, self.got, self.over, self.come = sib, got, over, come
            self.first, self.sent = wires.reserve(3), []

        def put_core(self, index):
            def put(lanes, block):
                self.sib[index, :, lanes] = block.astype(BF16)

            return put

        def to_core(self, index):
            self.sent.append(wires.go(self.first + index, self.sib.at[index], self.got.at[index], at_c))

        def wait_far(self):
            wires.make(self.first + 1, self.sib.at[1], self.got.at[1], at_c).wait_recv()

        def put_y(self):
            def put(lanes, block):
                self.over[:, lanes] = (block + self.got[1, :, lanes].astype(F32)).astype(BF16)

            return put

        def to_y(self):
            self.sent.append(wires.go(self.first + 2, self.over, self.come, at_y))

        def settle(self):
            for copy in self.sent:
                wires.settle(copy)

        def wait(self):
            wires.make(self.first, self.sib.at[0], self.got.at[0], at_c).wait_recv()
            wires.make(self.first + 2, self.over, self.come, at_y).wait_recv()

        def total(self, own, place):
            return own[place, :] + self.got[0, place, :].astype(F32) + self.come[place, :].astype(F32)

    class DpReduce:
        def __init__(self, grad, got, come, mine, share):
            self.grad, self.got, self.come, self.mine, self.share = grad, got, come, mine, share
            self.first, self.second = wires.reserve(n.far), wires.reserve(n.far)
            self.gather = SeqGather(lambda t: self.share.at[t])

        def start(self):
            for k in (*range(1, n.far), 0):
                to = z_plus(k)
                wires.go(self.first + k, self.grad.at[ox, to], self.got.at[to], at_x)

        def along_z(self, k):
            to = z_plus(k)
            wires.make(self.first + k, self.grad.at[ox, to], self.got.at[to], at_x).wait_recv()
            self.grad[x, to] = (self.grad[x, to].astype(F32) + self.got[to].astype(F32)).astype(BF16)
            if k:
                wires.go(self.second + k, self.grad.at[x, to], self.come.at[k - 1], at_z(k))

        def finish(self):
            total = self.grad[x, z].astype(F32)
            for k in range(1, n.far):
                wires.make(self.second + k, self.grad.at[x, z], self.come.at[k - 1], at_z(k)).wait_recv()
                total = total + self.come[k - 1].astype(F32)
            self.mine[...] = total.astype(BF16)
            self.own = local(self.mine, self.share.at[s])
            self.gather.start(self.mine)

        def hand_on(self):
            self.gather.hand_on()

        def wait(self):
            self.gather.wait_core()
            self.gather.wait_last()
            self.own.wait()

    step = 64

    def by_rows(count, work, start=0, unroll=2):
        def one(q, carry):
            return work(pl.ds(pl.multiple_of(q * step, step), step), carry)

        return lax.fori_loop(0, count // step, one, start, unroll=unroll)

    wide = 2 * LANES

    def by_lanes(count, work):
        def one(q, _):
            work(pl.ds(pl.multiple_of(q * wide, wide), wide))
            return 0

        lax.fori_loop(0, count // wide, one, 0, unroll=True)

    def fold_rows(array):
        return jnp.sum(array.reshape(step // 8, 8, width), axis=0)

    hidden_all, grads_all = r.hidden_all, r.grads_all

    def rows_of(ref):
        return lambda t: ref.at[pl.ds(pl.multiple_of(t * rows, rows), rows)]

    hidden_gather, up_gather = SeqGather(rows_of(hidden_all)), SeqGather(rows_of(grads_all))
    def shard_rows(ref, height, lanes=slice(None)):
        return lambda t: ref.at[pl.ds(pl.multiple_of(t * height, height), height), lanes]

    def lane_half(side):
        return pl.ds(pl.multiple_of(side * (width // 2), width // 2), width // 2)

    lanes_y = lane_half(y)
    qkv_gathers = [
        DpGather(None, shard_rows(r.w_qkv, n.shard, lanes), True)
        for lanes in (slice(0, 2 * LANES), slice(2 * LANES, 3 * part))
    ]
    out_gather = DpGather(
        r.out.at[pl.ds(pl.multiple_of(c * n.half, n.half), n.half), lanes_y],
        lambda t: r.w_out.at[t, c, :, lanes_y],
    )
    half_strip = n.strip // 2

    def down_half(kind, side):
        low = side * half_strip
        return kind(
            r.down.at[pl.ds(pl.multiple_of(s * n.strip + low, half_strip), half_strip)],
            lambda t: r.w_down.at[pl.ds(pl.multiple_of(t * n.strip + low, half_strip), half_strip)],
        )

    down_near, down_gather = down_half(DpGather, 0), down_half(DpGatherX, 1)
    pieces = [
        DpGather(None, shard_rows(r.w_gate_up, n.shard, slice(q * (hid // 2), (q + 1) * (hid // 2))))
        for q in (0, 2, 1, 3)
    ]

    def out_block(t):
        ty, tc = t // 2, lax.rem(t, 2)
        return r.w_out.at[:, tc, :, lane_half(ty)]

    out_share = SeqGather(out_block)

    cond_first, mod_first = wires.reserve(len(dp_peers)), wires.reserve(len(dp_peers))
    cond_all, mod_send, mod_recv = r.cond_all, r.mod_send, r.mod_recv
    for i, (k, e) in enumerate(dp_peers):
        wires.go(cond_first + i, cond_all.at[d], cond_all.at[d], (dp_peer(k, e)[0], s))
    for piece in qkv_gathers:
        piece.along_z()
        piece.start()
    own_hidden = local(r.hidden, hidden_gather.block(s))
    keep_hidden = local(r.hidden, r.hidden_own)
    keep_grads = local(r.out_grad, r.upstream)
    hidden_gather.start(r.hidden)
    own_grads = local(r.out_grad, up_gather.block(s))


    for i, (k, e) in enumerate(dp_peers):
        place = cond_all.at[dp_peer(k, e)[1]]
        wires.make(cond_first + i, place, place, (dp_peer(k, e)[0], s)).wait_recv()
    item_of = lax.broadcasted_iota(jnp.int32, (n.dp, n.conditioning), 0)
    conditions = jnp.where(item_of == 0, cond_all[0], 0.0)
    for i in range(1, n.dp):
        conditions = jnp.where(item_of == i, cond_all[i], conditions)
    squashed = (conditions * (1.0 / (1.0 + jnp.exp(-conditions)))).astype(BF16).astype(F32)
    r.squashed[...] = squashed.T
    squashed_rows = r.squashed[pl.ds(pl.multiple_of(d * n.ada_rows, n.ada_rows), n.ada_rows), :]
    ada_part = tn(squashed_rows.astype(BF16), r.ada[...])
    for i in range(n.dp):
        mod_send[i] = ada_part[i : i + 1]
    mod_recv[d] = mod_send[d]
    for i, (k, e) in enumerate(dp_peers):
        wires.go(mod_first + i, mod_send.at[dp_peer(k, e)[0]], mod_recv.at[d], (dp_peer(k, e)[0], s))
    for copy in staged_gate_up:
        copy.wait()
    group = n.seq * n.strip
    for side in range(n.seq):

        @pl.when(s == side)
        def _():
            strips = []
            for number in range(2 * n.dp):
                block, low = divmod(number * group, 2 * hid)
                low += side * n.strip
                strips.append(gate_up_stage[block * n.shard : (block + 1) * n.shard, low : low + n.strip])
            r.w_gate_up[own_shard, :] = jnp.concatenate(strips, axis=1)

    for piece in (out_gather, *pieces[:2]):
        piece.start()
        piece.along_z()
    down_gather.start()
    down_gather.along_z()
    down_near.start()
    down_near.along_z()
    for piece in pieces[2:]:
        piece.start()
    hidden_gather.hand_on()
    up_gather.start(r.out_grad)
    for piece in qkv_gathers:
        piece.relay()
        piece.hand_on()

    bias, table_t = r.bias, r.table_t
    embed = r.pair_embed[...].astype(F32)
    normal, _ = layer_norm(embed, 1e-05)
    scaled = normal * r.pair_gain[...].astype(F32)
    scaled = jnp.concatenate([scaled, jnp.zeros((LANES - CLASSES, scaled.shape[1]), F32)], axis=0)
    table_t[...] = lax.dot_general(
        r.pair_weight[...].astype(F32),
        scaled,
        (((1,), (1,)), ((), ())),
        precision=HIGHEST,
        preferred_element_type=F32,
    )

    def table_line(h):
        return table_t[pl.ds(s * heads + h, 1), :]

    key_in = lax.broadcasted_iota(jnp.int32, (LANES, LANES), 0)
    query_in = lax.broadcasted_iota(jnp.int32, (LANES, LANES), 1)
    middle_tile = n.blocks - 1

    def build_bias(h, _):
        line = table_line(h)
        near = skew(jnp.broadcast_to(pltpu.roll(line, LANES - RR, 1), (LANES, LANES)), False)
        low_end = jnp.broadcast_to(line[:, 0:1], (LANES, LANES))
        high_end = jnp.broadcast_to(line[:, 2 * RR : 2 * RR + 1], (LANES, LANES))
        for tile in range(2 * n.blocks - 1):
            away = tile - middle_tile
            apart = query_in - key_in - away * LANES
            if away < -1:
                value = high_end
            elif away > 1:
                value = low_end
            else:
                value = jnp.where(apart >= RR, high_end, jnp.where(apart <= -RR, low_end, near))
            bias[h, tile * LANES : (tile + 1) * LANES] = value
        return 0

    lax.fori_loop(0, heads, build_bias, 0)

    own_hidden.wait()
    hidden_gather.wait_core()
    hidden_gather.wait_last()
    for i, (k, e) in enumerate(dp_peers):
        place = mod_recv.at[dp_peer(k, e)[1]]
        wires.make(mod_first + i, mod_send.at[d], place, (dp_peer(k, e)[0], s)).wait_recv()
    modulation = mod_recv[0]
    for i in range(1, n.dp):
        modulation = modulation + mod_recv[i]
    r.modulation[...] = modulation

    def vector(index):
        return r.modulation[:, index * width : (index + 1) * width]

    shift_one, scale_one, gate_one, shift_two, scale_two, gate_two = range(6)
    first = hidden_all
    hidden_gather.settle()

    def make_first(place, _):
        normal, _ = layer_norm(hidden_all[place, :].astype(F32))
        first[place, :] = (normal * (1.0 + vector(scale_one)) + vector(shift_one)).astype(BF16)
        return 0

    by_rows(length, make_first)
    out_gather.relay()
    out_gather.hand_on()
    pieces[0].relay()

    for piece in qkv_gathers:
        piece.wait()
    w_qkv = r.w_qkv
    keys, values, queries = r.keys, r.values, r.queries
    keys_t, values_t, queries_t = r.keys_t, r.values_t, r.queries_t
    w_qkv_t = r.inner_t

    def turn_weight(q, _):
        place = pl.ds(pl.multiple_of(q * 2 * LANES, 2 * LANES), 2 * LANES)
        w_qkv_t[0 : 3 * part, place] = w_qkv[place, :].T
        return 0

    lax.fori_loop(0, width // (2 * LANES), turn_weight, 0)

    def project(t, _):
        place = pl.ds(pl.multiple_of(t * rows, rows), rows)
        block = first[place, :]
        for low in range(0, 3 * part, wide):
            merged = nn(block, w_qkv[:, low : min(low + wide, 3 * part)]).astype(BF16)
            for q in range(merged.shape[1] // DH):
                kind, h = divmod(low // DH + q, heads)
                column = merged[:, q * DH : (q + 1) * DH]
                if kind == 0:
                    column = (column.astype(F32) * 0.125).astype(BF16)
                (queries, keys, values)[kind][h, place, :] = column
        for kind, target in enumerate((queries_t, keys_t, values_t)):
            merged_t = nt(w_qkv_t[kind * part : (kind + 1) * part, 0:width], block).astype(BF16)
            if kind == 0:
                merged_t = (merged_t.astype(F32) * 0.125).astype(BF16)
            for h in range(heads):
                target[h, t] = merged_t[h * DH : (h + 1) * DH]
        return 0

    lax.fori_loop(0, n.seq, project, 0)
    pieces[0].hand_on()
    down_gather.cross()
    for piece in pieces[2:]:
        piece.along_z()
    pieces[1].relay()

    valid, broken = r.valid_len[0], r.chain_break[0]
    exps, outs_t, inverse = r.exps, r.outs_t, r.inverse
    tiles = rows // LANES
    order = [oy * 2 + c, oy * 2 + oc, y * 2 + oc, s]

    raw = r.raw

    def tile_parts(t, tile):
        number = t * tiles + tile
        query_side = number * LANES + lax.broadcasted_iota(jnp.int32, (1, LANES), 1) >= broken
        for q in range(n.blocks):
            key_pos = q * LANES + lax.broadcasted_iota(jnp.int32, (LANES, LANES), 0)
            strip = pl.ds(pl.multiple_of((n.blocks - 1 + q - number) * LANES, LANES), LANES)
            yield slice(q * LANES, (q + 1) * LANES), strip, key_pos, (key_pos >= broken) == query_side

    def eights(array):
        return array.reshape(LANES // 8, 8, LANES)

    def attend(t):
        def one_head(h, _):
            for q in range(n.seq):
                place = slice(q * rows, (q + 1) * rows)
                raw[place, 0:rows] = nn(keys[h, place, :], queries_t[h, t])
            for tile in range(tiles):
                lanes = slice(tile * LANES, (tile + 1) * LANES)
                far_side = jnp.broadcast_to(table_line(h)[:, CLASSES - 1 : CLASSES], (1, LANES))
                top = jnp.full((8, LANES), -1e30, F32)
                for place, strip, key_pos, same in tile_parts(t, tile):
                    logits = raw[place, lanes] + jnp.where(same, bias[h, strip, :], far_side)
                    logits = jnp.where(key_pos < valid, logits, -1e30)
                    raw[place, lanes] = logits
                    top = jnp.maximum(top, jnp.max(eights(logits), axis=0))
                top = jnp.max(top, axis=0, keepdims=True)
                total = jnp.zeros((8, LANES), F32)
                for q in range(n.blocks):
                    place = slice(q * LANES, (q + 1) * LANES)
                    powers = jnp.exp(raw[place, lanes] - top)
                    total = total + jnp.sum(eights(powers), axis=0)
                    exps[h, t, place, lanes] = powers.astype(BF16)
                inverse[h, t, :, lanes] = 1.0 / jnp.sum(total, axis=0, keepdims=True)
            values_wide = jnp.concatenate([values_t[h, q] for q in range(n.seq)], axis=1)
            outs_t[h, t] = nn(values_wide, exps[h, t]) * inverse[h, t]
            return 0

        lax.fori_loop(0, heads, one_head, 0)

    mixed_first = wires.reserve(3)
    mixed_send, mixed_recv = r.mixed_send, r.mixed_recv
    mixed_sent = []
    to_send = [at_y, (d, oy * 2 + oc), at_c]
    out_gather.wait()
    out_share.start()
    for i, t in enumerate(order):
        attend(t)
        block = jnp.concatenate([outs_t[h, t] for h in range(heads)], axis=0).T.astype(BF16)
        if i < 3:
            mixed_send[i] = block
            mixed_sent.append(wires.go(mixed_first + i, mixed_send.at[i], mixed_recv.at[s], to_send[i]))
        else:
            mixed_recv[s] = block
        if i == 0:
            pieces[1].hand_on()
        if i == 1:
            down_gather.relay(0)
        if i == 2:
            down_near.relay()
            down_near.hand_on()
        if i == 0:
            up_gather.hand_on()
        if i == 1:
            out_share.hand_on()

    out_share.wait_core()
    out_share.wait_last()

    def w_out(q, lanes=slice(None)):
        shards = part // n.shard
        block = r.w_out[q * shards : (q + 1) * shards, :, :, lanes]
        return block.reshape(part, block.shape[-1])

    for i in range(3):
        place = mixed_recv.at[order[i]]
        wires.make(mixed_first + i, mixed_send.at[i], place, to_send[i]).wait_recv()
    keep_hidden.wait()

    def make_branch(lanes):
        branch = nn(mixed_recv[0], w_out(0, lanes))
        for q in range(1, n.seq):
            branch = branch + nn(mixed_recv[q], w_out(q, lanes))
        r.branch[:, lanes] = branch

    by_lanes(width, make_branch)
    second_all = r.second_all
    second_gather = SeqGather(rows_of(second_all))

    def make_second(place, _):
        middle = r.hidden_own[place, :].astype(F32) + vector(gate_one) * r.branch[place, :]
        r.middle[place, :] = middle
        normal, _ = layer_norm(middle)
        r.branch_grad[place, :] = (normal * (1.0 + vector(scale_two)) + vector(shift_two)).astype(BF16)
        return 0

    by_rows(rows, make_second)
    second_all[pl.ds(pl.multiple_of(s * rows, rows), rows), :] = r.branch_grad[...]
    second_gather.start()

    own_grads.wait()
    up_gather.wait_core()
    up_gather.wait_last()
    up_gather.settle()
    feed_grads = grads_all

    def make_feed_grads(place, _):
        feed_grads[place, :] = (vector(gate_two) * grads_all[place, :].astype(F32)).astype(BF16)
        return 0

    by_rows(length, make_feed_grads)
    down_gather.relay(1)
    for piece in (pieces[0], pieces[1], down_near, down_gather):
        piece.wait()
    w_gate_up, w_down = r.w_gate_up, r.w_down
    inner, inner_t, gate_up_grads, second_t = r.inner, r.inner_t, r.gate_up_grads, r.second_t
    feed_places = (r.feed_sib, r.feed_got, r.feed_over, r.feed_come)
    feed_reduce = SeqReduce(*feed_places)
    second_reduce = SeqReduce(r.second_sib, r.second_got, r.second_over, r.second_come)
    half_hid = hid // 2

    def rows_at(t):
        return pl.ds(pl.multiple_of(t * rows, rows), rows)

    def units(t, side):
        place, low = rows_at(t), side * half_hid
        block, given = second_all[place, :], feed_grads[place, :]
        gates, ups, inner_grads = (raw.at[i * rows : (i + 1) * rows] for i in range(3))
        gates[...] = nn(block, w_gate_up[:, low : low + half_hid])
        ups[...] = nn(block, w_gate_up[:, hid + low : hid + low + half_hid])
        inner_grads[...] = nt(given, w_down[low : low + half_hid, :])
        for first_row in range(0, rows, step):
            few = slice(first_row, first_row + step)
            gate, up, inner_grad = gates[few, :], ups[few, :], inner_grads[few, :]
            sigmoid = 1.0 / (1.0 + jnp.exp(-gate))
            silu = gate * sigmoid
            to = pl.ds(pl.multiple_of(t * rows + first_row, step), step)
            inner[to, low : low + half_hid] = (silu * up).astype(BF16)
            gate_up_grads[to, low : low + half_hid] = (
                inner_grad * up * sigmoid * (1.0 + gate * (1.0 - sigmoid))
            ).astype(BF16)
            gate_up_grads[to, hid + low : hid + low + half_hid] = (inner_grad * silu).astype(BF16)

    def second_part(t, put):
        by_lanes(width, lambda lanes: put(lanes, nt(gate_up_grads[rows_at(t), :], w_gate_up[lanes, :])))

    def feed_part(t, put):
        by_lanes(width, lambda lanes: put(lanes, nn(inner[rows_at(t), :], w_down[:, lanes])))

    def put_in(ref):
        def put(lanes, block):
            ref[:, lanes] = block.astype(ref.dtype)

        return put

    units(s, 0)
    second_gather.wait_core()
    units(y * 2 + oc, 0)
    second_gather.hand_on()
    pieces[2].relay()
    units(oy * 2 + c, 0)
    pieces[2].hand_on()
    pieces[3].relay()
    second_gather.wait_last()
    units(oy * 2 + oc, 0)
    pieces[3].hand_on()
    pieces[2].wait()
    pieces[3].wait()
    far, over, near = oy * 2 + oc, oy * 2 + c, y * 2 + oc
    units(far, 1)
    second_part(far, second_reduce.put_core(1))
    second_reduce.to_core(1)
    units(over, 1)
    second_reduce.wait_far()
    second_part(over, second_reduce.put_y())
    second_reduce.to_y()
    units(near, 1)
    second_part(near, second_reduce.put_core(0))
    second_reduce.to_core(0)
    units(s, 1)
    second_part(s, put_in(r.second_own))

    def turn_rows(source, target):
        def turn(t, _):
            target[:, rows_at(t)] = source[rows_at(t), :].T
            return 0

        lax.fori_loop(0, n.seq, turn, 0)

    turn_rows(second_all, second_t)

    gate_up_reduce = DpReduce(r.gate_up_grad, r.gate_up_got, r.gate_up_come, r.gate_up_mine, r.gate_up_share)
    down_reduce = DpReduce(r.down_grad, r.down_got, r.down_come, r.down_mine, r.down_share)
    out_reduce = DpReduce(r.proj_grad, r.proj_got, r.proj_come, r.proj_mine, r.proj_share)
    qkv_reduce = DpReduce(r.qkv_grad, r.qkv_got, r.qkv_come, r.qkv_mine, r.qkv_share)

    def weight_grad(left_t, right, reduce, columns, step):
        def block(q, _):
            low = pl.multiple_of(q * step, step)
            height = reduce.grad.shape[2]
            few = n.dp // 2
            for first_of in range(0, n.dp, few):
                grad = nn(left_t[first_of * height : (first_of + few) * height, :], right[:, pl.ds(low, step)]).astype(BF16)
                for i in range(few):
                    to = first_of + i
                    reduce.grad[to % 2, to // 2, :, pl.ds(low, step)] = grad[i * height : (i + 1) * height]
            return 0

        lax.fori_loop(0, columns // step, block, 0)

    weight_grad(second_t, gate_up_grads, gate_up_reduce, 2 * hid, wide)
    gate_up_reduce.start()
    turn_rows(inner, inner_t)
    weight_grad(inner_t, feed_grads, down_reduce, width, wide)
    down_reduce.start()
    feed_part(far, feed_reduce.put_core(1))
    feed_reduce.to_core(1)
    feed_part(near, feed_reduce.put_core(0))
    feed_reduce.to_core(0)
    feed_reduce.wait_far()
    feed_part(over, feed_reduce.put_y())
    feed_reduce.to_y()
    feed_part(s, put_in(r.feed_own))
    lax.fori_loop(0, width // (2 * LANES), turn_weight, 0)

    sums = r.mod_sums

    upstream = r.upstream
    keep_grads.wait()
    second_reduce.wait()
    kept_middle_grad, branch_grad = r.second_own, r.branch_grad
    empty = jnp.zeros((8, width), F32)

    def put_sum(index, array):
        sums[s, :, index * width : (index + 1) * width] = jnp.sum(array, axis=0, keepdims=True)

    def second_back(place, carry):
        second_grad = second_reduce.total(r.second_own, place)
        normal, inverted = layer_norm(r.middle[place, :])
        middle_grad = upstream[place, :].astype(F32) + norm_back(
            second_grad * (1.0 + vector(scale_two)), normal, inverted
        )
        kept_middle_grad[place, :] = middle_grad
        branch_grad[place, :] = (vector(gate_one) * middle_grad).astype(BF16)
        terms = (second_grad, second_grad * normal, middle_grad * r.branch[place, :])
        return tuple(total + fold_rows(term) for total, term in zip(carry, terms))

    for index, total in zip(
        (shift_two, scale_two, gate_one), by_rows(rows, second_back, (empty, empty, empty))
    ):
        put_sum(index, total)
    back_first = wires.reserve(3)
    for copy in mixed_sent:
        wires.settle(copy)
    back_all, back_recv = mixed_send, r.back_recv
    for q in range(n.seq):
        back_all[q] = nt(branch_grad[...], w_out(q)).astype(BF16)
    for i in range(3):
        wires.go(back_first + i, back_all.at[order[i]], back_recv.at[s], to_send[i])
    back_recv[s] = back_all[s]

    out_first = wires.reserve(2)
    second_gather.settle()
    out_parts, quarter = second_all, n.dp * n.half

    def make_out_grad(lanes):
        for q in range(n.seq):
            grad = tn(mixed_recv[q], branch_grad[:, lanes]).astype(BF16)
            for i in range(part // n.half):
                number = q * (part // n.half) + i
                low = (number % 2) * quarter + (number // 2) * n.half
                out_parts[low : low + n.half, lanes] = grad[i * n.half : (i + 1) * n.half]

    by_lanes(width, make_out_grad)

    def out_rows(core):
        return out_parts.at[pl.ds(pl.multiple_of(core * quarter, quarter), quarter)]

    lanes_oy = pl.ds(pl.multiple_of(oy * (width // 2), width // 2), width // 2)

    def out_cores():
        wires.make(out_first, out_rows(oc), r.out_near, at_c).wait_recv()
        mine = out_parts[pl.ds(pl.multiple_of(c * quarter, quarter), quarter), :]
        r.out_near[...] = (r.out_near[...].astype(F32) + mine.astype(F32)).astype(BF16)
        wires.go(out_first + 1, r.out_near.at[:, lanes_oy], r.out_far, at_y)

    def out_sum():
        wires.make(out_first + 1, r.out_near.at[:, lanes_oy], r.out_far, at_y).wait_recv()
        total = (r.out_near[:, lanes_y].astype(F32) + r.out_far[...].astype(F32)).astype(BF16)
        for to in range(n.dp):
            r.proj_grad[to % 2, to // 2] = total[to * n.half : (to + 1) * n.half]
        out_reduce.start()

    dots, dots_t, delta = r.dots, r.dots_t, r.delta
    pair_grads, query_grads = r.pair_grads, r.query_grads
    bias[...] = jnp.zeros_like(bias)
    pair_grads[...] = jnp.zeros_like(pair_grads)
    crossed, score_grad = r.crossed, inner.at[:, 0:rows]
    crossed[...] = jnp.zeros_like(crossed)

    def attend_back(t):
        given_t = back_recv[t].T.astype(F32)
        for h in range(heads):
            scaled = (given_t[h * DH : (h + 1) * DH] * inverse[h, t]).astype(BF16)
            dots_t[h] = scaled
            dots[h] = scaled.T
            delta[h] = jnp.sum(scaled.astype(F32) * outs_t[h, t], axis=0, keepdims=True)
        place = pl.ds(pl.multiple_of(t * rows, rows), rows)

        def one_head(h, _):
            for q in range(n.seq):
                some = slice(q * rows, (q + 1) * rows)
                raw[some, 0:rows] = nn(values[h, some, :], dots_t[h])
            for tile in range(tiles):
                lanes = slice(tile * LANES, (tile + 1) * LANES)
                across = jnp.zeros((8, LANES), F32)
                for keys_of, strip, _, same in tile_parts(t, tile):
                    grad = exps[h, t, keys_of, lanes].astype(F32) * (raw[keys_of, lanes] - delta[h, :, lanes])
                    kept = jnp.where(same, grad, 0.0)
                    bias[h, strip, :] = bias[h, strip, :] + kept
                    across = across + jnp.sum(eights(grad - kept), axis=0)
                    score_grad[keys_of, lanes] = grad.astype(BF16)
                crossed[h] = crossed[h] + jnp.sum(across, axis=0, keepdims=True)
            keys_wide = jnp.concatenate([keys_t[h, q] for q in range(n.seq)], axis=1)
            query_grads[h, place, :] = (nn(keys_wide, score_grad[...]) * 0.125).T.astype(BF16)
            for q in range(n.seq):
                some = slice(q * rows, (q + 1) * rows)
                pair_grads[h, some, :] = pair_grads[h, some, :] + jnp.concatenate(
                    [nn(score_grad[some, :], queries[h, place, :]), nn(exps[h, t, some, :], dots[h])], axis=1
                )
            return 0

        lax.fori_loop(0, heads, one_head, 0)

    gate_up_reduce.along_z(1)
    attend_back(order[3])
    feed_reduce.wait()

    def make_result(place, total):
        feed = feed_reduce.total(r.feed_own, place)
        r.result[place, :] = (r.middle[place, :] + vector(gate_two) * feed).astype(BF16)
        return total + fold_rows(upstream[place, :].astype(F32) * feed)

    put_sum(gate_two, by_rows(rows, make_result, empty))
    wires.go(out_first, out_rows(oc), r.out_near, at_c)
    gate_up_reduce.along_z(2)
    out_cores()
    wires.make(back_first + 2, back_recv.at[order[2]], back_recv.at[order[2]], to_send[2]).wait_recv()
    attend_back(order[2])
    gate_up_reduce.along_z(3)
    out_sum()
    wires.make(back_first, back_recv.at[order[0]], back_recv.at[order[0]], to_send[0]).wait_recv()
    attend_back(order[0])
    gate_up_reduce.along_z(0)
    down_reduce.along_z(1)
    wires.make(back_first + 1, back_recv.at[order[1]], back_recv.at[order[1]], to_send[1]).wait_recv()
    attend_back(order[1])
    down_reduce.along_z(2)

    feed_reduce.settle()
    first_reduce = SeqReduce(*feed_places)
    merged_grads = gate_up_grads

    def first_part(t, put):
        place = pl.ds(pl.multiple_of(t * rows, rows), rows)
        merged = jnp.concatenate(
            [query_grads[h, place, :] for h in range(heads)]
            + [pair_grads[h, place, 0:DH].astype(BF16) for h in range(heads)]
            + [pair_grads[h, place, DH : 2 * DH].astype(BF16) for h in range(heads)],
            axis=1,
        )
        merged_grads[place, 0 : 3 * part] = merged
        by_lanes(width, lambda lanes: put(lanes, nn(merged_grads[place, 0 : 3 * part], w_qkv_t[0 : 3 * part, lanes])))

    first_part(oy * 2 + oc, first_reduce.put_core(1))
    first_reduce.to_core(1)
    first_part(y * 2 + oc, first_reduce.put_core(0))
    first_reduce.to_core(0)
    first_reduce.wait_far()
    first_part(oy * 2 + c, first_reduce.put_y())
    first_reduce.to_y()
    first_part(s, put_in(r.feed_own))

    turn_rows(first, second_t)

    def qkv_grad(q, _):
        low = pl.multiple_of(q * 2 * n.shard, 2 * n.shard)
        grad = nn(second_t[pl.ds(low, 2 * n.shard), :], merged_grads[:, 0 : 3 * part]).astype(BF16)
        qkv_reduce.grad[0, q] = grad[: n.shard]
        qkv_reduce.grad[1, q] = grad[n.shard :]
        return 0

    lax.fori_loop(0, n.far, qkv_grad, 0)
    qkv_reduce.start()
    for k in (3, 0):
        down_reduce.along_z(k)

    table_sums, table_all = r.table_sums, r.table_all

    def fold(h, _):
        lane = lax.broadcasted_iota(jnp.int32, (1, LANES), 1)
        near = jnp.zeros((LANES, LANES), F32)
        low_end = jnp.zeros((LANES, LANES), F32)
        high_end = jnp.zeros((LANES, LANES), F32)
        for tile in range(2 * n.blocks - 1):
            away = tile - middle_tile
            apart = query_in - key_in - away * LANES
            value = bias[h, tile * LANES : (tile + 1) * LANES]
            if away < -1:
                high_end = high_end + value
            elif away > 1:
                low_end = low_end + value
            else:
                high_end = high_end + jnp.where(apart >= RR, value, 0.0)
                low_end = low_end + jnp.where(apart <= -RR, value, 0.0)
                near = near + jnp.where((apart < RR) & (apart > -RR), value, 0.0)
        line = jnp.sum(skew(near, True), axis=0, keepdims=True)
        for where, array in ((40, low_end), (41, high_end), (42, crossed[h])):
            line = jnp.where(lane == where, jnp.sum(array), line)
        table_sums[d, h] = line
        return 0

    lax.fori_loop(0, heads, fold, 0)
    table_first = wires.reserve(len(dp_peers))
    for i, (k, e) in enumerate(dp_peers):
        wires.go(table_first + i, table_sums.at[d], table_sums.at[d], (dp_peer(k, e)[0], s))

    first_reduce.wait()

    def first_back(place, carry):
        first_grad = first_reduce.total(r.feed_own, place)
        normal, inverted = layer_norm(r.hidden_own[place, :].astype(F32))
        r.input_grad[place, :] = (
            kept_middle_grad[place, :] + norm_back(first_grad * (1.0 + vector(scale_one)), normal, inverted)
        ).astype(BF16)
        return tuple(total + fold_rows(term) for total, term in zip(carry, (first_grad, first_grad * normal)))

    for index, total in zip((shift_one, scale_one), by_rows(rows, first_back, (empty, empty))):
        put_sum(index, total)
    sums_first = wires.reserve(3)
    for i, (a, b) in enumerate(seq_peers):
        wires.go(sums_first + i, sums.at[s], sums.at[s], (d, seq_peer(a, b)))
    for k in (1, 2, 3, 0):
        out_reduce.along_z(k)
    gate_up_reduce.finish()
    for k in (1, 2, 3, 0):
        qkv_reduce.along_z(k)
    down_reduce.finish()
    out_reduce.finish()
    for i, (k, e) in enumerate(dp_peers):
        place = table_sums.at[dp_peer(k, e)[1]]
        wires.make(table_first + i, place, place, (dp_peer(k, e)[0], s)).wait_recv()
    total = table_sums[0]
    for i in range(1, n.dp):
        total = total + table_sums[i]
    table_all[s] = total
    table_second = wires.reserve(3)
    for i, (a, b) in enumerate(seq_peers):
        wires.go(table_second + i, table_all.at[s], table_all.at[s], (d, seq_peer(a, b)))
    for i, (a, b) in enumerate(seq_peers):
        place = sums.at[seq_peer(a, b)]
        wires.make(sums_first + i, place, place, (d, seq_peer(a, b))).wait_recv()
    mod_total = sums[0]
    for i in range(1, n.seq):
        mod_total = mod_total + sums[i]
    mod_totals = r.mod_totals
    mod_totals[d] = mod_total
    totals_first = wires.reserve(len(dp_peers))
    for i, (k, e) in enumerate(dp_peers):
        wires.go(totals_first + i, mod_totals.at[d], mod_totals.at[d], (dp_peer(k, e)[0], s))
    qkv_reduce.finish()
    for i, (k, e) in enumerate(dp_peers):
        place = mod_totals.at[dp_peer(k, e)[1]]
        wires.make(totals_first + i, place, place, (dp_peer(k, e)[0], s)).wait_recv()
    squashed_rows = r.squashed[pl.ds(pl.multiple_of(d * n.ada_rows, n.ada_rows), n.ada_rows), :]
    ada = squashed_rows[:, 0:1] * mod_totals[0]
    for i in range(1, n.dp):
        ada = ada + squashed_rows[:, i : i + 1] * mod_totals[i]
    r.grad_ada[...] = ada
    for i, (a, b) in enumerate(seq_peers):
        place = table_all.at[seq_peer(a, b)]
        wires.make(table_second + i, place, place, (d, seq_peer(a, b))).wait_recv()
    r.table[...] = table_all[...]
    for reduce in (gate_up_reduce, down_reduce, out_reduce, qkv_reduce):
        reduce.hand_on()
    for reduce in (gate_up_reduce, down_reduce, out_reduce, qkv_reduce):
        reduce.wait()
    wires.finish()


def write_outputs(sizes, inputs, outputs):
    n = sizes
    result, input_grad, grad_ada, table, gate_up, down, proj, qkv, pair_embed, pair_gain, pair_weight = inputs
    o_result, o_input, o_qkv, o_out, o_gate_up, o_down, o_ada, o_embed, o_gain, o_pair = outputs
    o_result[...] = result[...]
    o_input[...] = input_grad[...]
    o_ada[...] = grad_ada[...]
    everyone = range(n.seq)
    for kind in range(3):
        lanes = slice(kind * n.part, (kind + 1) * n.part)
        o_qkv[:, kind * n.width : (kind + 1) * n.width] = jnp.concatenate(
            [qkv[q, :, lanes] for q in everyone], axis=1
        ).astype(F32)
    group = n.seq * n.strip
    for number in range(2 * n.dp):
        lanes = slice(number * n.strip, (number + 1) * n.strip)
        o_gate_up[:, number * group : (number + 1) * group] = jnp.concatenate(
            [gate_up[q, :, lanes] for q in everyone], axis=1
        ).astype(F32)
    for q in everyone:
        o_down[q * n.strip : (q + 1) * n.strip, :] = down[q].astype(F32)
        side, core = divmod(q, 2)
        lanes = slice(side * (n.width // 2), (side + 1) * (n.width // 2))
        o_out[core * n.half : (core + 1) * n.half, lanes] = proj[q].astype(F32)

    lines = jnp.concatenate([table[q, h] for q in everyone for h in range(n.heads)], axis=0)
    lane = lax.broadcasted_iota(jnp.int32, lines.shape, 1)
    table_t = jnp.where(lane < 2 * RR, pltpu.roll(lines, RR, 1), 0.0)
    for number, at in ((0, 40), (2 * RR, 41), (CLASSES - 1, 42)):
        table_t = jnp.where(lane == number, jnp.broadcast_to(lines[:, at : at + 1], lines.shape), table_t)
    embed = pair_embed[...].astype(F32)
    embed = jnp.concatenate([embed, jnp.zeros((LANES - CLASSES, embed.shape[1]), F32)], axis=0)
    gain = pair_gain[...].astype(F32)
    normal, inverted = layer_norm(embed, 1e-05)

    def exact(a, b):
        return jnp.dot(a, b, precision=HIGHEST, preferred_element_type=F32)

    o_pair[...] = exact(table_t, normal * gain)
    scaled_grad = exact(table_t.T, pair_weight[...].astype(F32))
    o_gain[...] = jnp.sum(scaled_grad * normal, axis=0)
    o_embed[...] = norm_back(scaled_grad * gain, normal, inverted)[0:CLASSES]


def fused_layer(
    sizes, valid_len, chain_break, hidden, out_grad, condition, qkv, out, gate_up, down, ada, embed, gain, weight
):
    n = sizes
    rows, width, length, heads, part, hid = n.rows, n.width, n.length, n.heads, n.part, n.hidden
    any_space, vmem, smem = pl.ANY, pltpu.VMEM, pltpu.SMEM
    inputs = dict(
        valid_len=(valid_len, smem),
        chain_break=(chain_break, smem),
        hidden=(hidden, any_space),
        out_grad=(out_grad, any_space),
        condition=(condition, vmem),
        qkv=(qkv, any_space),
        out=(out, any_space),
        gate_up=(gate_up, any_space),
        down=(down, any_space),
        ada=(ada, vmem),
        pair_embed=(embed, vmem),
        pair_gain=(gain, vmem),
        pair_weight=(weight, vmem),
    )
    modulations = 6 * width

    def reduced(height, columns):
        return (
            ((2, n.far, height, columns), BF16),
            ((n.far, height, columns), BF16),
            ((n.far - 1, height, columns), BF16),
            ((height, columns), BF16),
        )

    def shares(height, columns):
        return (n.seq, height, columns), BF16, any_space

    sums = ((2, rows, width), BF16), ((2, rows, width), BF16), ((rows, width), BF16), ((rows, width), BF16)
    gate_up_sizes, down_sizes = (n.shard, 2 * hid), (n.strip, width)
    proj_sizes, qkv_sizes = (n.half, width // 2), (n.shard, 3 * part)
    outputs = dict(
        result=((rows, width), BF16, vmem),
        input_grad=((rows, width), BF16, vmem),
        grad_ada=((n.ada_rows, modulations), F32, vmem),
        table=((n.seq, heads, 1, LANES), F32, vmem),
        gate_up_share=shares(*gate_up_sizes),
        down_share=shares(*down_sizes),
        proj_share=shares(*proj_sizes),
        qkv_share=shares(*qkv_sizes),
    )
    scratch = dict(
        w_qkv=((width, 3 * part), BF16),
        w_out=((n.dp, 2, n.half, width), BF16),
        w_gate_up=((width, 2 * hid), BF16),
        w_down=((hid, width), BF16),
        hidden_all=((length, width), BF16),
        grads_all=((length, width), BF16),
        hidden_own=((rows, width), BF16),
        upstream=((rows, width), BF16),
        cond_all=((n.dp, 8, n.conditioning), F32),
        squashed=((n.conditioning, n.dp), F32),
        mod_send=((n.dp, 1, modulations), F32),
        mod_recv=((n.dp, 1, modulations), F32),
        modulation=((1, modulations), F32),
        mod_sums=((n.seq, 1, modulations), F32),
        mod_totals=((n.dp, 1, modulations), F32),
        bias=((heads, (2 * n.blocks - 1) * LANES, LANES), F32),
        crossed=((heads, 1, LANES), F32),
        table_t=((H, LANES), F32),
        table_sums=((n.dp, heads, 1, LANES), F32),
        table_all=((n.seq, heads, 1, LANES), F32),
        keys=((heads, length, DH), BF16),
        values=((heads, length, DH), BF16),
        queries=((heads, length, DH), BF16),
        keys_t=((heads, n.seq, DH, rows), BF16),
        values_t=((heads, n.seq, DH, rows), BF16),
        queries_t=((heads, n.seq, DH, rows), BF16),
        exps=((heads, n.seq, length, rows), BF16),
        outs_t=((heads, n.seq, DH, rows), F32),
        inverse=((heads, n.seq, 1, rows), F32),
        mixed_send=((n.seq, rows, part), BF16),
        mixed_recv=((n.seq, rows, part), BF16),
        back_recv=((n.seq, rows, part), BF16),
        branch=((rows, width), F32),
        middle=((rows, width), F32),
        feed_own=((rows, width), F32),
        second_own=((rows, width), F32),
        branch_grad=((rows, width), BF16),
        second_all=((length, width), BF16),
        second_t=((width, length), BF16),
        inner=((length, hid), BF16),
        inner_t=((hid, length), BF16),
        gate_up_grads=((length, 2 * hid), BF16),
        out_near=((n.dp * n.half, width), BF16),
        out_far=((n.dp * n.half, width // 2), BF16),
        raw=((length, hid // 2), F32),
        dots=((heads, rows, DH), BF16),
        dots_t=((heads, DH, rows), BF16),
        delta=((heads, 1, rows), F32),
        pair_grads=((heads, length, 2 * DH), F32),
        query_grads=((heads, length, DH), BF16),
        feed_sib=sums[0],
        feed_got=sums[1],
        feed_over=sums[2],
        feed_come=sums[3],
        second_sib=sums[0],
        second_got=sums[1],
        second_over=sums[2],
        second_come=sums[3],
        gate_up_grad=reduced(*gate_up_sizes)[0],
        gate_up_got=reduced(*gate_up_sizes)[1],
        gate_up_come=reduced(*gate_up_sizes)[2],
        gate_up_mine=reduced(*gate_up_sizes)[3],
        down_grad=reduced(*down_sizes)[0],
        down_got=reduced(*down_sizes)[1],
        down_come=reduced(*down_sizes)[2],
        down_mine=reduced(*down_sizes)[3],
        proj_grad=reduced(*proj_sizes)[0],
        proj_got=reduced(*proj_sizes)[1],
        proj_come=reduced(*proj_sizes)[2],
        proj_mine=reduced(*proj_sizes)[3],
        qkv_grad=reduced(*qkv_sizes)[0],
        qkv_got=reduced(*qkv_sizes)[1],
        qkv_come=reduced(*qkv_sizes)[2],
        qkv_mine=reduced(*qkv_sizes)[3],
    )
    semaphores = dict(send_sem=192, recv_sem=192, local_sem=20)
    names = [*inputs, *outputs, *scratch, *semaphores]
    made = pl.pallas_call(
        functools.partial(layer_kernel, n, names),
        out_shape=[jax.ShapeDtypeStruct(shape, kind) for shape, kind, _ in outputs.values()],
        in_specs=[pl.BlockSpec(memory_space=space) for _, space in inputs.values()],
        out_specs=[pl.BlockSpec(memory_space=space) for _, _, space in outputs.values()],
        scratch_shapes=[pltpu.VMEM(shape, kind) for shape, kind in scratch.values()]
        + [pltpu.SemaphoreType.DMA((count,)) for count in semaphores.values()],
        compiler_params=pltpu.CompilerParams(
            collective_id=0, has_side_effects=True, vmem_limit_bytes=VMEM_LIMIT
        ),
    )(*[array for array, _ in inputs.values()])
    gradients = (
        ((rows, width), BF16),
        ((rows, width), BF16),
        ((n.shard, 3 * width), F32),
        ((n.shard, width), F32),
        ((n.shard, 2 * n.seq * hid), F32),
        ((n.seq * n.strip, width), F32),
        ((n.ada_rows, modulations), F32),
        (embed.shape, F32),
        (gain.shape, F32),
        (weight.shape, F32),
    )
    count = len(made) + 3

    def write(*refs):
        write_outputs(n, refs[:count], refs[count:])

    return pl.pallas_call(
        write,
        out_shape=[jax.ShapeDtypeStruct(shape, kind) for shape, kind in gradients],
        in_specs=[pl.BlockSpec(memory_space=vmem)] * count,
        out_specs=[pl.BlockSpec(memory_space=vmem)] * len(gradients),
        compiler_params=pltpu.CompilerParams(vmem_limit_bytes=VMEM_LIMIT),
    )(*made, embed, gain, weight)


def fused_body(
    hidden_in,
    condition,
    qkv_weight,
    out_weight,
    gate_up_weight,
    down_weight,
    ada_weight,
    pair_embed,
    pair_gain,
    pair_weight,
    valid_len,
    chain_break,
    out_grad,
):
    _, rows, width = hidden_in.shape
    seq = lax.axis_size("seq")
    dp = lax.axis_size("dp")
    shard = qkv_weight.shape[0]
    sizes = Sizes(
        rows, width, seq, dp, shard, down_weight.shape[0], ada_weight.shape[0], condition.shape[1]
    )
    outs = fused_layer(
        sizes,
        valid_len,
        chain_break,
        hidden_in[0],
        out_grad[0],
        condition,
        qkv_weight,
        out_weight,
        gate_up_weight,
        down_weight,
        ada_weight,
        pair_embed,
        pair_gain,
        pair_weight.T,
    )
    result, input_grad, *grads, grad_gain, grad_pair = outs
    return (result[None], input_grad[None], *grads, grad_gain, grad_pair.T)


def body(*arguments):
    hidden_in, _, qkv_weight, _, _, down_weight = arguments[:6]
    seq, dp = lax.axis_size("seq"), lax.axis_size("dp")
    whole_tiles = qkv_weight.shape[0] % 32 == 0 and down_weight.shape[0] % (16 * seq) == 0
    if whole_tiles and hidden_in.shape[0] == 1 and seq == 4 and dp == 8:
        return fused_body(*arguments)
    return plain_body(*arguments)


def solution(mesh):
    rows = P("dp", "seq", None)
    share = P("dp", None)
    return jax.shard_map(
        body,
        mesh=mesh,
        in_specs=(rows, share, share, share, share, share, share, P(), P(), P(), P("dp"), P("dp"), rows),
        out_specs=(rows, rows, share, share, share, share, share, P(), P(), P()),
        check_vma=False,
    )
```

```python
import functools
import types

import jax
import jax.numpy as jnp
from jax import lax
from jax.experimental import pallas as pl
from jax.experimental.pallas import tpu as pltpu
from jax.sharding import PartitionSpec as P

H = 12
DH = 64
RR = 32
CLASSES = 66

HIGHEST = lax.Precision.HIGHEST
F32 = jnp.float32
BF16 = jnp.bfloat16


VMEM_LIMIT = 65400 * 2**10


def layer_norm(values, epsilon=1e-06):
    average = jnp.mean(values, axis=-1, keepdims=True)
    centered = values - average
    inv_std = lax.rsqrt(jnp.mean(centered * centered, axis=-1, keepdims=True) + epsilon)
    return (centered * inv_std, inv_std)


def norm_back(upstream, normal, inv_std):
    return inv_std * (
        upstream
        - jnp.mean(upstream, axis=-1, keepdims=True)
        - normal * jnp.mean(upstream * normal, axis=-1, keepdims=True)
    )


def pair_table(pair_embed, pair_gain, pair_weight):
    average = jnp.mean(pair_embed, axis=-1, keepdims=True)
    centered = pair_embed - average
    normal = centered * lax.rsqrt(jnp.mean(centered * centered, axis=-1, keepdims=True) + 1e-05)
    return jnp.dot(normal * pair_gain, pair_weight, precision=HIGHEST)


def mm(spec, a, b):
    return jnp.einsum(spec, a, b, preferred_element_type=F32)


def plain_body(
    hidden_in,
    condition,
    qkv_weight,
    out_weight,
    gate_up_weight,
    down_weight,
    ada_weight,
    pair_embed,
    pair_gain,
    pair_weight,
    valid_len,
    chain_break,
    out_grad,
):
    items, rows, width = hidden_in.shape
    seq = lax.axis_size("seq")
    dp = lax.axis_size("dp")
    me = lax.axis_index("seq")
    at = lax.axis_index("dp")
    length = rows * seq
    heads = H // seq
    part = heads * DH
    shard = qkv_weight.shape[0]
    strip = down_weight.shape[0] // seq
    hidden_units = dp * strip

    def pick(array, axis):
        return lax.dynamic_index_in_dim(array, me, axis, keepdims=False)

    def gather(array, name, axis):
        return lax.all_gather(array, name, axis=axis, tiled=True)

    def scatter(array, name, axis):
        return lax.psum_scatter(array, name, scatter_dimension=axis, tiled=True)

    conditions = gather(condition, "dp", 0)
    squashed = jax.nn.silu(conditions.astype(F32)).astype(BF16)
    ada_rows = ada_weight.shape[0]
    squashed_part = lax.dynamic_slice_in_dim(squashed, at * ada_rows, ada_rows, 1)
    modulation = scatter(mm("ic,ce->ie", squashed_part, ada_weight), "dp", 0)
    shift_one, scale_one, gate_one, shift_two, scale_two, gate_two = jnp.split(
        modulation[:, None, :], 6, axis=-1
    )
    qkv_w = gather(pick(qkv_weight.reshape(shard, 3, seq, part), 2).reshape(shard, 3 * part), "dp", 0)
    gate_up_w = gather(
        pick(gate_up_weight.reshape(shard, 2, dp, seq, strip), 3).reshape(shard, 2 * hidden_units), "dp", 0
    )
    down_w = gather(pick(down_weight.reshape(seq, strip, width), 0), "dp", 0)
    out_w = gather(gather(pick(out_weight.reshape(shard, seq, width // seq), 1), "dp", 0), "seq", 1)

    table, pair_pull = jax.vjp(
        pair_table, pair_embed.astype(F32), pair_gain.astype(F32), pair_weight.astype(F32)
    )
    my_table = lax.dynamic_slice_in_dim(table, me * heads, heads, 1)
    spread = jnp.arange(2 * length)
    distance = jnp.where(spread < length, -spread, 2 * length - spread)
    line = jnp.take(my_table, jnp.clip(distance, -RR, RR) + RR, axis=0).T
    toeplitz = jnp.tile(line, (1, length))[:, : length * (2 * length - 1)]
    toeplitz = toeplitz.reshape(heads, length, 2 * length - 1)[:, :, :length]
    positions = jnp.arange(length, dtype=jnp.int32)
    side = positions[None] >= chain_break[:, None]
    same = side[:, :, None] == side[:, None, :]
    alive = (positions[None] < valid_len[:, None])[:, None, None, :]

    hidden = gather(hidden_in, "seq", 1).astype(F32)
    upstream = out_grad.astype(F32)
    first_norm, first_inv = layer_norm(hidden)
    first = (first_norm * (1.0 + scale_one) + shift_one).astype(BF16)
    merged = mm("ird,de->ire", first, qkv_w).astype(BF16)
    queries, keys, values = (
        part_of.reshape(items, length, heads, DH) for part_of in jnp.split(merged, 3, axis=-1)
    )
    logits = mm("iqhd,ikhd->ihqk", queries, keys) * 0.125
    logits = logits + jnp.where(same[:, None], toeplitz[None], my_table[CLASSES - 1][None, :, None, None])
    logits = jnp.where(alive, logits, -1e30)
    powers = jnp.exp(logits - jnp.max(logits, axis=-1, keepdims=True))
    probs = powers / jnp.sum(powers, axis=-1, keepdims=True)
    probs_low = probs.astype(BF16)
    mixed_heads = mm("ihqk,ikhd->iqhd", probs_low, values)
    mixed_part = mixed_heads.reshape(items, length, part).astype(BF16)
    mixed_all = gather(mixed_part, "seq", 2)

    def mine(array):
        return lax.dynamic_slice_in_dim(array, me * rows, rows, 1)

    branch = mm("ire,ed->ird", mine(mixed_all), out_w)
    middle = hidden_in.astype(F32) + gate_one * branch
    second_norm, second_inv = layer_norm(middle)
    second = gather((second_norm * (1.0 + scale_two) + shift_two).astype(BF16), "seq", 1)
    gate_up = mm("ird,de->ire", second, gate_up_w)
    gate_part, up_part = jnp.split(gate_up, 2, axis=-1)
    sigmoid_gate = jax.nn.sigmoid(gate_part)
    inner = (gate_part * sigmoid_gate * up_part).astype(BF16)
    feed = scatter(mm("irf,fd->ird", inner, down_w).astype(BF16), "seq", 1).astype(F32)
    result = (middle + gate_two * feed).astype(BF16)

    feed_grad = (gate_two * gather(out_grad, "seq", 1).astype(F32)).astype(BF16)
    d_gate_two = jnp.sum(upstream * feed, axis=1)
    grad_down = mm("irf,ird->fd", inner, feed_grad)
    inner_grad = mm("ird,fd->irf", feed_grad, down_w)
    gate_grad = inner_grad * up_part * sigmoid_gate * (1.0 + gate_part * (1.0 - sigmoid_gate))
    up_grad = inner_grad * gate_part * sigmoid_gate
    gate_up_grad = jnp.concatenate([gate_grad, up_grad], axis=-1).astype(BF16)
    grad_gate_up = mm("ird,ire->de", second, gate_up_grad)
    second_grad = scatter(mm("ire,de->ird", gate_up_grad, gate_up_w).astype(BF16), "seq", 1).astype(F32)
    d_shift_two = jnp.sum(second_grad, axis=1)
    d_scale_two = jnp.sum(second_grad * second_norm, axis=1)
    middle_grad = upstream + norm_back(second_grad * (1.0 + scale_two), second_norm, second_inv)
    branch_grad = (gate_one * middle_grad).astype(BF16)
    d_gate_one = jnp.sum(middle_grad * branch, axis=1)
    branch_grad_all = gather(branch_grad, "seq", 1)
    my_columns = lax.dynamic_slice_in_dim(branch_grad_all, me * part, part, 2)
    grad_out = mm("ire,ird->ed", mixed_all, my_columns)
    out_w_rows = lax.dynamic_slice_in_dim(out_w, me * part, part, 0)
    mixed_grad = mm("ird,ed->ire", branch_grad_all, out_w_rows).astype(BF16).reshape(items, length, heads, DH)

    prob_grad = mm("iqhd,ikhd->ihqk", mixed_grad, values)
    delta = jnp.sum(probs * prob_grad, axis=-1, keepdims=True)
    score_grad = (probs * (prob_grad - delta)).astype(BF16)
    query_grad = mm("ihqk,ikhd->iqhd", score_grad, keys) * 0.125
    key_grad = mm("ihqk,iqhd->ikhd", score_grad, queries) * 0.125
    value_grad = mm("ihqk,iqhd->ikhd", probs_low, mixed_grad)
    merged_grad = jnp.concatenate(
        [term.reshape(items, length, part) for term in (query_grad, key_grad, value_grad)], axis=-1
    ).astype(BF16)
    wide = score_grad.astype(F32)
    kept = jnp.sum(jnp.where(same[:, None], wide, 0.0), axis=0)
    crossed = jnp.sum(jnp.where(same[:, None], 0.0, wide), axis=(0, 2, 3))
    skewed = jnp.pad(kept[:, :, ::-1], ((0, 0), (0, 0), (0, length))).reshape(heads, -1)
    skewed = skewed[:, : length * (2 * length - 1)].reshape(heads, length, 2 * length - 1)
    lines = jnp.sum(skewed, axis=1)
    middle_line = length - 1
    low_end = jnp.sum(lines[:, : middle_line - RR + 1], axis=1)
    high_end = jnp.sum(lines[:, middle_line + RR :], axis=1)
    near = lines[:, middle_line - RR + 1 : middle_line + RR]
    my_table_grad = jnp.concatenate([low_end[:, None], near, high_end[:, None], crossed[:, None]], axis=1).T
    table_grad = lax.psum(
        lax.dynamic_update_slice_in_dim(jnp.zeros((CLASSES, H), F32), my_table_grad, me * heads, 1), ("dp", "seq")
    )
    grad_embed, grad_gain, grad_pair = pair_pull(table_grad)

    grad_qkv = mm("ird,ire->de", first, merged_grad)
    first_grad = scatter(mm("ire,de->ird", merged_grad, qkv_w).astype(BF16), "seq", 1).astype(F32)
    my_norm, my_inv = mine(first_norm), mine(first_inv)
    d_shift_one = jnp.sum(first_grad, axis=1)
    d_scale_one = jnp.sum(first_grad * my_norm, axis=1)
    input_grad = middle_grad + norm_back(first_grad * (1.0 + scale_one), my_norm, my_inv)
    modulation_grad = jnp.concatenate(
        [d_shift_one, d_scale_one, d_gate_one, d_shift_two, d_scale_two, d_gate_two], axis=-1
    )
    modulation_grads = gather(lax.psum(modulation_grad, "seq"), "dp", 0)
    grad_ada = jnp.einsum("ic,ie->ce", squashed_part.astype(F32), modulation_grads, precision=HIGHEST)

    def owned(grad):
        return scatter(grad.astype(BF16), "dp", 0)

    def everyone(grad):
        return lax.all_gather(grad, "seq", axis=0)

    shares_qkv = everyone(owned(grad_qkv)).reshape(seq, shard, 3, part)
    shares_out = everyone(owned(grad_out))
    shares_gate_up = everyone(owned(grad_gate_up)).reshape(seq, shard, 2, dp, strip)
    shares_down = everyone(owned(grad_down))
    return (
        result,
        input_grad.astype(BF16),
        jnp.transpose(shares_qkv, (1, 2, 0, 3)).reshape(shard, -1).astype(F32),
        jnp.transpose(shares_out, (1, 0, 2)).reshape(shard, -1).astype(F32),
        jnp.transpose(shares_gate_up, (1, 2, 3, 0, 4)).reshape(shard, -1).astype(F32),
        shares_down.reshape(seq * strip, width).astype(F32),
        grad_ada,
        grad_embed,
        grad_gain,
        grad_pair,
    )


MESH = pl.DeviceIdType.MESH
LANES = 128


def nn(a, b):
    return jnp.dot(a, b, preferred_element_type=F32)


def nt(a, b):
    return lax.dot_general(a, b, (((1,), (1,)), ((), ())), preferred_element_type=F32)


def tn(a, b):
    return lax.dot_general(a, b, (((0,), (0,)), ((), ())), preferred_element_type=F32)


def skew(tile, back):
    row = lax.broadcasted_iota(jnp.int32, tile.shape, 0)
    for bit in range(7):
        turn = LANES - (1 << bit) if back else 1 << bit
        tile = jnp.where(((row >> bit) & 1) == 1, pltpu.roll(tile, turn, 1), tile)
    return tile


class Sizes:
    def __init__(self, rows, width, seq, dp, shard, down_shard, ada_rows, conditioning):
        self.rows, self.width, self.seq, self.dp = rows, width, seq, dp
        self.shard, self.ada_rows, self.conditioning = shard, ada_rows, conditioning
        self.strip = down_shard // seq
        self.length = rows * seq
        self.heads = H // seq
        self.part = self.heads * DH
        self.hidden = self.strip * dp
        self.far = dp // 2
        self.half = shard // 2
        self.blocks = self.length // LANES


def under(where, work):
    if where is None:
        work()
    else:
        pl.when(where)(work)


class Wires:
    def __init__(self, send, recv):
        self.send, self.recv, self.count, self.started = send, recv, 0, []

    def reserve(self, count=1):
        first = self.count
        self.count += count
        return first

    def make(self, number, source, target, device):
        return pltpu.make_async_remote_copy(
            src_ref=source,
            dst_ref=target,
            send_sem=self.send.at[number],
            recv_sem=self.recv.at[number],
            device_id=device,
            device_id_type=MESH,
        )

    def go(self, number, source, target, device, where=None):
        copy = self.make(number, source, target, device)
        under(where, copy.start)
        self.started.append((copy, where))
        return copy

    def settle(self, copy):
        copy.wait_send()
        self.started = [other for other in self.started if other[0] is not copy]

    def finish(self):
        for copy, where in self.started:
            under(where, copy.wait_send)
        self.started = []


def layer_kernel(sizes, names, *refs):
    r = types.SimpleNamespace(**dict(zip(names, refs, strict=True)))
    n = sizes
    rows, width, part, heads, length, hid = n.rows, n.width, n.part, n.heads, n.length, n.hidden
    half_rows = rows // 2
    d, s = lax.axis_index("dp"), lax.axis_index("seq")
    z, x = d // 2, lax.rem(d, 2)
    y, c = s // 2, lax.rem(s, 2)
    ox, oy, oc = 1 - x, 1 - y, 1 - c
    at_x = (z * 2 + ox, s)
    at_y = (d, oy * 2 + c)
    at_c = (d, y * 2 + oc)

    def z_plus(k):
        return lax.rem(z + k, n.far)

    def at_z(k):
        return (z_plus(k) * 2 + x, s)

    wires = Wires(r.send_sem, r.recv_sem)
    dp_peers = [(k, e) for k in range(n.far) for e in range(2) if k or e]
    seq_peers = [(1, 0), (0, 1), (1, 1)]

    def dp_peer(k, e):
        xx = lax.rem(x + e, 2)
        return z_plus(k) * 2 + xx, lax.rem(z + n.far - k, n.far) * 2 + xx

    def seq_peer(a, b):
        return lax.rem(y + a, 2) * 2 + lax.rem(c + b, 2)

    local_count = [0]

    def local(source, target):
        copy = pltpu.make_async_copy(source, target, r.local_sem.at[local_count[0]])
        local_count[0] += 1
        copy.start()
        return copy

    qkv_stage, gate_up_stage = r.second_t, r.gate_up_grads
    staged = [
        local(r.qkv.at[:, q * width : (q + 1) * width], qkv_stage.at[q * n.shard : (q + 1) * n.shard, 0:width])
        for q in range(3)
    ]
    staged_gate_up = [
        local(r.gate_up.at[:, q * 2 * hid : (q + 1) * 2 * hid], gate_up_stage.at[q * n.shard : (q + 1) * n.shard])
        for q in range(n.seq)
    ]
    own_shard = pl.ds(pl.multiple_of(d * n.shard, n.shard), n.shard)
    r.cond_all[d] = jnp.broadcast_to(r.condition[...].astype(F32), (8, n.conditioning))
    barrier = pltpu.get_barrier_semaphore()
    for k, e in dp_peers:
        pl.semaphore_signal(barrier, inc=1, device_id=(dp_peer(k, e)[0], s), device_id_type=MESH)
    for a, b in seq_peers:
        pl.semaphore_signal(barrier, inc=1, device_id=(d, seq_peer(a, b)), device_id_type=MESH)
    for copy in staged:
        copy.wait()
    for side in range(n.seq):

        @pl.when(s == side)
        def _():
            r.w_qkv[own_shard, :] = jnp.concatenate(
                [
                    qkv_stage[q * n.shard : (q + 1) * n.shard, side * part + h * DH : side * part + (h + 1) * DH]
                    for h in range(heads)
                    for q in range(3)
                ],
                axis=1,
            )

    pl.semaphore_wait(barrier, len(dp_peers) + len(seq_peers))

    class SeqGather:
        def __init__(self, block):
            self.block, self.first = block, wires.reserve(3)
            self.mine, self.from_y, self.from_c, self.from_yc = s, at_y[1], at_c[1], oy * 2 + oc

        def start(self, source=None):
            mine = self.block(self.mine)
            source = mine if source is None else source
            self.sent = [wires.go(self.first, source, mine, at_y), wires.go(self.first + 1, source, mine, at_c)]

        def hand_on(self):
            place = self.block(self.from_y)
            wires.make(self.first, place, place, at_y).wait_recv()
            self.sent.append(wires.go(self.first + 2, place, place, at_c))

        def settle(self):
            for copy in self.sent:
                wires.settle(copy)

        def wait_core(self):
            place = self.block(self.from_c)
            wires.make(self.first + 1, place, place, at_c).wait_recv()

        def wait_last(self):
            place = self.block(self.from_yc)
            wires.make(self.first + 2, place, place, at_c).wait_recv()

        def wait(self):
            self.hand_on()
            self.wait_core()
            self.wait_last()

    last_z = n.far - 1

    class Wave:
        def __init__(self, block, direct=False):
            self.block, self.first, self.direct = block, wires.reserve(4), direct

        def send(self, source=None):
            mine = self.block(z)
            source = mine if source is None else source
            wires.go(self.first + 1, source, mine, at_z(1), None if self.direct else z != last_z)
            wires.go(self.first + 3, source, mine, at_z(3), None if self.direct else z != 0)
            wires.go(self.first + 2, source, mine, at_z(2))

        def relay(self):
            place = self.block(z_plus(2))
            wires.make(self.first + 2, place, place, at_z(2)).wait_recv()
            if not self.direct:
                wires.go(self.first, place, place, at_z(1), z == last_z - 1)
                wires.go(self.first, place, place, at_z(3), z == 1)

        def arrive(self, k):
            place = self.block(z_plus(n.far - k))
            far_end = z == (0 if k == 1 else last_z)
            near = wires.make(self.first + k, place, place, at_z(k))
            if self.direct:
                near.wait_recv()
                return
            far = wires.make(self.first, place, place, at_z(k))
            under(far_end, far.wait_recv)
            under(jnp.logical_not(far_end), near.wait_recv)

    class DpGather:
        def __init__(self, source, place, direct=False):
            self.source, self.place, self.first = source, place, wires.reserve(n.far)
            self.wave = Wave(lambda zz: place(zz * 2 + x), direct)

        def start(self):
            mine = self.place(d)
            self.own = None if self.source is None else local(self.source, mine)
            wires.go(self.first, mine if self.source is None else self.source, mine, at_x)

        def along_z(self):
            self.wave.send(self.source)

        def across(self, k):
            place = self.place(z_plus(n.far - k) * 2 + x)
            wires.go(self.first + k, place, place, at_x)

        def relay(self):
            self.wave.relay()
            self.across(2)

        def hand_on(self):
            for k in (1, 3):
                self.wave.arrive(k)
                self.across(k)

        def wait(self):
            if self.own is not None:
                self.own.wait()
            for k in range(n.far):
                place = self.place(z_plus(n.far - k) * 2 + ox)
                wires.make(self.first + k, place, place, at_x).wait_recv()

    class DpGatherX:
        def __init__(self, source, place):
            self.source, self.place, self.first = source, place, wires.reserve()
            self.waves = Wave(lambda zz: place(zz * 2 + x)), Wave(lambda zz: place(zz * 2 + ox))

        def start(self):
            self.own = local(self.source, self.place(d))
            wires.go(self.first, self.source, self.place(d), at_x)

        def along_z(self):
            self.waves[0].send(self.source)

        def cross(self):
            place = self.place(z * 2 + ox)
            wires.make(self.first, place, place, at_x).wait_recv()
            self.waves[1].send()

        def relay(self, which):
            self.waves[which].relay()

        def wait(self):
            self.own.wait()
            for wave in self.waves:
                wave.arrive(1)
                wave.arrive(3)

    class SeqReduce:
        def __init__(self, sib, got, over, come):
            self.sib, self.got, self.over, self.come = sib, got, over, come
            self.first, self.sent = wires.reserve(3), []

        def put_core(self, index):
            def put(lanes, block):
                self.sib[index, :, lanes] = block.astype(BF16)

            return put

        def to_core(self, index):
            self.sent.append(wires.go(self.first + index, self.sib.at[index], self.got.at[index], at_c))

        def wait_far(self):
            wires.make(self.first + 1, self.sib.at[1], self.got.at[1], at_c).wait_recv()

        def put_y(self):
            def put(lanes, block):
                self.over[:, lanes] = (block + self.got[1, :, lanes].astype(F32)).astype(BF16)

            return put

        def to_y(self):
            self.sent.append(wires.go(self.first + 2, self.over, self.come, at_y))

        def settle(self):
            for copy in self.sent:
                wires.settle(copy)

        def wait(self):
            wires.make(self.first, self.sib.at[0], self.got.at[0], at_c).wait_recv()
            wires.make(self.first + 2, self.over, self.come, at_y).wait_recv()

        def total(self, own, place):
            return own[place, :] + self.got[0, place, :].astype(F32) + self.come[place, :].astype(F32)

    at_end = z * (last_z - z) == 0
    inside = z * (last_z - z) != 0

    def mirror(k):
        return (z, z + 1 - 2 * lax.rem(z, 2), lax.rem(z + 2, n.far), last_z - z)[k]

    def at_mirror(k):
        return (mirror(k) * 2 + x, s)

    class Shares:
        def __init__(self, mine, share):
            self.mine, self.share = mine, share
            self.gather = SeqGather(lambda t: share.at[t])

        def start(self):
            self.own = local(self.mine, self.share.at[s])
            self.gather.start(self.mine)

        def hand_on(self):
            self.gather.hand_on()

        def wait(self):
            self.gather.wait_core()
            self.gather.wait_last()
            self.own.wait()

    class DpReduce:
        def __init__(self, grad, got, come, far, mine, share):
            self.grad, self.got, self.come, self.far, self.mine = grad, got, come, far, mine
            self.first, self.second, self.shares = wires.reserve(n.far), wires.reserve(n.far), Shares(mine, share)

        def start(self):
            for k in (3, 1, 2, 0):
                to = mirror(k)
                wires.go(self.first + k, self.grad.at[ox, to], self.got.at[to], at_x)

        def along_z(self, k):
            to = mirror(k)
            block = self.grad.at[x, to]
            wires.make(self.first + k, self.grad.at[ox, to], self.got.at[to], at_x).wait_recv()
            block[...] = (block[...].astype(F32) + self.got[to].astype(F32)).astype(BF16)
            if k == 3:
                wires.go(self.second, block, self.far, at_mirror(1), at_end)
                wires.go(self.second + 3, block, self.come.at[0], at_mirror(3), inside)
            elif k == 1:
                wires.go(self.second + 1, block, self.come.at[2], at_mirror(1))
            elif k == 2:

                @pl.when(inside)
                def _():
                    wires.make(self.second, block, self.far, at_mirror(1)).wait_recv()
                    block[...] = (block[...].astype(F32) + self.far[...].astype(F32)).astype(BF16)

                wires.go(self.second + 2, block, self.come.at[1], at_mirror(2))

        def finish(self):
            for k in (2, 1):
                wires.make(self.second + k, self.mine, self.come.at[3 - k], at_mirror(k)).wait_recv()
            total = self.grad[x, z].astype(F32) + self.come[1].astype(F32) + self.come[2].astype(F32)

            @pl.when(at_end)
            def _():
                self.mine[...] = total.astype(BF16)

            @pl.when(inside)
            def _():
                wires.make(self.second + 3, self.mine, self.come.at[0], at_mirror(3)).wait_recv()
                self.mine[...] = (total + self.come[0].astype(F32)).astype(BF16)

            self.shares.start()

    class DpReduceZ:
        def __init__(self, grad, come, far, got, mine, share):
            self.grad, self.come, self.far, self.got, self.mine = grad, come, far, got, mine
            self.first, self.cross, self.shares = wires.reserve(4), wires.reserve(), Shares(mine, share)

        def start(self, which):
            ways = (
                (0, self.far, 1, at_end),
                (3, self.come.at[0], 3, inside),
                (1, self.come.at[2], 1, None),
                (2, self.come.at[1], 2, at_end),
            )
            for k, place, to, where in ways[2 * which : 2 * which + 2]:
                block = self.grad.at[:, mirror(k or 3)]
                wires.go(self.first + k, block, place, at_mirror(to), where)

        def merge(self):
            block = self.grad.at[:, mirror(2)]

            @pl.when(inside)
            def _():
                wires.make(self.first, block, self.far, at_mirror(1)).wait_recv()
                block[...] = (block[...].astype(F32) + self.far[...].astype(F32)).astype(BF16)

            wires.go(self.first + 2, block, self.come.at[1], at_mirror(2), inside)

        def across(self):
            block = self.grad.at[:, z]
            for k in (2, 1):
                wires.make(self.first + k, self.far, self.come.at[3 - k], at_mirror(k)).wait_recv()
            total = block[...].astype(F32) + self.come[1].astype(F32) + self.come[2].astype(F32)

            @pl.when(at_end)
            def _():
                block[...] = total.astype(BF16)

            @pl.when(inside)
            def _():
                wires.make(self.first + 3, self.far, self.come.at[0], at_mirror(3)).wait_recv()
                block[...] = (total + self.come[0].astype(F32)).astype(BF16)

            wires.go(self.cross, self.grad.at[ox, z], self.got, at_x)

        def finish(self):
            wires.make(self.cross, self.mine, self.got, at_x).wait_recv()
            self.mine[...] = (self.grad[x, z].astype(F32) + self.got[...].astype(F32)).astype(BF16)
            self.shares.start()

    step = 64

    def by_rows(count, work, start=0, unroll=2):
        def one(q, carry):
            return work(pl.ds(pl.multiple_of(q * step, step), step), carry)

        return lax.fori_loop(0, count // step, one, start, unroll=unroll)

    wide = 2 * LANES

    def by_lanes(count, work):
        def one(q, _):
            work(pl.ds(pl.multiple_of(q * wide, wide), wide))
            return 0

        lax.fori_loop(0, count // wide, one, 0, unroll=True)

    def fold_rows(array):
        return jnp.sum(array.reshape(step // 8, 8, width), axis=0)

    hidden_all, grads_all = r.hidden_all, r.grads_all

    def rows_of(ref):
        return lambda t: ref.at[pl.ds(pl.multiple_of(t * rows, rows), rows)]

    hidden_gather, up_gather = SeqGather(rows_of(hidden_all)), SeqGather(rows_of(grads_all))
    def shard_rows(ref, height, lanes=slice(None)):
        return lambda t: ref.at[pl.ds(pl.multiple_of(t * height, height), height), lanes]

    def lane_half(side):
        return pl.ds(pl.multiple_of(side * (width // 2), width // 2), width // 2)

    lanes_y = lane_half(y)
    qkv_gathers = [
        DpGather(None, shard_rows(r.w_qkv, n.shard, lanes), True)
        for lanes in (slice(0, 2 * LANES), slice(2 * LANES, 3 * part))
    ]
    out_gather = DpGather(
        r.out.at[pl.ds(pl.multiple_of(c * n.half, n.half), n.half), lanes_y],
        lambda t: r.w_out.at[t, c, :, lanes_y],
    )
    half_strip = n.strip // 2

    def down_half(kind, side):
        low = side * half_strip
        return kind(
            r.down.at[pl.ds(pl.multiple_of(s * n.strip + low, half_strip), half_strip)],
            lambda t: r.w_down.at[pl.ds(pl.multiple_of(t * n.strip + low, half_strip), half_strip)],
        )

    down_near, down_gather = down_half(DpGather, 0), down_half(DpGatherX, 1)
    pieces = [
        DpGather(None, shard_rows(r.w_gate_up, n.shard, slice(q * (hid // 2), (q + 1) * (hid // 2))))
        for q in (0, 2, 1, 3)
    ]

    def out_block(t):
        ty, tc = t // 2, lax.rem(t, 2)
        return r.w_out.at[:, tc, :, lane_half(ty)]

    out_share = SeqGather(out_block)

    cond_first, mod_first = wires.reserve(len(dp_peers)), wires.reserve(len(dp_peers))
    cond_all, mod_send, mod_recv = r.cond_all, r.mod_send, r.mod_recv
    for i, (k, e) in enumerate(dp_peers):
        wires.go(cond_first + i, cond_all.at[d], cond_all.at[d], (dp_peer(k, e)[0], s))
    for piece in qkv_gathers:
        piece.along_z()
        piece.start()
    own_hidden = local(r.hidden, hidden_gather.block(s))
    keep_hidden = local(r.hidden, r.hidden_own)
    keep_grads = local(r.out_grad, r.upstream)
    hidden_gather.start(r.hidden)
    own_grads = local(r.out_grad, up_gather.block(s))


    for i, (k, e) in enumerate(dp_peers):
        place = cond_all.at[dp_peer(k, e)[1]]
        wires.make(cond_first + i, place, place, (dp_peer(k, e)[0], s)).wait_recv()
    item_of = lax.broadcasted_iota(jnp.int32, (n.dp, n.conditioning), 0)
    conditions = jnp.where(item_of == 0, cond_all[0], 0.0)
    for i in range(1, n.dp):
        conditions = jnp.where(item_of == i, cond_all[i], conditions)
    squashed = (conditions * (1.0 / (1.0 + jnp.exp(-conditions)))).astype(BF16).astype(F32)
    r.squashed[...] = squashed.T
    squashed_rows = r.squashed[pl.ds(pl.multiple_of(d * n.ada_rows, n.ada_rows), n.ada_rows), :]
    ada_part = tn(squashed_rows.astype(BF16), r.ada[...])
    for i in range(n.dp):
        mod_send[i] = ada_part[i : i + 1]
    mod_recv[d] = mod_send[d]
    for i, (k, e) in enumerate(dp_peers):
        wires.go(mod_first + i, mod_send.at[dp_peer(k, e)[0]], mod_recv.at[d], (dp_peer(k, e)[0], s))
    for copy in staged_gate_up:
        copy.wait()
    group = n.seq * n.strip
    for side in range(n.seq):

        @pl.when(s == side)
        def _():
            strips = []
            for number in range(2 * n.dp):
                block, low = divmod(number * group, 2 * hid)
                low += side * n.strip
                strips.append(gate_up_stage[block * n.shard : (block + 1) * n.shard, low : low + n.strip])
            r.w_gate_up[own_shard, :] = jnp.concatenate(strips, axis=1)

    for piece in (out_gather, *pieces[:2]):
        piece.start()
        piece.along_z()
    down_gather.start()
    down_gather.along_z()
    down_near.start()
    down_near.along_z()
    for piece in pieces[2:]:
        piece.start()
    hidden_gather.hand_on()
    up_gather.start(r.out_grad)
    for piece in qkv_gathers:
        piece.relay()
        piece.hand_on()

    bias, table_t = r.bias, r.table_t
    embed = r.pair_embed[...].astype(F32)
    normal, _ = layer_norm(embed, 1e-05)
    scaled = normal * r.pair_gain[...].astype(F32)
    scaled = jnp.concatenate([scaled, jnp.zeros((LANES - CLASSES, scaled.shape[1]), F32)], axis=0)
    table_t[...] = lax.dot_general(
        r.pair_weight[...].astype(F32),
        scaled,
        (((1,), (1,)), ((), ())),
        precision=HIGHEST,
        preferred_element_type=F32,
    )

    def table_line(h):
        return table_t[pl.ds(s * heads + h, 1), :]

    key_in = lax.broadcasted_iota(jnp.int32, (LANES, LANES), 0)
    query_in = lax.broadcasted_iota(jnp.int32, (LANES, LANES), 1)
    middle_tile = n.blocks - 1

    def build_bias(h, _):
        line = table_line(h)
        near = skew(jnp.broadcast_to(pltpu.roll(line, LANES - RR, 1), (LANES, LANES)), False)
        low_end = jnp.broadcast_to(line[:, 0:1], (LANES, LANES))
        high_end = jnp.broadcast_to(line[:, 2 * RR : 2 * RR + 1], (LANES, LANES))
        for tile in range(2 * n.blocks - 1):
            away = tile - middle_tile
            apart = query_in - key_in - away * LANES
            if away < -1:
                value = high_end
            elif away > 1:
                value = low_end
            else:
                value = jnp.where(apart >= RR, high_end, jnp.where(apart <= -RR, low_end, near))
            bias[h, tile * LANES : (tile + 1) * LANES] = value
        return 0

    lax.fori_loop(0, heads, build_bias, 0)

    own_hidden.wait()
    hidden_gather.wait_core()
    hidden_gather.wait_last()
    for i, (k, e) in enumerate(dp_peers):
        place = mod_recv.at[dp_peer(k, e)[1]]
        wires.make(mod_first + i, mod_send.at[d], place, (dp_peer(k, e)[0], s)).wait_recv()
    modulation = mod_recv[0]
    for i in range(1, n.dp):
        modulation = modulation + mod_recv[i]
    r.modulation[...] = modulation

    def vector(index):
        return r.modulation[:, index * width : (index + 1) * width]

    shift_one, scale_one, gate_one, shift_two, scale_two, gate_two = range(6)
    first = hidden_all
    hidden_gather.settle()

    def make_first(t, _):
        place = pl.ds(pl.multiple_of(t * LANES, LANES), LANES)
        normal, _ = layer_norm(hidden_all[place, :].astype(F32))
        first[place, :] = (normal * (1.0 + vector(scale_one)) + vector(shift_one)).astype(BF16)
        r.norm_t[:, place] = normal.astype(BF16).T
        return 0

    lax.fori_loop(0, n.blocks, make_first, 0, unroll=2)
    few_rows = jnp.concatenate([vector(q) for q in range(6)] + [vector(0)] * 2, axis=0)
    r.mod_t[...] = few_rows.T
    out_gather.relay()
    out_gather.hand_on()
    pieces[0].relay()

    for piece in qkv_gathers:
        piece.wait()
    w_qkv = r.w_qkv
    keys = r.keys
    keys_t, values_t, queries_t = r.keys_t, r.values_t, r.queries_t
    w_qkv_t = r.inner_t

    def turn_weight(q, _):
        place = pl.ds(pl.multiple_of(q * 2 * LANES, 2 * LANES), 2 * LANES)
        w_qkv_t[0 : 3 * part, place] = w_qkv[place, :].T
        return 0

    lax.fori_loop(0, width // (2 * LANES), turn_weight, 0)

    def project(t, _):
        place = pl.ds(pl.multiple_of(t * rows, rows), rows)
        block = first[place, :]
        for low in range(0, 3 * part, wide):
            merged = nn(block, w_qkv[:, low : min(low + wide, 3 * part)]).astype(BF16)
            for q in range(merged.shape[1] // DH):
                h, kind = divmod(low // DH + q, 3)
                if kind == 1:
                    keys[h, place, :] = merged[:, q * DH : (q + 1) * DH]
        for h in range(heads):
            merged_t = nt(w_qkv_t[h * 3 * DH : (h + 1) * 3 * DH, 0:width], block).astype(BF16)
            queries_t[h, t] = (merged_t[:DH].astype(F32) * 0.125).astype(BF16)
            keys_t[h, t] = merged_t[DH : 2 * DH]
            values_t[h, t] = merged_t[2 * DH :]
        return 0

    lax.fori_loop(0, n.seq, project, 0)
    pieces[0].hand_on()
    down_gather.cross()
    for piece in pieces[2:]:
        piece.along_z()
    pieces[1].relay()

    valid, broken = r.valid_len[0], r.chain_break[0]
    exps, outs_t, inverse = r.exps, r.outs_t, r.inverse
    tiles = rows // LANES
    order = [oy * 2 + c, oy * 2 + oc, y * 2 + oc, s]

    raw = r.raw

    def tile_parts(t, tile):
        number = t * tiles + tile
        query_side = number * LANES + lax.broadcasted_iota(jnp.int32, (1, LANES), 1) >= broken
        for q in range(n.blocks):
            key_pos = q * LANES + lax.broadcasted_iota(jnp.int32, (LANES, LANES), 0)
            strip = pl.ds(pl.multiple_of((n.blocks - 1 + q - number) * LANES, LANES), LANES)
            yield slice(q * LANES, (q + 1) * LANES), strip, key_pos, (key_pos >= broken) == query_side

    def eights(array):
        return array.reshape(LANES // 8, 8, LANES)

    def attend(t):
        def one_head(h, _):
            for q in range(n.seq):
                place = slice(q * rows, (q + 1) * rows)
                raw[place, 0:rows] = nn(keys[h, place, :], queries_t[h, t])
            for tile in range(tiles):
                lanes = slice(tile * LANES, (tile + 1) * LANES)
                far_side = jnp.broadcast_to(table_line(h)[:, CLASSES - 1 : CLASSES], (1, LANES))
                top = jnp.full((8, LANES), -1e30, F32)
                for place, strip, key_pos, same in tile_parts(t, tile):
                    logits = raw[place, lanes] + jnp.where(same, bias[h, strip, :], far_side)
                    logits = jnp.where(key_pos < valid, logits, -1e30)
                    raw[place, lanes] = logits
                    top = jnp.maximum(top, jnp.max(eights(logits), axis=0))
                top = jnp.max(top, axis=0, keepdims=True)
                total = jnp.zeros((8, LANES), F32)
                for q in range(n.blocks):
                    place = slice(q * LANES, (q + 1) * LANES)
                    powers = jnp.exp(raw[place, lanes] - top)
                    total = total + jnp.sum(eights(powers), axis=0)
                    exps[h, t, place, lanes] = powers.astype(BF16)
                inverse[h, t, :, lanes] = 1.0 / jnp.sum(total, axis=0, keepdims=True)
            values_wide = jnp.concatenate([values_t[h, q] for q in range(n.seq)], axis=1)
            outs_t[h, t] = nn(values_wide, exps[h, t]) * inverse[h, t]
            return 0

        lax.fori_loop(0, heads, one_head, 0)

    mixed_first = wires.reserve(3)
    mixed_send, mixed_recv = r.mixed_send, r.mixed_recv
    mixed_sent = []
    to_send = [at_y, (d, oy * 2 + oc), at_c]
    out_gather.wait()
    out_share.start()
    for i, t in enumerate(order):
        attend(t)
        block = jnp.concatenate([outs_t[h, t] for h in range(heads)], axis=0).T.astype(BF16)
        if i < 3:
            mixed_send[i] = block
            mixed_sent.append(wires.go(mixed_first + i, mixed_send.at[i], mixed_recv.at[s], to_send[i]))
        else:
            mixed_recv[s] = block
        if i == 1:
            pieces[1].hand_on()
            down_gather.relay(0)
        if i == 2:
            down_near.relay()
        if i == 3:
            down_near.hand_on()
        if i == 0:
            up_gather.hand_on()
        if i == 1:
            out_share.hand_on()

    out_share.wait_core()
    out_share.wait_last()

    def w_out(q, lanes=slice(None)):
        shards = part // n.shard
        block = r.w_out[q * shards : (q + 1) * shards, :, :, lanes]
        return block.reshape(part, block.shape[-1])

    for i in range(3):
        place = mixed_recv.at[order[i]]
        wires.make(mixed_first + i, mixed_send.at[i], place, to_send[i]).wait_recv()
    keep_hidden.wait()

    def make_branch(lanes):
        branch = nn(mixed_recv[0], w_out(0, lanes))
        for q in range(1, n.seq):
            branch = branch + nn(mixed_recv[q], w_out(q, lanes))
        r.branch[:, lanes] = branch

    by_lanes(width, make_branch)
    second_all = r.second_all
    second_gather = SeqGather(rows_of(second_all))

    def make_second(place, _):
        middle = r.hidden_own[place, :].astype(F32) + vector(gate_one) * r.branch[place, :]
        r.middle[place, :] = middle
        normal, _ = layer_norm(middle)
        r.branch_grad[place, :] = (normal * (1.0 + vector(scale_two)) + vector(shift_two)).astype(BF16)
        return 0

    by_rows(rows, make_second)
    second_all[pl.ds(pl.multiple_of(s * rows, rows), rows), :] = r.branch_grad[...]
    second_gather.start()

    own_grads.wait()
    up_gather.wait_core()
    up_gather.wait_last()
    up_gather.settle()
    feed_grads = grads_all

    def make_feed_grads(place, _):
        feed_grads[place, :] = (vector(gate_two) * grads_all[place, :].astype(F32)).astype(BF16)
        return 0

    by_rows(length, make_feed_grads)
    down_gather.relay(1)
    for piece in (pieces[0], pieces[1], down_near, down_gather):
        piece.wait()
    w_gate_up, w_down = r.w_gate_up, r.w_down
    inner, inner_t, gate_up_grads, second_t = r.inner, r.inner_t, r.gate_up_grads, r.second_t
    feed_places = (r.feed_sib, r.feed_got, r.feed_over, r.feed_come)
    feed_reduce = SeqReduce(*feed_places)
    second_reduce = SeqReduce(r.second_sib, r.second_got, r.second_over, r.second_come)
    half_hid = hid // 2

    def rows_at(t):
        return pl.ds(pl.multiple_of(t * rows, rows), rows)

    def units(t, side):
        place, low = rows_at(t), side * half_hid
        block, given = second_all[place, :], feed_grads[place, :]
        gates, ups, inner_grads = (raw.at[i * rows : (i + 1) * rows] for i in range(3))
        gates[...] = nn(block, w_gate_up[:, low : low + half_hid])
        ups[...] = nn(block, w_gate_up[:, hid + low : hid + low + half_hid])
        inner_grads[...] = nt(given, w_down[low : low + half_hid, :])
        for first_row in range(0, rows, step):
            few = slice(first_row, first_row + step)
            gate, up, inner_grad = gates[few, :], ups[few, :], inner_grads[few, :]
            sigmoid = 1.0 / (1.0 + jnp.exp(-gate))
            silu = gate * sigmoid
            to = pl.ds(pl.multiple_of(t * rows + first_row, step), step)
            inner[to, low : low + half_hid] = (silu * up).astype(BF16)
            gate_up_grads[to, low : low + half_hid] = (
                inner_grad * up * sigmoid * (1.0 + gate * (1.0 - sigmoid))
            ).astype(BF16)
            gate_up_grads[to, hid + low : hid + low + half_hid] = (inner_grad * silu).astype(BF16)

    def second_part(t, put):
        by_lanes(width, lambda lanes: put(lanes, nt(gate_up_grads[rows_at(t), :], w_gate_up[lanes, :])))

    def feed_part(t, put):
        by_lanes(width, lambda lanes: put(lanes, nn(inner[rows_at(t), :], w_down[:, lanes])))

    def put_in(ref):
        def put(lanes, block):
            ref[:, lanes] = block.astype(ref.dtype)

        return put

    units(s, 0)
    second_gather.wait_core()
    units(y * 2 + oc, 0)
    second_gather.hand_on()
    pieces[2].relay()
    units(oy * 2 + c, 0)
    pieces[2].hand_on()
    pieces[3].relay()
    second_gather.wait_last()
    units(oy * 2 + oc, 0)
    pieces[3].hand_on()

    gate_up_reduces = (
        DpReduce(r.gate_up0_grad, r.gate_up0_got, r.gate_up0_come, r.gate_up0_far, r.gate_up0_mine, r.gate_up0_share),
        DpReduce(r.gate_up1_grad, r.gate_up1_got, r.gate_up1_come, r.gate_up1_far, r.gate_up1_mine, r.gate_up1_share),
    )
    down_reduce = DpReduceZ(r.down_grad, r.down_come, r.down_far, r.down_got, r.down_mine, r.down_share)
    out_reduce = DpReduce(r.proj_grad, r.proj_got, r.proj_come, r.proj_far, r.proj_mine, r.proj_share)
    qkv_reduces = (
        DpReduce(r.qkv0_grad, r.qkv0_got, r.qkv0_come, r.qkv0_far, r.qkv0_mine, r.qkv0_share),
        DpReduce(r.qkv1_grad, r.qkv1_got, r.qkv1_come, r.qkv1_far, r.qkv1_mine, r.qkv1_share),
        DpReduce(r.qkv2_grad, r.qkv2_got, r.qkv2_come, r.qkv2_far, r.qkv2_mine, r.qkv2_share),
    )

    def turn_rows(source, target):
        def turn(t, _):
            target[:, rows_at(t)] = source[rows_at(t), :].T
            return 0

        lax.fori_loop(0, n.seq, turn, 0)

    def weight_grad(left_t, right, reduce, lows):
        height, few = reduce.grad.shape[2], n.dp // 2
        columns = reduce.grad.shape[3] // len(lows)
        for at, low in enumerate(lows):
            for first_of in range(0, n.dp, few):
                grad = nn(
                    left_t[first_of * height : (first_of + few) * height, :], right[:, low : low + columns]
                ).astype(BF16)
                for i in range(few):
                    to = first_of + i
                    reduce.grad[to % 2, to // 2, :, at * columns : (at + 1) * columns] = grad[
                        i * height : (i + 1) * height
                    ]

    turn_rows(second_all, second_t)
    weight_grad(second_t, gate_up_grads, gate_up_reduces[0], (0, hid))
    gate_up_reduces[0].start()
    pieces[2].wait()
    pieces[3].wait()
    far, over, near = oy * 2 + oc, oy * 2 + c, y * 2 + oc
    units(far, 1)
    second_part(far, second_reduce.put_core(1))
    second_reduce.to_core(1)
    units(over, 1)
    second_reduce.wait_far()
    second_part(over, second_reduce.put_y())
    second_reduce.to_y()
    units(near, 1)
    second_part(near, second_reduce.put_core(0))
    second_reduce.to_core(0)
    units(s, 1)
    second_part(s, put_in(r.second_own))

    weight_grad(second_t, gate_up_grads, gate_up_reduces[1], (half_hid, hid + half_hid))
    gate_up_reduces[1].start()
    gate_up_reduces[0].along_z(3)
    turn_rows(inner, inner_t)
    weight_grad(inner_t, feed_grads, down_reduce, (0, half_hid))
    down_reduce.start(0)
    gate_up_reduces[0].along_z(1)
    down_reduce.start(1)
    feed_part(far, feed_reduce.put_core(1))
    feed_reduce.to_core(1)
    feed_part(near, feed_reduce.put_core(0))
    feed_reduce.to_core(0)
    feed_reduce.wait_far()
    feed_part(over, feed_reduce.put_y())
    feed_part(s, put_in(r.feed_own))
    lax.fori_loop(0, width // (2 * LANES), turn_weight, 0)
    values = keys

    def turn_values(t, _):
        for h in range(heads):
            values[h, rows_at(t), :] = values_t[h, t].T
        return 0

    lax.fori_loop(0, n.seq, turn_values, 0)

    sums = r.mod_sums

    upstream = r.upstream
    keep_grads.wait()
    second_reduce.wait()
    kept_middle_grad, branch_grad = r.second_own, r.branch_grad
    empty = jnp.zeros((8, width), F32)

    def put_sum(index, array):
        sums[s, :, index * width : (index + 1) * width] = jnp.sum(array, axis=0, keepdims=True)

    def second_back(place, carry):
        second_grad = second_reduce.total(r.second_own, place)
        normal, inverted = layer_norm(r.middle[place, :])
        middle_grad = upstream[place, :].astype(F32) + norm_back(
            second_grad * (1.0 + vector(scale_two)), normal, inverted
        )
        kept_middle_grad[place, :] = middle_grad
        branch_grad[place, :] = (vector(gate_one) * middle_grad).astype(BF16)
        terms = (second_grad, second_grad * normal, middle_grad * r.branch[place, :])
        return tuple(total + fold_rows(term) for total, term in zip(carry, terms))

    for index, total in zip(
        (shift_two, scale_two, gate_one), by_rows(rows, second_back, (empty, empty, empty))
    ):
        put_sum(index, total)
    back_first = wires.reserve(3)
    for copy in mixed_sent:
        wires.settle(copy)
    back_all, back_recv = mixed_send, r.back_recv
    for q in range(n.seq):
        back_all[q] = nt(branch_grad[...], w_out(q)).astype(BF16)
    for i in range(3):
        wires.go(back_first + i, back_all.at[order[i]], back_recv.at[s], to_send[i])
    back_recv[s] = back_all[s]
    feed_reduce.to_y()

    out_first = wires.reserve(2)
    second_gather.settle()
    out_parts, quarter = second_all, n.dp * n.half

    def make_out_grad(lanes):
        for q in range(n.seq):
            grad = tn(mixed_recv[q], branch_grad[:, lanes]).astype(BF16)
            for i in range(part // n.half):
                number = q * (part // n.half) + i
                low = (number % 2) * quarter + (number // 2) * n.half
                out_parts[low : low + n.half, lanes] = grad[i * n.half : (i + 1) * n.half]

    by_lanes(width, make_out_grad)

    def out_rows(core):
        return out_parts.at[pl.ds(pl.multiple_of(core * quarter, quarter), quarter)]

    lanes_oy = pl.ds(pl.multiple_of(oy * (width // 2), width // 2), width // 2)

    def out_cores():
        wires.make(out_first, out_rows(oc), r.out_near, at_c).wait_recv()
        mine = out_parts[pl.ds(pl.multiple_of(c * quarter, quarter), quarter), :]
        r.out_near[...] = (r.out_near[...].astype(F32) + mine.astype(F32)).astype(BF16)
        wires.go(out_first + 1, r.out_near.at[:, lanes_oy], r.out_far, at_y)

    def out_sum():
        wires.make(out_first + 1, r.out_near.at[:, lanes_oy], r.out_far, at_y).wait_recv()
        total = (r.out_near[:, lanes_y].astype(F32) + r.out_far[...].astype(F32)).astype(BF16)
        for to in range(n.dp):
            r.proj_grad[to % 2, to // 2] = total[to * n.half : (to + 1) * n.half]
        out_reduce.start()

    dots_t, delta = r.dots_t, r.delta
    pair_grads, query_grads = r.pair_grads, r.query_grads
    bias[...] = jnp.zeros_like(bias)
    crossed, score_grad = r.crossed, inner.at[:, 0:rows]
    crossed[...] = jnp.zeros_like(crossed)
    merged_grads = gate_up_grads

    def take_back(t):
        given_t = back_recv[t].T.astype(F32)
        for h in range(heads):
            scaled = (given_t[h * DH : (h + 1) * DH] * inverse[h, t]).astype(BF16)
            dots_t[h, t] = scaled
            delta[h, t] = jnp.sum(scaled.astype(F32) * outs_t[h, t], axis=0, keepdims=True)

    def attend_back(h, t, first_of):
        place = rows_at(t)
        for q in range(n.seq):
            some = slice(q * rows, (q + 1) * rows)
            raw[some, 0:rows] = nn(values[h, some, :], dots_t[h, t])
        for tile in range(tiles):
            lanes = slice(tile * LANES, (tile + 1) * LANES)
            across = jnp.zeros((8, LANES), F32)
            for keys_of, strip, _, same in tile_parts(t, tile):
                grad = exps[h, t, keys_of, lanes].astype(F32) * (raw[keys_of, lanes] - delta[h, t, :, lanes])
                kept = jnp.where(same, grad, 0.0)
                bias[h, strip, :] = bias[h, strip, :] + kept
                across = across + jnp.sum(eights(grad - kept), axis=0)
                score_grad[keys_of, lanes] = grad.astype(BF16)
            crossed[h] = crossed[h] + jnp.sum(across, axis=0, keepdims=True)
        keys_wide = jnp.concatenate([keys_t[h, q] for q in range(n.seq)], axis=1)
        query_grads[place, :] = (nn(keys_wide, score_grad[...]) * 0.125).T.astype(BF16)
        queries, dots = queries_t[h, t].T, dots_t[h, t].T
        for q in range(n.seq):
            some = slice(q * rows, (q + 1) * rows)
            grad = jnp.concatenate([nn(score_grad[some, :], queries), nn(exps[h, t, some, :], dots)], axis=1)
            pair_grads[some, :] = grad if first_of else pair_grads[some, :] + grad

    def end_head(h):
        for q in range(n.seq):
            some = slice(q * rows, (q + 1) * rows)
            merged_grads[some, h * wide : h * wide + 3 * DH] = jnp.concatenate(
                [query_grads[some, :], pair_grads[some, :].astype(BF16)], axis=1
            )
        merged = merged_grads.at[:, h * wide : h * wide + 3 * DH]
        totals = nn(jnp.ones((16, length), BF16), merged[...])[0:1]
        few = n.dp // 2 * n.shard
        for first_of in range(0, width, few):
            place = slice(first_of, first_of + few)
            scale, shift = 1.0 + r.mod_t[place, 1:2], r.mod_t[place, 0:1]
            weights = w_qkv[place, h * 3 * DH : (h + 1) * 3 * DH].astype(F32)
            product = nn(r.norm_t[place, :], merged[...])
            d_shift = jnp.sum(weights * totals, axis=1, keepdims=True)
            d_scale = jnp.sum(weights * product, axis=1, keepdims=True)
            lane = lax.broadcasted_iota(jnp.int32, (few, LANES), 1)
            both = jnp.where(lane == 0, d_shift, jnp.where(lane == 1, d_scale, 0.0))
            r.first_sums[place, :] = both if h == 0 else r.first_sums[place, :] + both
            grad = (product * scale + totals * shift).astype(BF16)
            for i in range(n.dp // 2):
                to = first_of // n.shard + i
                low = i * n.shard
                qkv_reduces[h].grad[to % 2, to // 2] = jnp.concatenate(
                    [grad[low : low + n.half], grad[low + n.half : low + n.shard]], axis=1
                )
        qkv_reduces[h].start()

    def back_block(i):
        wires.make(back_first + i, back_recv.at[order[i]], back_recv.at[order[i]], to_send[i]).wait_recv()
        take_back(order[i])

    def rest_of_head(h, start):
        def one(i, _):
            attend_back(h, lax.rem(y + i // 2, 2) * 2 + lax.rem(c + lax.rem(i, 2), 2), False)
            return 0

        lax.fori_loop(start, n.seq, one, 0)

    wires.go(out_first, out_rows(oc), r.out_near, at_c)
    gate_up_reduces[0].along_z(2)
    gate_up_reduces[0].along_z(0)
    gate_up_reduces[1].along_z(3)
    take_back(s)
    attend_back(0, s, True)
    back_block(2)
    attend_back(0, order[2], False)
    gate_up_reduces[1].along_z(1)
    out_cores()
    back_block(0)
    attend_back(0, order[0], False)
    back_block(1)
    attend_back(0, order[1], False)
    end_head(0)
    attend_back(1, s, True)
    rest_of_head(1, 1)
    end_head(1)
    down_reduce.merge()
    attend_back(2, s, True)
    rest_of_head(2, 1)
    end_head(2)

    second_reduce.settle()
    first_reduce = SeqReduce(r.second_sib, r.second_got, r.second_over, r.second_come)

    def first_part(t, put):
        def by_heads(lanes):
            total = nn(merged_grads[rows_at(t), 0 : 3 * DH], w_qkv_t[0 : 3 * DH, lanes])
            for h in range(1, heads):
                total = total + nn(
                    merged_grads[rows_at(t), h * wide : h * wide + 3 * DH],
                    w_qkv_t[h * 3 * DH : (h + 1) * 3 * DH, lanes],
                )
            put(lanes, total)

        by_lanes(width, by_heads)

    first_part(oy * 2 + oc, first_reduce.put_core(1))
    first_reduce.to_core(1)
    first_reduce.wait_far()
    first_part(oy * 2 + c, first_reduce.put_y())
    first_reduce.to_y()
    first_part(y * 2 + oc, first_reduce.put_core(0))
    first_reduce.to_core(0)
    first_part(s, put_in(r.branch))
    gate_up_reduces[1].along_z(2)
    gate_up_reduces[1].along_z(0)
    for k in (3, 1, 2, 0):
        qkv_reduces[0].along_z(k)
    qkv_reduces[1].along_z(3)
    feed_reduce.wait()

    def make_result(place, total):
        feed = feed_reduce.total(r.feed_own, place)
        r.result[place, :] = (r.middle[place, :] + vector(gate_two) * feed).astype(BF16)
        return total + fold_rows(upstream[place, :].astype(F32) * feed)

    put_sum(gate_two, by_rows(rows, make_result, empty))
    turned = r.first_sums[...].T
    put_sum(shift_one, turned[0:1])
    put_sum(scale_one, turned[1:2])
    sums_first = wires.reserve(3)
    for i, (a, b) in enumerate(seq_peers):
        wires.go(sums_first + i, sums.at[s], sums.at[s], (d, seq_peer(a, b)))
    qkv_reduces[1].along_z(1)
    down_reduce.across()
    qkv_reduces[2].along_z(3)
    qkv_reduces[1].along_z(2)
    qkv_reduces[1].along_z(0)
    out_sum()
    qkv_reduces[2].along_z(1)

    table_sums, table_all = r.table_sums, r.table_all

    def fold(h, _):
        lane = lax.broadcasted_iota(jnp.int32, (1, LANES), 1)
        near = jnp.zeros((LANES, LANES), F32)
        low_end = jnp.zeros((LANES, LANES), F32)
        high_end = jnp.zeros((LANES, LANES), F32)
        for tile in range(2 * n.blocks - 1):
            away = tile - middle_tile
            apart = query_in - key_in - away * LANES
            value = bias[h, tile * LANES : (tile + 1) * LANES]
            if away < -1:
                high_end = high_end + value
            elif away > 1:
                low_end = low_end + value
            else:
                high_end = high_end + jnp.where(apart >= RR, value, 0.0)
                low_end = low_end + jnp.where(apart <= -RR, value, 0.0)
                near = near + jnp.where((apart < RR) & (apart > -RR), value, 0.0)
        line = jnp.sum(skew(near, True), axis=0, keepdims=True)
        for where, array in ((40, low_end), (41, high_end), (42, crossed[h])):
            line = jnp.where(lane == where, jnp.sum(array), line)
        table_sums[d, h] = line
        return 0

    lax.fori_loop(0, heads, fold, 0)
    table_first = wires.reserve(len(dp_peers))
    for i, (k, e) in enumerate(dp_peers):
        wires.go(table_first + i, table_sums.at[d], table_sums.at[d], (dp_peer(k, e)[0], s))

    for i, (a, b) in enumerate(seq_peers):
        place = sums.at[seq_peer(a, b)]
        wires.make(sums_first + i, place, place, (d, seq_peer(a, b))).wait_recv()
    mod_total = sums[0]
    for i in range(1, n.seq):
        mod_total = mod_total + sums[i]
    mod_totals = r.mod_totals
    mod_totals[d] = mod_total
    totals_first = wires.reserve(len(dp_peers))
    for i, (k, e) in enumerate(dp_peers):
        wires.go(totals_first + i, mod_totals.at[d], mod_totals.at[d], (dp_peer(k, e)[0], s))
    qkv_reduces[2].along_z(2)
    qkv_reduces[2].along_z(0)
    gate_up_reduces[0].finish()
    gate_up_reduces[1].finish()
    down_reduce.finish()
    out_reduce.along_z(3)
    first_reduce.wait()

    def first_back(place, _):
        first_grad = first_reduce.total(r.branch, place)
        normal, inverted = layer_norm(r.hidden_own[place, :].astype(F32))
        r.input_grad[place, :] = (
            kept_middle_grad[place, :] + norm_back(first_grad * (1.0 + vector(scale_one)), normal, inverted)
        ).astype(BF16)
        return 0

    by_rows(rows, first_back)
    for k in (1, 2, 0):
        out_reduce.along_z(k)
    for reduce in qkv_reduces:
        reduce.finish()
    for reduce in (*gate_up_reduces, down_reduce):
        reduce.shares.hand_on()
    for i, (k, e) in enumerate(dp_peers):
        place = table_sums.at[dp_peer(k, e)[1]]
        wires.make(table_first + i, place, place, (dp_peer(k, e)[0], s)).wait_recv()
    total = table_sums[0]
    for i in range(1, n.dp):
        total = total + table_sums[i]
    table_all[s] = total
    table_second = wires.reserve(3)
    for i, (a, b) in enumerate(seq_peers):
        wires.go(table_second + i, table_all.at[s], table_all.at[s], (d, seq_peer(a, b)))
    out_reduce.finish()
    for i, (k, e) in enumerate(dp_peers):
        place = mod_totals.at[dp_peer(k, e)[1]]
        wires.make(totals_first + i, place, place, (dp_peer(k, e)[0], s)).wait_recv()
    squashed_rows = r.squashed[pl.ds(pl.multiple_of(d * n.ada_rows, n.ada_rows), n.ada_rows), :]
    ada = squashed_rows[:, 0:1] * mod_totals[0]
    for i in range(1, n.dp):
        ada = ada + squashed_rows[:, i : i + 1] * mod_totals[i]
    r.grad_ada[...] = ada
    for i, (a, b) in enumerate(seq_peers):
        place = table_all.at[seq_peer(a, b)]
        wires.make(table_second + i, place, place, (d, seq_peer(a, b))).wait_recv()
    r.table[...] = table_all[...]
    for reduce in (*qkv_reduces, out_reduce):
        reduce.shares.hand_on()
    for reduce in (*gate_up_reduces, down_reduce, *qkv_reduces, out_reduce):
        reduce.shares.wait()
    wires.finish()


def write_outputs(sizes, inputs, outputs):
    n = sizes
    result, input_grad, grad_ada, table, gate_up0, gate_up1, down, proj, qkv0, qkv1, qkv2 = inputs[:-3]
    pair_embed, pair_gain, pair_weight = inputs[-3:]
    o_result, o_input, o_qkv, o_out, o_gate_up, o_down, o_ada, o_embed, o_gain, o_pair = outputs
    o_result[...] = result[...]
    o_input[...] = input_grad[...]
    o_ada[...] = grad_ada[...]
    everyone = range(n.seq)
    for kind in range(3):
        for side in range(2):
            low = (3 * side + kind) * DH
            o_qkv[side * n.half : (side + 1) * n.half, kind * n.width : (kind + 1) * n.width] = jnp.concatenate(
                [head[q, :, low : low + DH] for q in everyone for head in (qkv0, qkv1, qkv2)], axis=1
            ).astype(F32)
    group = n.seq * n.strip
    for number in range(2 * n.dp):
        side, block = divmod(number % n.dp, n.dp // 2)
        low = (number // n.dp) * (n.hidden // 2) + block * n.strip
        gate_up = (gate_up0, gate_up1)[side]
        o_gate_up[:, number * group : (number + 1) * group] = jnp.concatenate(
            [gate_up[q, :, low : low + n.strip] for q in everyone], axis=1
        ).astype(F32)
    for q in everyone:
        o_down[q * n.strip : (q + 1) * n.strip, :] = down[q].astype(F32)
        side, core = divmod(q, 2)
        lanes = slice(side * (n.width // 2), (side + 1) * (n.width // 2))
        o_out[core * n.half : (core + 1) * n.half, lanes] = proj[q].astype(F32)

    lines = jnp.concatenate([table[q, h] for q in everyone for h in range(n.heads)], axis=0)
    lane = lax.broadcasted_iota(jnp.int32, lines.shape, 1)
    table_t = jnp.where(lane < 2 * RR, pltpu.roll(lines, RR, 1), 0.0)
    for number, at in ((0, 40), (2 * RR, 41), (CLASSES - 1, 42)):
        table_t = jnp.where(lane == number, jnp.broadcast_to(lines[:, at : at + 1], lines.shape), table_t)
    embed = pair_embed[...].astype(F32)
    embed = jnp.concatenate([embed, jnp.zeros((LANES - CLASSES, embed.shape[1]), F32)], axis=0)
    gain = pair_gain[...].astype(F32)
    normal, inverted = layer_norm(embed, 1e-05)

    def exact(a, b):
        return jnp.dot(a, b, precision=HIGHEST, preferred_element_type=F32)

    o_pair[...] = exact(table_t, normal * gain)
    scaled_grad = exact(table_t.T, pair_weight[...].astype(F32))
    o_gain[...] = jnp.sum(scaled_grad * normal, axis=0)
    o_embed[...] = norm_back(scaled_grad * gain, normal, inverted)[0:CLASSES]


def fused_layer(
    sizes, valid_len, chain_break, hidden, out_grad, condition, qkv, out, gate_up, down, ada, embed, gain, weight
):
    n = sizes
    rows, width, length, heads, part, hid = n.rows, n.width, n.length, n.heads, n.part, n.hidden
    any_space, vmem, smem = pl.ANY, pltpu.VMEM, pltpu.SMEM
    inputs = dict(
        valid_len=(valid_len, smem),
        chain_break=(chain_break, smem),
        hidden=(hidden, any_space),
        out_grad=(out_grad, any_space),
        condition=(condition, vmem),
        qkv=(qkv, any_space),
        out=(out, any_space),
        gate_up=(gate_up, any_space),
        down=(down, any_space),
        ada=(ada, vmem),
        pair_embed=(embed, vmem),
        pair_gain=(gain, vmem),
        pair_weight=(weight, vmem),
    )
    modulations = 6 * width

    def reduced(height, columns):
        return (
            ((2, n.far, height, columns), BF16),
            ((n.far, height, columns), BF16),
            ((n.far - 1, height, columns), BF16),
            ((height, columns), BF16),
            ((height, columns), BF16),
        )

    def shares(height, columns):
        return (n.seq, height, columns), BF16, any_space

    sums = ((2, rows, width), BF16), ((2, rows, width), BF16), ((rows, width), BF16), ((rows, width), BF16)
    gate_up_sizes, down_sizes = (n.shard, hid), (n.strip, width)
    proj_sizes, qkv_sizes = (n.half, width // 2), (n.half, 6 * DH)
    outputs = dict(
        result=((rows, width), BF16, vmem),
        input_grad=((rows, width), BF16, vmem),
        grad_ada=((n.ada_rows, modulations), F32, vmem),
        table=((n.seq, heads, 1, LANES), F32, vmem),
        gate_up0_share=shares(*gate_up_sizes),
        gate_up1_share=shares(*gate_up_sizes),
        down_share=shares(*down_sizes),
        proj_share=shares(*proj_sizes),
        qkv0_share=shares(*qkv_sizes),
        qkv1_share=shares(*qkv_sizes),
        qkv2_share=shares(*qkv_sizes),
    )
    scratch = dict(
        w_qkv=((width, 3 * part), BF16),
        w_out=((n.dp, 2, n.half, width), BF16),
        w_gate_up=((width, 2 * hid), BF16),
        w_down=((hid, width), BF16),
        hidden_all=((length, width), BF16),
        grads_all=((length, width), BF16),
        hidden_own=((rows, width), BF16),
        upstream=((rows, width), BF16),
        cond_all=((n.dp, 8, n.conditioning), F32),
        squashed=((n.conditioning, n.dp), F32),
        mod_send=((n.dp, 1, modulations), F32),
        mod_recv=((n.dp, 1, modulations), F32),
        modulation=((1, modulations), F32),
        mod_sums=((n.seq, 1, modulations), F32),
        mod_totals=((n.dp, 1, modulations), F32),
        bias=((heads, (2 * n.blocks - 1) * LANES, LANES), F32),
        crossed=((heads, 1, LANES), F32),
        table_t=((H, LANES), F32),
        table_sums=((n.dp, heads, 1, LANES), F32),
        table_all=((n.seq, heads, 1, LANES), F32),
        keys=((heads, length, DH), BF16),
        keys_t=((heads, n.seq, DH, rows), BF16),
        values_t=((heads, n.seq, DH, rows), BF16),
        queries_t=((heads, n.seq, DH, rows), BF16),
        exps=((heads, n.seq, length, rows), BF16),
        outs_t=((heads, n.seq, DH, rows), F32),
        inverse=((heads, n.seq, 1, rows), F32),
        mixed_send=((n.seq, rows, part), BF16),
        mixed_recv=((n.seq, rows, part), BF16),
        back_recv=((n.seq, rows, part), BF16),
        branch=((rows, width), F32),
        middle=((rows, width), F32),
        feed_own=((rows, width), F32),
        second_own=((rows, width), F32),
        branch_grad=((rows, width), BF16),
        second_all=((length, width), BF16),
        second_t=((width, length), BF16),
        norm_t=((width, length), BF16),
        mod_t=((width, 8), F32),
        first_sums=((width, LANES), F32),
        inner=((length, hid), BF16),
        inner_t=((hid, length), BF16),
        gate_up_grads=((length, 2 * hid), BF16),
        out_near=((n.dp * n.half, width), BF16),
        out_far=((n.dp * n.half, width // 2), BF16),
        raw=((length, hid // 2), F32),
        dots_t=((heads, n.seq, DH, rows), BF16),
        delta=((heads, n.seq, 1, rows), F32),
        pair_grads=((length, 2 * DH), F32),
        query_grads=((length, DH), BF16),
        feed_sib=sums[0],
        feed_got=sums[1],
        feed_over=sums[2],
        feed_come=sums[3],
        second_sib=sums[0],
        second_got=sums[1],
        second_over=sums[2],
        second_come=sums[3],
        gate_up0_grad=reduced(*gate_up_sizes)[0],
        gate_up0_got=reduced(*gate_up_sizes)[1],
        gate_up0_come=reduced(*gate_up_sizes)[2],
        gate_up0_far=reduced(*gate_up_sizes)[3],
        gate_up0_mine=reduced(*gate_up_sizes)[4],
        gate_up1_grad=reduced(*gate_up_sizes)[0],
        gate_up1_got=reduced(*gate_up_sizes)[1],
        gate_up1_come=reduced(*gate_up_sizes)[2],
        gate_up1_far=reduced(*gate_up_sizes)[3],
        gate_up1_mine=reduced(*gate_up_sizes)[4],
        proj_grad=reduced(*proj_sizes)[0],
        proj_got=reduced(*proj_sizes)[1],
        proj_come=reduced(*proj_sizes)[2],
        proj_far=reduced(*proj_sizes)[3],
        proj_mine=reduced(*proj_sizes)[4],
        qkv0_grad=reduced(*qkv_sizes)[0],
        qkv0_got=reduced(*qkv_sizes)[1],
        qkv0_come=reduced(*qkv_sizes)[2],
        qkv0_far=reduced(*qkv_sizes)[3],
        qkv0_mine=reduced(*qkv_sizes)[4],
        qkv1_grad=reduced(*qkv_sizes)[0],
        qkv1_got=reduced(*qkv_sizes)[1],
        qkv1_come=reduced(*qkv_sizes)[2],
        qkv1_far=reduced(*qkv_sizes)[3],
        qkv1_mine=reduced(*qkv_sizes)[4],
        qkv2_grad=reduced(*qkv_sizes)[0],
        qkv2_got=reduced(*qkv_sizes)[1],
        qkv2_come=reduced(*qkv_sizes)[2],
        qkv2_far=reduced(*qkv_sizes)[3],
        qkv2_mine=reduced(*qkv_sizes)[4],
        down_grad=reduced(*down_sizes)[0],
        down_come=((n.far - 1, 2, *down_sizes), BF16),
        down_far=((2, *down_sizes), BF16),
        down_got=(down_sizes, BF16),
        down_mine=(down_sizes, BF16),
    )
    semaphores = dict(send_sem=210, recv_sem=210, local_sem=21)
    names = [*inputs, *outputs, *scratch, *semaphores]
    made = pl.pallas_call(
        functools.partial(layer_kernel, n, names),
        out_shape=[jax.ShapeDtypeStruct(shape, kind) for shape, kind, _ in outputs.values()],
        in_specs=[pl.BlockSpec(memory_space=space) for _, space in inputs.values()],
        out_specs=[pl.BlockSpec(memory_space=space) for _, _, space in outputs.values()],
        scratch_shapes=[pltpu.VMEM(shape, kind) for shape, kind in scratch.values()]
        + [pltpu.SemaphoreType.DMA((count,)) for count in semaphores.values()],
        compiler_params=pltpu.CompilerParams(
            collective_id=0, has_side_effects=True, vmem_limit_bytes=VMEM_LIMIT
        ),
    )(*[array for array, _ in inputs.values()])
    gradients = (
        ((rows, width), BF16),
        ((rows, width), BF16),
        ((n.shard, 3 * width), F32),
        ((n.shard, width), F32),
        ((n.shard, 2 * n.seq * hid), F32),
        ((n.seq * n.strip, width), F32),
        ((n.ada_rows, modulations), F32),
        (embed.shape, F32),
        (gain.shape, F32),
        (weight.shape, F32),
    )
    count = len(made) + 3

    def write(*refs):
        write_outputs(n, refs[:count], refs[count:])

    return pl.pallas_call(
        write,
        out_shape=[jax.ShapeDtypeStruct(shape, kind) for shape, kind in gradients],
        in_specs=[pl.BlockSpec(memory_space=vmem)] * count,
        out_specs=[pl.BlockSpec(memory_space=vmem)] * len(gradients),
        compiler_params=pltpu.CompilerParams(vmem_limit_bytes=VMEM_LIMIT),
    )(*made, embed, gain, weight)


def fused_body(
    hidden_in,
    condition,
    qkv_weight,
    out_weight,
    gate_up_weight,
    down_weight,
    ada_weight,
    pair_embed,
    pair_gain,
    pair_weight,
    valid_len,
    chain_break,
    out_grad,
):
    _, rows, width = hidden_in.shape
    seq = lax.axis_size("seq")
    dp = lax.axis_size("dp")
    shard = qkv_weight.shape[0]
    sizes = Sizes(
        rows, width, seq, dp, shard, down_weight.shape[0], ada_weight.shape[0], condition.shape[1]
    )
    outs = fused_layer(
        sizes,
        valid_len,
        chain_break,
        hidden_in[0],
        out_grad[0],
        condition,
        qkv_weight,
        out_weight,
        gate_up_weight,
        down_weight,
        ada_weight,
        pair_embed,
        pair_gain,
        pair_weight.T,
    )
    result, input_grad, *grads, grad_gain, grad_pair = outs
    return (result[None], input_grad[None], *grads, grad_gain, grad_pair.T)


def body(*arguments):
    hidden_in, _, qkv_weight, _, _, down_weight = arguments[:6]
    seq, dp = lax.axis_size("seq"), lax.axis_size("dp")
    whole_tiles = qkv_weight.shape[0] % 32 == 0 and down_weight.shape[0] % (16 * seq) == 0
    if whole_tiles and hidden_in.shape[0] == 1 and seq == 4 and dp == 8:
        return fused_body(*arguments)
    return plain_body(*arguments)


def solution(mesh):
    rows = P("dp", "seq", None)
    share = P("dp", None)
    return jax.shard_map(
        body,
        mesh=mesh,
        in_specs=(rows, share, share, share, share, share, share, P(), P(), P(), P("dp"), P("dp"), rows),
        out_specs=(rows, rows, share, share, share, share, share, P(), P(), P()),
        check_vma=False,
    )
```

```python
import functools
import types

import jax
import jax.numpy as jnp
from jax import lax
from jax.experimental import pallas as pl
from jax.experimental.pallas import tpu as pltpu
from jax.sharding import PartitionSpec as P

H = 12
DH = 64
RR = 32
CLASSES = 66

HIGHEST = lax.Precision.HIGHEST
F32 = jnp.float32
BF16 = jnp.bfloat16


VMEM_LIMIT = 65400 * 2**10


def layer_norm(values, epsilon=1e-06):
    average = jnp.mean(values, axis=-1, keepdims=True)
    centered = values - average
    inv_std = lax.rsqrt(jnp.mean(centered * centered, axis=-1, keepdims=True) + epsilon)
    return (centered * inv_std, inv_std)


def norm_back(upstream, normal, inv_std):
    return inv_std * (
        upstream
        - jnp.mean(upstream, axis=-1, keepdims=True)
        - normal * jnp.mean(upstream * normal, axis=-1, keepdims=True)
    )


def pair_table(pair_embed, pair_gain, pair_weight):
    average = jnp.mean(pair_embed, axis=-1, keepdims=True)
    centered = pair_embed - average
    normal = centered * lax.rsqrt(jnp.mean(centered * centered, axis=-1, keepdims=True) + 1e-05)
    return jnp.dot(normal * pair_gain, pair_weight, precision=HIGHEST)


def mm(spec, a, b):
    return jnp.einsum(spec, a, b, preferred_element_type=F32)


def plain_body(
    hidden_in,
    condition,
    qkv_weight,
    out_weight,
    gate_up_weight,
    down_weight,
    ada_weight,
    pair_embed,
    pair_gain,
    pair_weight,
    valid_len,
    chain_break,
    out_grad,
):
    items, rows, width = hidden_in.shape
    seq = lax.axis_size("seq")
    dp = lax.axis_size("dp")
    me = lax.axis_index("seq")
    at = lax.axis_index("dp")
    length = rows * seq
    heads = H // seq
    part = heads * DH
    shard = qkv_weight.shape[0]
    strip = down_weight.shape[0] // seq
    hidden_units = dp * strip

    def pick(array, axis):
        return lax.dynamic_index_in_dim(array, me, axis, keepdims=False)

    def gather(array, name, axis):
        return lax.all_gather(array, name, axis=axis, tiled=True)

    def scatter(array, name, axis):
        return lax.psum_scatter(array, name, scatter_dimension=axis, tiled=True)

    conditions = gather(condition, "dp", 0)
    squashed = jax.nn.silu(conditions.astype(F32)).astype(BF16)
    ada_rows = ada_weight.shape[0]
    squashed_part = lax.dynamic_slice_in_dim(squashed, at * ada_rows, ada_rows, 1)
    modulation = scatter(mm("ic,ce->ie", squashed_part, ada_weight), "dp", 0)
    shift_one, scale_one, gate_one, shift_two, scale_two, gate_two = jnp.split(
        modulation[:, None, :], 6, axis=-1
    )
    qkv_w = gather(pick(qkv_weight.reshape(shard, 3, seq, part), 2).reshape(shard, 3 * part), "dp", 0)
    gate_up_w = gather(
        pick(gate_up_weight.reshape(shard, 2, dp, seq, strip), 3).reshape(shard, 2 * hidden_units), "dp", 0
    )
    down_w = gather(pick(down_weight.reshape(seq, strip, width), 0), "dp", 0)
    out_w = gather(gather(pick(out_weight.reshape(shard, seq, width // seq), 1), "dp", 0), "seq", 1)

    table, pair_pull = jax.vjp(
        pair_table, pair_embed.astype(F32), pair_gain.astype(F32), pair_weight.astype(F32)
    )
    my_table = lax.dynamic_slice_in_dim(table, me * heads, heads, 1)
    spread = jnp.arange(2 * length)
    distance = jnp.where(spread < length, -spread, 2 * length - spread)
    line = jnp.take(my_table, jnp.clip(distance, -RR, RR) + RR, axis=0).T
    toeplitz = jnp.tile(line, (1, length))[:, : length * (2 * length - 1)]
    toeplitz = toeplitz.reshape(heads, length, 2 * length - 1)[:, :, :length]
    positions = jnp.arange(length, dtype=jnp.int32)
    side = positions[None] >= chain_break[:, None]
    same = side[:, :, None] == side[:, None, :]
    alive = (positions[None] < valid_len[:, None])[:, None, None, :]

    hidden = gather(hidden_in, "seq", 1).astype(F32)
    upstream = out_grad.astype(F32)
    first_norm, first_inv = layer_norm(hidden)
    first = (first_norm * (1.0 + scale_one) + shift_one).astype(BF16)
    merged = mm("ird,de->ire", first, qkv_w).astype(BF16)
    queries, keys, values = (
        part_of.reshape(items, length, heads, DH) for part_of in jnp.split(merged, 3, axis=-1)
    )
    logits = mm("iqhd,ikhd->ihqk", queries, keys) * 0.125
    logits = logits + jnp.where(same[:, None], toeplitz[None], my_table[CLASSES - 1][None, :, None, None])
    logits = jnp.where(alive, logits, -1e30)
    powers = jnp.exp(logits - jnp.max(logits, axis=-1, keepdims=True))
    probs = powers / jnp.sum(powers, axis=-1, keepdims=True)
    probs_low = probs.astype(BF16)
    mixed_heads = mm("ihqk,ikhd->iqhd", probs_low, values)
    mixed_part = mixed_heads.reshape(items, length, part).astype(BF16)
    mixed_all = gather(mixed_part, "seq", 2)

    def mine(array):
        return lax.dynamic_slice_in_dim(array, me * rows, rows, 1)

    branch = mm("ire,ed->ird", mine(mixed_all), out_w)
    middle = hidden_in.astype(F32) + gate_one * branch
    second_norm, second_inv = layer_norm(middle)
    second = gather((second_norm * (1.0 + scale_two) + shift_two).astype(BF16), "seq", 1)
    gate_up = mm("ird,de->ire", second, gate_up_w)
    gate_part, up_part = jnp.split(gate_up, 2, axis=-1)
    sigmoid_gate = jax.nn.sigmoid(gate_part)
    inner = (gate_part * sigmoid_gate * up_part).astype(BF16)
    feed = scatter(mm("irf,fd->ird", inner, down_w).astype(BF16), "seq", 1).astype(F32)
    result = (middle + gate_two * feed).astype(BF16)

    feed_grad = (gate_two * gather(out_grad, "seq", 1).astype(F32)).astype(BF16)
    d_gate_two = jnp.sum(upstream * feed, axis=1)
    grad_down = mm("irf,ird->fd", inner, feed_grad)
    inner_grad = mm("ird,fd->irf", feed_grad, down_w)
    gate_grad = inner_grad * up_part * sigmoid_gate * (1.0 + gate_part * (1.0 - sigmoid_gate))
    up_grad = inner_grad * gate_part * sigmoid_gate
    gate_up_grad = jnp.concatenate([gate_grad, up_grad], axis=-1).astype(BF16)
    grad_gate_up = mm("ird,ire->de", second, gate_up_grad)
    second_grad = scatter(mm("ire,de->ird", gate_up_grad, gate_up_w).astype(BF16), "seq", 1).astype(F32)
    d_shift_two = jnp.sum(second_grad, axis=1)
    d_scale_two = jnp.sum(second_grad * second_norm, axis=1)
    middle_grad = upstream + norm_back(second_grad * (1.0 + scale_two), second_norm, second_inv)
    branch_grad = (gate_one * middle_grad).astype(BF16)
    d_gate_one = jnp.sum(middle_grad * branch, axis=1)
    branch_grad_all = gather(branch_grad, "seq", 1)
    my_columns = lax.dynamic_slice_in_dim(branch_grad_all, me * part, part, 2)
    grad_out = mm("ire,ird->ed", mixed_all, my_columns)
    out_w_rows = lax.dynamic_slice_in_dim(out_w, me * part, part, 0)
    mixed_grad = mm("ird,ed->ire", branch_grad_all, out_w_rows).astype(BF16).reshape(items, length, heads, DH)

    prob_grad = mm("iqhd,ikhd->ihqk", mixed_grad, values)
    delta = jnp.sum(probs * prob_grad, axis=-1, keepdims=True)
    score_grad = (probs * (prob_grad - delta)).astype(BF16)
    query_grad = mm("ihqk,ikhd->iqhd", score_grad, keys) * 0.125
    key_grad = mm("ihqk,iqhd->ikhd", score_grad, queries) * 0.125
    value_grad = mm("ihqk,iqhd->ikhd", probs_low, mixed_grad)
    merged_grad = jnp.concatenate(
        [term.reshape(items, length, part) for term in (query_grad, key_grad, value_grad)], axis=-1
    ).astype(BF16)
    wide = score_grad.astype(F32)
    kept = jnp.sum(jnp.where(same[:, None], wide, 0.0), axis=0)
    crossed = jnp.sum(jnp.where(same[:, None], 0.0, wide), axis=(0, 2, 3))
    skewed = jnp.pad(kept[:, :, ::-1], ((0, 0), (0, 0), (0, length))).reshape(heads, -1)
    skewed = skewed[:, : length * (2 * length - 1)].reshape(heads, length, 2 * length - 1)
    lines = jnp.sum(skewed, axis=1)
    middle_line = length - 1
    low_end = jnp.sum(lines[:, : middle_line - RR + 1], axis=1)
    high_end = jnp.sum(lines[:, middle_line + RR :], axis=1)
    near = lines[:, middle_line - RR + 1 : middle_line + RR]
    my_table_grad = jnp.concatenate([low_end[:, None], near, high_end[:, None], crossed[:, None]], axis=1).T
    table_grad = lax.psum(
        lax.dynamic_update_slice_in_dim(jnp.zeros((CLASSES, H), F32), my_table_grad, me * heads, 1), ("dp", "seq")
    )
    grad_embed, grad_gain, grad_pair = pair_pull(table_grad)

    grad_qkv = mm("ird,ire->de", first, merged_grad)
    first_grad = scatter(mm("ire,de->ird", merged_grad, qkv_w).astype(BF16), "seq", 1).astype(F32)
    my_norm, my_inv = mine(first_norm), mine(first_inv)
    d_shift_one = jnp.sum(first_grad, axis=1)
    d_scale_one = jnp.sum(first_grad * my_norm, axis=1)
    input_grad = middle_grad + norm_back(first_grad * (1.0 + scale_one), my_norm, my_inv)
    modulation_grad = jnp.concatenate(
        [d_shift_one, d_scale_one, d_gate_one, d_shift_two, d_scale_two, d_gate_two], axis=-1
    )
    modulation_grads = gather(lax.psum(modulation_grad, "seq"), "dp", 0)
    grad_ada = jnp.einsum("ic,ie->ce", squashed_part.astype(F32), modulation_grads, precision=HIGHEST)

    def owned(grad):
        return scatter(grad.astype(BF16), "dp", 0)

    def everyone(grad):
        return lax.all_gather(grad, "seq", axis=0)

    shares_qkv = everyone(owned(grad_qkv)).reshape(seq, shard, 3, part)
    shares_out = everyone(owned(grad_out))
    shares_gate_up = everyone(owned(grad_gate_up)).reshape(seq, shard, 2, dp, strip)
    shares_down = everyone(owned(grad_down))
    return (
        result,
        input_grad.astype(BF16),
        jnp.transpose(shares_qkv, (1, 2, 0, 3)).reshape(shard, -1).astype(F32),
        jnp.transpose(shares_out, (1, 0, 2)).reshape(shard, -1).astype(F32),
        jnp.transpose(shares_gate_up, (1, 2, 3, 0, 4)).reshape(shard, -1).astype(F32),
        shares_down.reshape(seq * strip, width).astype(F32),
        grad_ada,
        grad_embed,
        grad_gain,
        grad_pair,
    )


MESH = pl.DeviceIdType.MESH
LANES = 128


def nn(a, b):
    return jnp.dot(a, b, preferred_element_type=F32)


def nt(a, b):
    return lax.dot_general(a, b, (((1,), (1,)), ((), ())), preferred_element_type=F32)


def tn(a, b):
    return lax.dot_general(a, b, (((0,), (0,)), ((), ())), preferred_element_type=F32)


def skew(tile, back):
    row = lax.broadcasted_iota(jnp.int32, tile.shape, 0)
    for bit in range(7):
        turn = LANES - (1 << bit) if back else 1 << bit
        tile = jnp.where(((row >> bit) & 1) == 1, pltpu.roll(tile, turn, 1), tile)
    return tile


class Sizes:
    def __init__(self, rows, width, seq, dp, shard, down_shard, ada_rows, conditioning):
        self.rows, self.width, self.seq, self.dp = rows, width, seq, dp
        self.shard, self.ada_rows, self.conditioning = shard, ada_rows, conditioning
        self.strip = down_shard // seq
        self.length = rows * seq
        self.heads = H // seq
        self.part = self.heads * DH
        self.hidden = self.strip * dp
        self.far = dp // 2
        self.half = shard // 2
        self.blocks = self.length // LANES


def under(where, work):
    if where is None:
        work()
    else:
        pl.when(where)(work)


class Wires:
    def __init__(self, send, recv):
        self.send, self.recv, self.count, self.started = send, recv, 0, []

    def reserve(self, count=1):
        first = self.count
        self.count += count
        return first

    def make(self, number, source, target, device):
        return pltpu.make_async_remote_copy(
            src_ref=source,
            dst_ref=target,
            send_sem=self.send.at[number],
            recv_sem=self.recv.at[number],
            device_id=device,
            device_id_type=MESH,
        )

    def go(self, number, source, target, device, where=None):
        copy = self.make(number, source, target, device)
        under(where, copy.start)
        self.started.append((copy, where))
        return copy

    def settle(self, copy):
        copy.wait_send()
        self.started = [other for other in self.started if other[0] is not copy]

    def finish(self):
        for copy, where in self.started:
            under(where, copy.wait_send)
        self.started = []


def layer_kernel(sizes, names, *refs):
    r = types.SimpleNamespace(**dict(zip(names, refs, strict=True)))
    n = sizes
    rows, width, part, heads, length, hid = n.rows, n.width, n.part, n.heads, n.length, n.hidden
    half_rows = rows // 2
    d, s = lax.axis_index("dp"), lax.axis_index("seq")
    z, x = d // 2, lax.rem(d, 2)
    y, c = s // 2, lax.rem(s, 2)
    ox, oy, oc = 1 - x, 1 - y, 1 - c
    at_x = (z * 2 + ox, s)
    at_y = (d, oy * 2 + c)
    at_c = (d, y * 2 + oc)

    def z_plus(k):
        return lax.rem(z + k, n.far)

    def at_z(k):
        return (z_plus(k) * 2 + x, s)

    wires = Wires(r.send_sem, r.recv_sem)
    dp_peers = [(k, e) for k in range(n.far) for e in range(2) if k or e]
    seq_peers = [(1, 0), (0, 1), (1, 1)]

    def dp_peer(k, e):
        xx = lax.rem(x + e, 2)
        return z_plus(k) * 2 + xx, lax.rem(z + n.far - k, n.far) * 2 + xx

    def seq_peer(a, b):
        return lax.rem(y + a, 2) * 2 + lax.rem(c + b, 2)

    local_count = [0]

    def local(source, target):
        copy = pltpu.make_async_copy(source, target, r.local_sem.at[local_count[0]])
        local_count[0] += 1
        copy.start()
        return copy

    qkv_stage, gate_up_stage = r.second_t, r.gate_up_grads
    staged = [
        local(r.qkv.at[:, q * width : (q + 1) * width], qkv_stage.at[q * n.shard : (q + 1) * n.shard, 0:width])
        for q in range(3)
    ]
    staged_gate_up = [
        local(r.gate_up.at[:, q * 2 * hid : (q + 1) * 2 * hid], gate_up_stage.at[q * n.shard : (q + 1) * n.shard])
        for q in range(n.seq)
    ]
    own_shard = pl.ds(pl.multiple_of(d * n.shard, n.shard), n.shard)
    r.cond_all[d] = jnp.broadcast_to(r.condition[...].astype(F32), (8, n.conditioning))
    barrier = pltpu.get_barrier_semaphore()
    for k, e in dp_peers:
        pl.semaphore_signal(barrier, inc=1, device_id=(dp_peer(k, e)[0], s), device_id_type=MESH)
    for a, b in seq_peers:
        pl.semaphore_signal(barrier, inc=1, device_id=(d, seq_peer(a, b)), device_id_type=MESH)
    for copy in staged:
        copy.wait()
    for side in range(n.seq):

        @pl.when(s == side)
        def _():
            r.w_qkv[own_shard, :] = jnp.concatenate(
                [
                    qkv_stage[q * n.shard : (q + 1) * n.shard, side * part + h * DH : side * part + (h + 1) * DH]
                    for h in range(heads)
                    for q in range(3)
                ],
                axis=1,
            )

    pl.semaphore_wait(barrier, len(dp_peers) + len(seq_peers))

    class SeqGather:
        def __init__(self, block):
            self.block, self.first = block, wires.reserve(3)
            self.mine, self.from_y, self.from_c, self.from_yc = s, at_y[1], at_c[1], oy * 2 + oc

        def start(self, source=None):
            mine = self.block(self.mine)
            source = mine if source is None else source
            self.sent = [wires.go(self.first, source, mine, at_y), wires.go(self.first + 1, source, mine, at_c)]

        def hand_on(self):
            place = self.block(self.from_y)
            wires.make(self.first, place, place, at_y).wait_recv()
            self.sent.append(wires.go(self.first + 2, place, place, at_c))

        def settle(self):
            for copy in self.sent:
                wires.settle(copy)

        def wait_core(self):
            place = self.block(self.from_c)
            wires.make(self.first + 1, place, place, at_c).wait_recv()

        def wait_last(self):
            place = self.block(self.from_yc)
            wires.make(self.first + 2, place, place, at_c).wait_recv()

        def wait(self):
            self.hand_on()
            self.wait_core()
            self.wait_last()

    last_z = n.far - 1

    class Wave:
        def __init__(self, block, direct=False):
            self.block, self.first, self.direct = block, wires.reserve(4), direct

        def send(self, source=None):
            mine = self.block(z)
            source = mine if source is None else source
            wires.go(self.first + 1, source, mine, at_z(1), None if self.direct else z != last_z)
            wires.go(self.first + 3, source, mine, at_z(3), None if self.direct else z != 0)
            wires.go(self.first + 2, source, mine, at_z(2))

        def relay(self):
            place = self.block(z_plus(2))
            wires.make(self.first + 2, place, place, at_z(2)).wait_recv()
            if not self.direct:
                wires.go(self.first, place, place, at_z(1), z == last_z - 1)
                wires.go(self.first, place, place, at_z(3), z == 1)

        def arrive(self, k):
            place = self.block(z_plus(n.far - k))
            far_end = z == (0 if k == 1 else last_z)
            near = wires.make(self.first + k, place, place, at_z(k))
            if self.direct:
                near.wait_recv()
                return
            far = wires.make(self.first, place, place, at_z(k))
            under(far_end, far.wait_recv)
            under(jnp.logical_not(far_end), near.wait_recv)

    class DpGather:
        def __init__(self, source, place, direct=False):
            self.source, self.place, self.first = source, place, wires.reserve(n.far)
            self.wave = Wave(lambda zz: place(zz * 2 + x), direct)

        def start(self):
            mine = self.place(d)
            self.own = None if self.source is None else local(self.source, mine)
            wires.go(self.first, mine if self.source is None else self.source, mine, at_x)

        def along_z(self):
            self.wave.send(self.source)

        def across(self, k):
            place = self.place(z_plus(n.far - k) * 2 + x)
            wires.go(self.first + k, place, place, at_x)

        def relay(self):
            self.wave.relay()
            self.across(2)

        def hand_on(self):
            for k in (1, 3):
                self.wave.arrive(k)
                self.across(k)

        def wait(self):
            if self.own is not None:
                self.own.wait()
            for k in range(n.far):
                place = self.place(z_plus(n.far - k) * 2 + ox)
                wires.make(self.first + k, place, place, at_x).wait_recv()

    class DpGatherX:
        def __init__(self, source, place):
            self.source, self.place, self.first = source, place, wires.reserve()
            self.waves = Wave(lambda zz: place(zz * 2 + x)), Wave(lambda zz: place(zz * 2 + ox))

        def start(self):
            self.own = local(self.source, self.place(d))
            wires.go(self.first, self.source, self.place(d), at_x)

        def along_z(self):
            self.waves[0].send(self.source)

        def cross(self):
            place = self.place(z * 2 + ox)
            wires.make(self.first, place, place, at_x).wait_recv()
            self.waves[1].send()

        def relay(self, which):
            self.waves[which].relay()

        def wait(self):
            self.own.wait()
            for wave in self.waves:
                wave.arrive(1)
                wave.arrive(3)

    class SeqReduce:
        def __init__(self, sib, got, over, come):
            self.sib, self.got, self.over, self.come = sib, got, over, come
            self.first, self.sent = wires.reserve(3), []

        def put_core(self, index):
            def put(lanes, block):
                self.sib[index, :, lanes] = block.astype(BF16)

            return put

        def to_core(self, index):
            self.sent.append(wires.go(self.first + index, self.sib.at[index], self.got.at[index], at_c))

        def wait_far(self):
            wires.make(self.first + 1, self.sib.at[1], self.got.at[1], at_c).wait_recv()

        def put_y(self):
            def put(lanes, block):
                self.over[:, lanes] = (block + self.got[1, :, lanes].astype(F32)).astype(BF16)

            return put

        def to_y(self):
            self.sent.append(wires.go(self.first + 2, self.over, self.come, at_y))

        def settle(self):
            for copy in self.sent:
                wires.settle(copy)

        def wait(self):
            wires.make(self.first, self.sib.at[0], self.got.at[0], at_c).wait_recv()
            wires.make(self.first + 2, self.over, self.come, at_y).wait_recv()

        def total(self, own, place):
            return own[place, :] + self.got[0, place, :].astype(F32) + self.come[place, :].astype(F32)

    at_end = z * (last_z - z) == 0
    inside = z * (last_z - z) != 0

    def mirror(k):
        return (z, z + 1 - 2 * lax.rem(z, 2), lax.rem(z + 2, n.far), last_z - z)[k]

    def at_mirror(k):
        return (mirror(k) * 2 + x, s)

    def add_up(target, parts):
        def one(q, _):
            place = pl.ds(pl.multiple_of(q * 16, 16), 16)
            total = parts[0][..., place, :].astype(F32)
            for other in parts[1:]:
                total = total + other[..., place, :].astype(F32)
            target[..., place, :] = total.astype(BF16)
            return 0

        lax.fori_loop(0, target.shape[-2] // 16, one, 0)

    class Shares:
        def __init__(self, mine, share):
            self.mine, self.share = mine, share
            self.gather = SeqGather(lambda t: share.at[t])

        def start(self):
            self.own = local(self.mine, self.share.at[s])
            self.gather.start(self.mine)

        def hand_on(self):
            self.gather.hand_on()

        def wait(self):
            self.gather.wait_core()
            self.gather.wait_last()
            self.own.wait()

    class DpReduce:
        def __init__(self, grad, got, come, far, mine, share):
            self.grad, self.got, self.come, self.far, self.mine = grad, got, come, far, mine
            self.first, self.second, self.shares = wires.reserve(n.far), wires.reserve(n.far), Shares(mine, share)

        def start(self):
            for k in (3, 1, 2, 0):
                to = mirror(k)
                wires.go(self.first + k, self.grad.at[ox, to], self.got.at[to], at_x)

        def along_z(self, k):
            to = mirror(k)
            block = self.grad.at[x, to]
            wires.make(self.first + k, self.grad.at[ox, to], self.got.at[to], at_x).wait_recv()
            add_up(block, (block, self.got.at[to]))
            if k == 3:
                wires.go(self.second, block, self.far, at_mirror(1), at_end)
                wires.go(self.second + 3, block, self.come.at[0], at_mirror(3), inside)
            elif k == 1:
                wires.go(self.second + 1, block, self.come.at[2], at_mirror(1))
            elif k == 2:

                @pl.when(inside)
                def _():
                    wires.make(self.second, block, self.far, at_mirror(1)).wait_recv()
                    add_up(block, (block, self.far))

                wires.go(self.second + 2, block, self.come.at[1], at_mirror(2))

        def finish(self):
            for k in (2, 1):
                wires.make(self.second + k, self.mine, self.come.at[3 - k], at_mirror(k)).wait_recv()
            near = self.grad.at[x, z], self.come.at[1], self.come.at[2]

            @pl.when(at_end)
            def _():
                add_up(self.mine, near)

            @pl.when(inside)
            def _():
                wires.make(self.second + 3, self.mine, self.come.at[0], at_mirror(3)).wait_recv()
                add_up(self.mine, (*near, self.come.at[0]))

            self.shares.start()

    class DpReduceZ:
        def __init__(self, grad, come, far, got, mine, share):
            self.grad, self.come, self.far, self.got, self.mine = grad, come, far, got, mine
            self.first, self.cross, self.shares = wires.reserve(4), wires.reserve(), Shares(mine, share)

        def start(self, which):
            ways = (
                (0, self.far, 1, at_end),
                (3, self.come.at[0], 3, inside),
                (1, self.come.at[2], 1, None),
                (2, self.come.at[1], 2, at_end),
            )
            for k, place, to, where in ways[2 * which : 2 * which + 2]:
                block = self.grad.at[:, mirror(k or 3)]
                wires.go(self.first + k, block, place, at_mirror(to), where)

        def merge(self):
            block = self.grad.at[:, mirror(2)]

            @pl.when(inside)
            def _():
                wires.make(self.first, block, self.far, at_mirror(1)).wait_recv()
                add_up(block, (block, self.far))

            wires.go(self.first + 2, block, self.come.at[1], at_mirror(2), inside)

        def across(self):
            block = self.grad.at[:, z]
            for k in (2, 1):
                wires.make(self.first + k, self.far, self.come.at[3 - k], at_mirror(k)).wait_recv()
            near = block, self.come.at[1], self.come.at[2]

            @pl.when(at_end)
            def _():
                add_up(block, near)

            @pl.when(inside)
            def _():
                wires.make(self.first + 3, self.far, self.come.at[0], at_mirror(3)).wait_recv()
                add_up(block, (*near, self.come.at[0]))

            wires.go(self.cross, self.grad.at[ox, z], self.got, at_x)

        def finish(self):
            wires.make(self.cross, self.mine, self.got, at_x).wait_recv()
            add_up(self.mine, (self.grad.at[x, z], self.got))
            self.shares.start()

    step = 64

    def by_rows(count, work, start=0, unroll=2):
        def one(q, carry):
            return work(pl.ds(pl.multiple_of(q * step, step), step), carry)

        return lax.fori_loop(0, count // step, one, start, unroll=unroll)

    wide = 2 * LANES

    def by_lanes(count, work, unroll=True):
        def one(q, _):
            work(pl.ds(pl.multiple_of(q * wide, wide), wide))
            return 0

        lax.fori_loop(0, count // wide, one, 0, unroll=unroll)

    def fold_rows(array):
        return jnp.sum(array.reshape(step // 8, 8, width), axis=0)

    hidden_all, grads_all = r.hidden_all, r.grads_all

    def rows_of(ref):
        return lambda t: ref.at[pl.ds(pl.multiple_of(t * rows, rows), rows)]

    hidden_gather, up_gather = SeqGather(rows_of(hidden_all)), SeqGather(rows_of(grads_all))
    def shard_rows(ref, height, lanes=slice(None)):
        return lambda t: ref.at[pl.ds(pl.multiple_of(t * height, height), height), lanes]

    def lane_half(side):
        return pl.ds(pl.multiple_of(side * (width // 2), width // 2), width // 2)

    lanes_y = lane_half(y)
    qkv_gathers = [
        DpGather(None, shard_rows(r.w_qkv, n.shard, lanes), True)
        for lanes in (slice(0, 2 * LANES), slice(2 * LANES, 3 * part))
    ]
    out_gather = DpGather(
        r.out.at[pl.ds(pl.multiple_of(c * n.half, n.half), n.half), lanes_y],
        lambda t: r.w_out.at[t, c, :, lanes_y],
    )
    half_strip = n.strip // 2

    def down_half(kind, side):
        low = side * half_strip
        return kind(
            r.down.at[pl.ds(pl.multiple_of(s * n.strip + low, half_strip), half_strip)],
            lambda t: r.w_down.at[pl.ds(pl.multiple_of(t * n.strip + low, half_strip), half_strip)],
        )

    down_near, down_gather = down_half(DpGather, 0), down_half(DpGatherX, 1)
    pieces = [
        DpGather(None, shard_rows(r.w_gate_up, n.shard, slice(q * (hid // 2), (q + 1) * (hid // 2))))
        for q in (0, 2, 1, 3)
    ]

    def out_block(t):
        ty, tc = t // 2, lax.rem(t, 2)
        return r.w_out.at[:, tc, :, lane_half(ty)]

    out_share = SeqGather(out_block)

    cond_first, mod_first = wires.reserve(len(dp_peers)), wires.reserve(len(dp_peers))
    cond_all, mod_send, mod_recv = r.cond_all, r.mod_send, r.mod_recv
    for i, (k, e) in enumerate(dp_peers):
        wires.go(cond_first + i, cond_all.at[d], cond_all.at[d], (dp_peer(k, e)[0], s))
    for piece in qkv_gathers:
        piece.along_z()
        piece.start()
    own_hidden = local(r.hidden, hidden_gather.block(s))
    keep_hidden = local(r.hidden, r.hidden_own)
    keep_grads = local(r.out_grad, r.upstream)
    hidden_gather.start(r.hidden)
    own_grads = local(r.out_grad, up_gather.block(s))


    for i, (k, e) in enumerate(dp_peers):
        place = cond_all.at[dp_peer(k, e)[1]]
        wires.make(cond_first + i, place, place, (dp_peer(k, e)[0], s)).wait_recv()
    item_of = lax.broadcasted_iota(jnp.int32, (n.dp, n.conditioning), 0)
    conditions = jnp.where(item_of == 0, cond_all[0], 0.0)
    for i in range(1, n.dp):
        conditions = jnp.where(item_of == i, cond_all[i], conditions)
    squashed = (conditions * (1.0 / (1.0 + jnp.exp(-conditions)))).astype(BF16).astype(F32)
    r.squashed[...] = squashed.T
    squashed_rows = r.squashed[pl.ds(pl.multiple_of(d * n.ada_rows, n.ada_rows), n.ada_rows), :]
    ada_part = tn(squashed_rows.astype(BF16), r.ada[...])
    for i in range(n.dp):
        mod_send[i] = ada_part[i : i + 1]
    mod_recv[d] = mod_send[d]
    for i, (k, e) in enumerate(dp_peers):
        wires.go(mod_first + i, mod_send.at[dp_peer(k, e)[0]], mod_recv.at[d], (dp_peer(k, e)[0], s))
    for copy in staged_gate_up:
        copy.wait()
    group = n.seq * n.strip
    for side in range(n.seq):

        @pl.when(s == side)
        def _():
            strips = []
            for number in range(2 * n.dp):
                block, low = divmod(number * group, 2 * hid)
                low += side * n.strip
                strips.append(gate_up_stage[block * n.shard : (block + 1) * n.shard, low : low + n.strip])
            r.w_gate_up[own_shard, :] = jnp.concatenate(strips, axis=1)

    for piece in (out_gather, *pieces[:2]):
        piece.start()
        piece.along_z()
    down_gather.start()
    down_gather.along_z()
    down_near.start()
    down_near.along_z()
    for piece in pieces[2:]:
        piece.start()
    hidden_gather.hand_on()
    up_gather.start(r.out_grad)
    for piece in qkv_gathers:
        piece.relay()
        piece.hand_on()

    bias, table_t = r.bias, r.table_t
    embed = r.pair_embed[...].astype(F32)
    normal, _ = layer_norm(embed, 1e-05)
    scaled = normal * r.pair_gain[...].astype(F32)
    scaled = jnp.concatenate([scaled, jnp.zeros((LANES - CLASSES, scaled.shape[1]), F32)], axis=0)
    table_t[...] = lax.dot_general(
        r.pair_weight[...].astype(F32),
        scaled,
        (((1,), (1,)), ((), ())),
        precision=HIGHEST,
        preferred_element_type=F32,
    )

    def table_line(h):
        return table_t[pl.ds(s * heads + h, 1), :]

    key_in = lax.broadcasted_iota(jnp.int32, (LANES, LANES), 0)
    query_in = lax.broadcasted_iota(jnp.int32, (LANES, LANES), 1)
    middle_tile = n.blocks - 1

    def build_bias(h, _):
        line = table_line(h)
        near = skew(jnp.broadcast_to(pltpu.roll(line, LANES - RR, 1), (LANES, LANES)), False)
        low_end = jnp.broadcast_to(line[:, 0:1], (LANES, LANES))
        high_end = jnp.broadcast_to(line[:, 2 * RR : 2 * RR + 1], (LANES, LANES))
        for tile in range(2 * n.blocks - 1):
            away = tile - middle_tile
            apart = query_in - key_in - away * LANES
            if away < -1:
                value = high_end
            elif away > 1:
                value = low_end
            else:
                value = jnp.where(apart >= RR, high_end, jnp.where(apart <= -RR, low_end, near))
            bias[h, tile * LANES : (tile + 1) * LANES] = value
        return 0

    lax.fori_loop(0, heads, build_bias, 0)

    own_hidden.wait()
    hidden_gather.wait_core()
    hidden_gather.wait_last()
    for i, (k, e) in enumerate(dp_peers):
        place = mod_recv.at[dp_peer(k, e)[1]]
        wires.make(mod_first + i, mod_send.at[d], place, (dp_peer(k, e)[0], s)).wait_recv()
    modulation = mod_recv[0]
    for i in range(1, n.dp):
        modulation = modulation + mod_recv[i]
    r.modulation[...] = modulation

    def vector(index):
        return r.modulation[:, index * width : (index + 1) * width]

    shift_one, scale_one, gate_one, shift_two, scale_two, gate_two = range(6)
    first = hidden_all
    hidden_gather.settle()

    def make_first(t, _):
        place = pl.ds(pl.multiple_of(t * LANES, LANES), LANES)
        normal, _ = layer_norm(hidden_all[place, :].astype(F32))
        first[place, :] = (normal * (1.0 + vector(scale_one)) + vector(shift_one)).astype(BF16)
        r.norm_t[:, place] = normal.astype(BF16).T
        return 0

    lax.fori_loop(0, n.blocks, make_first, 0)
    few_rows = jnp.concatenate([vector(q) for q in range(6)] + [vector(0)] * 2, axis=0)
    r.mod_t[...] = few_rows.T
    out_gather.relay()
    out_gather.hand_on()
    pieces[0].relay()

    for piece in qkv_gathers:
        piece.wait()
    w_qkv = r.w_qkv
    keys = r.keys
    keys_t, values_t, queries_t = r.keys_t, r.values_t, r.queries_t
    w_qkv_t = r.inner_t

    def turn_weight(q, _):
        place = pl.ds(pl.multiple_of(q * 2 * LANES, 2 * LANES), 2 * LANES)
        w_qkv_t[0 : 3 * part, place] = w_qkv[place, :].T
        return 0

    lax.fori_loop(0, width // (2 * LANES), turn_weight, 0)

    def project(t, _):
        place = pl.ds(pl.multiple_of(t * rows, rows), rows)
        block = first[place, :]
        for low in range(0, 3 * part, wide):
            merged = nn(block, w_qkv[:, low : min(low + wide, 3 * part)]).astype(BF16)
            for q in range(merged.shape[1] // DH):
                h, kind = divmod(low // DH + q, 3)
                if kind == 1:
                    keys[h, place, :] = merged[:, q * DH : (q + 1) * DH]
        for h in range(heads):
            merged_t = nt(w_qkv_t[h * 3 * DH : (h + 1) * 3 * DH, 0:width], block).astype(BF16)
            queries_t[h, t] = (merged_t[:DH].astype(F32) * 0.125).astype(BF16)
            keys_t[h, t] = merged_t[DH : 2 * DH]
            values_t[h, t] = merged_t[2 * DH :]
        return 0

    lax.fori_loop(0, n.seq, project, 0)
    pieces[0].hand_on()
    down_gather.cross()
    for piece in pieces[2:]:
        piece.along_z()
    pieces[1].relay()

    valid, broken = r.valid_len[0], r.chain_break[0]
    exps, outs_t, inverse = r.exps, r.outs_t, r.inverse
    tiles = rows // LANES
    order = [oy * 2 + c, oy * 2 + oc, y * 2 + oc, s]

    raw = r.raw

    def tile_parts(t, tile):
        number = t * tiles + tile
        query_side = number * LANES + lax.broadcasted_iota(jnp.int32, (1, LANES), 1) >= broken
        for q in range(n.blocks):
            key_pos = q * LANES + lax.broadcasted_iota(jnp.int32, (LANES, LANES), 0)
            strip = pl.ds(pl.multiple_of((n.blocks - 1 + q - number) * LANES, LANES), LANES)
            yield slice(q * LANES, (q + 1) * LANES), strip, key_pos, (key_pos >= broken) == query_side

    def eights(array):
        return array.reshape(LANES // 8, 8, LANES)

    def attend(t):
        def one_head(h, _):
            for q in range(n.seq):
                place = slice(q * rows, (q + 1) * rows)
                raw[place, 0:rows] = nn(keys[h, place, :], queries_t[h, t])
            for tile in range(tiles):
                lanes = slice(tile * LANES, (tile + 1) * LANES)
                far_side = jnp.broadcast_to(table_line(h)[:, CLASSES - 1 : CLASSES], (1, LANES))
                top = jnp.full((8, LANES), -1e30, F32)
                for place, strip, key_pos, same in tile_parts(t, tile):
                    logits = raw[place, lanes] + jnp.where(same, bias[h, strip, :], far_side)
                    logits = jnp.where(key_pos < valid, logits, -1e30)
                    raw[place, lanes] = logits
                    top = jnp.maximum(top, jnp.max(eights(logits), axis=0))
                top = jnp.max(top, axis=0, keepdims=True)
                total = jnp.zeros((8, LANES), F32)
                for q in range(n.blocks):
                    place = slice(q * LANES, (q + 1) * LANES)
                    powers = jnp.exp(raw[place, lanes] - top)
                    total = total + jnp.sum(eights(powers), axis=0)
                    exps[h, t, place, lanes] = powers.astype(BF16)
                inverse[h, t, :, lanes] = 1.0 / jnp.sum(total, axis=0, keepdims=True)
            values_wide = jnp.concatenate([values_t[h, q] for q in range(n.seq)], axis=1)
            outs_t[h, t] = nn(values_wide, exps[h, t]) * inverse[h, t]
            return 0

        lax.fori_loop(0, heads, one_head, 0)

    mixed_first = wires.reserve(3)
    mixed_send, mixed_recv = r.mixed_send, r.mixed_recv
    mixed_sent = []
    to_send = [at_y, (d, oy * 2 + oc), at_c]
    out_gather.wait()
    out_share.start()

    def mixed_block(t):
        return jnp.concatenate([outs_t[h, t] for h in range(heads)], axis=0).T.astype(BF16)

    def send_mixed(i):
        mixed_sent.append(wires.go(mixed_first + i, mixed_send.at[i], mixed_recv.at[s], to_send[i]))

    def far_blocks(i, _):
        t = oy * 2 + lax.rem(c + i, 2)
        attend(t)
        mixed_send[i] = mixed_block(t)
        return 0

    lax.fori_loop(0, 2, far_blocks, 0)
    send_mixed(0)
    send_mixed(1)
    up_gather.hand_on()
    pieces[1].hand_on()
    down_gather.relay(0)
    out_share.hand_on()
    attend(order[2])
    mixed_send[2] = mixed_block(order[2])
    send_mixed(2)
    down_near.relay()
    attend(s)
    mixed_recv[s] = mixed_block(s)
    down_near.hand_on()

    out_share.wait_core()
    out_share.wait_last()

    def w_out(q, lanes=slice(None)):
        shards = part // n.shard
        block = r.w_out[q * shards : (q + 1) * shards, :, :, lanes]
        return block.reshape(part, block.shape[-1])

    for i in range(3):
        place = mixed_recv.at[order[i]]
        wires.make(mixed_first + i, mixed_send.at[i], place, to_send[i]).wait_recv()
    keep_hidden.wait()

    def make_branch(lanes):
        branch = nn(mixed_recv[0], w_out(0, lanes))
        for q in range(1, n.seq):
            branch = branch + nn(mixed_recv[q], w_out(q, lanes))
        r.branch[:, lanes] = branch

    by_lanes(width, make_branch)
    second_all = r.second_all
    second_gather = SeqGather(rows_of(second_all))

    def make_second(place, _):
        middle = r.hidden_own[place, :].astype(F32) + vector(gate_one) * r.branch[place, :]
        r.middle[place, :] = middle
        normal, _ = layer_norm(middle)
        r.branch_grad[place, :] = (normal * (1.0 + vector(scale_two)) + vector(shift_two)).astype(BF16)
        return 0

    by_rows(rows, make_second)
    second_all[pl.ds(pl.multiple_of(s * rows, rows), rows), :] = r.branch_grad[...]
    second_gather.start()

    own_grads.wait()
    up_gather.wait_core()
    up_gather.wait_last()
    up_gather.settle()
    feed_grads = grads_all

    def make_feed_grads(place, _):
        feed_grads[place, :] = (vector(gate_two) * grads_all[place, :].astype(F32)).astype(BF16)
        return 0

    by_rows(length, make_feed_grads)
    down_gather.relay(1)
    for piece in (pieces[0], pieces[1], down_near, down_gather):
        piece.wait()
    w_gate_up, w_down = r.w_gate_up, r.w_down
    inner, inner_t, gate_up_grads, second_t = r.inner, r.inner_t, r.gate_up_grads, r.second_t
    feed_places = (r.feed_sib, r.feed_got, r.feed_over, r.feed_come)
    feed_reduce = SeqReduce(*feed_places)
    second_reduce = SeqReduce(r.second_sib, r.second_got, r.second_over, r.second_come)
    half_hid = hid // 2

    def rows_at(t):
        return pl.ds(pl.multiple_of(t * rows, rows), rows)

    def units(t, side):
        place, low = rows_at(t), side * half_hid
        block, given = second_all[place, :], feed_grads[place, :]
        gates, ups, inner_grads = (raw.at[i * rows : (i + 1) * rows] for i in range(3))
        gates[...] = nn(block, w_gate_up[:, low : low + half_hid])
        ups[...] = nn(block, w_gate_up[:, hid + low : hid + low + half_hid])
        inner_grads[...] = nt(given, w_down[low : low + half_hid, :])
        for first_row in range(0, rows, step):
            few = slice(first_row, first_row + step)
            gate, up, inner_grad = gates[few, :], ups[few, :], inner_grads[few, :]
            sigmoid = 1.0 / (1.0 + jnp.exp(-gate))
            silu = gate * sigmoid
            to = pl.ds(pl.multiple_of(t * rows + first_row, step), step)
            inner[to, low : low + half_hid] = (silu * up).astype(BF16)
            gate_up_grads[to, low : low + half_hid] = (
                inner_grad * up * sigmoid * (1.0 + gate * (1.0 - sigmoid))
            ).astype(BF16)
            gate_up_grads[to, hid + low : hid + low + half_hid] = (inner_grad * silu).astype(BF16)

    def second_part(t, put):
        by_lanes(width, lambda lanes: put(lanes, nt(gate_up_grads[rows_at(t), :], w_gate_up[lanes, :])))

    def feed_part(t, put):
        by_lanes(width, lambda lanes: put(lanes, nn(inner[rows_at(t), :], w_down[:, lanes])), False)

    def put_in(ref):
        def put(lanes, block):
            ref[:, lanes] = block.astype(ref.dtype)

        return put

    def units_of(side):
        def one(i, _):
            units(side * 2 + lax.rem(c + i, 2), 0)
            return 0

        lax.fori_loop(0, 2, one, 0)

    second_gather.wait_core()
    units_of(y)
    second_gather.hand_on()
    pieces[2].relay()
    second_gather.wait_last()
    pieces[2].hand_on()
    pieces[3].relay()
    units_of(oy)
    pieces[3].hand_on()

    gate_up_reduces = (
        DpReduce(r.gate_up0_grad, r.gate_up0_got, r.gate_up0_come, r.gate_up0_far, r.gate_up0_mine, r.gate_up0_share),
        DpReduce(r.gate_up1_grad, r.gate_up1_got, r.gate_up1_come, r.gate_up1_far, r.gate_up1_mine, r.gate_up1_share),
    )
    down_reduce = DpReduceZ(r.down_grad, r.down_come, r.down_far, r.down_got, r.down_mine, r.down_share)
    out_reduce = DpReduce(r.proj_grad, r.proj_got, r.proj_come, r.proj_far, r.proj_mine, r.proj_share)
    qkv_reduces = (
        DpReduce(r.qkv0_grad, r.qkv0_got, r.qkv0_come, r.qkv0_far, r.qkv0_mine, r.qkv0_share),
        DpReduce(r.qkv1_grad, r.qkv1_got, r.qkv1_come, r.qkv1_far, r.qkv1_mine, r.qkv1_share),
        DpReduce(r.qkv2_grad, r.qkv2_got, r.qkv2_come, r.qkv2_far, r.qkv2_mine, r.qkv2_share),
    )

    def turn_rows(source, target):
        def turn(t, _):
            target[:, rows_at(t)] = source[rows_at(t), :].T
            return 0

        lax.fori_loop(0, n.seq, turn, 0)

    def weight_grad(left_t, right, reduce, lows):
        height, few = reduce.grad.shape[2], n.dp // 2
        columns = reduce.grad.shape[3] // len(lows)
        for at, low in enumerate(lows):
            for first_of in range(0, n.dp, few):
                grad = nn(
                    left_t[first_of * height : (first_of + few) * height, :], right[:, low : low + columns]
                ).astype(BF16)
                for i in range(few):
                    to = first_of + i
                    reduce.grad[to % 2, to // 2, :, at * columns : (at + 1) * columns] = grad[
                        i * height : (i + 1) * height
                    ]

    turn_rows(second_all, second_t)
    weight_grad(second_t, gate_up_grads, gate_up_reduces[0], (0, hid))
    gate_up_reduces[0].start()
    pieces[2].wait()
    pieces[3].wait()
    far, over, near = oy * 2 + oc, oy * 2 + c, y * 2 + oc
    units(far, 1)
    second_part(far, second_reduce.put_core(1))
    second_reduce.to_core(1)
    units(over, 1)
    second_reduce.wait_far()
    second_part(over, second_reduce.put_y())
    second_reduce.to_y()
    units(near, 1)
    second_part(near, second_reduce.put_core(0))
    second_reduce.to_core(0)
    units(s, 1)
    second_part(s, put_in(r.second_own))

    weight_grad(second_t, gate_up_grads, gate_up_reduces[1], (half_hid, hid + half_hid))
    gate_up_reduces[1].start()
    gate_up_reduces[0].along_z(3)
    turn_rows(inner, inner_t)
    weight_grad(inner_t, feed_grads, down_reduce, (0, half_hid))
    down_reduce.start(0)
    gate_up_reduces[0].along_z(1)
    down_reduce.start(1)
    feed_part(far, feed_reduce.put_core(1))
    feed_reduce.to_core(1)
    feed_part(near, feed_reduce.put_core(0))
    feed_reduce.to_core(0)
    feed_reduce.wait_far()
    feed_part(over, feed_reduce.put_y())
    feed_part(s, put_in(r.feed_own))
    lax.fori_loop(0, width // (2 * LANES), turn_weight, 0)
    values = keys

    def turn_values(t, _):
        for h in range(heads):
            values[h, rows_at(t), :] = values_t[h, t].T
        return 0

    lax.fori_loop(0, n.seq, turn_values, 0)

    sums = r.mod_sums

    upstream = r.upstream
    keep_grads.wait()
    second_reduce.wait()
    kept_middle_grad, branch_grad = r.second_own, r.branch_grad
    empty = jnp.zeros((8, width), F32)

    def put_sum(index, array):
        sums[s, :, index * width : (index + 1) * width] = jnp.sum(array, axis=0, keepdims=True)

    def second_back(place, carry):
        second_grad = second_reduce.total(r.second_own, place)
        normal, inverted = layer_norm(r.middle[place, :])
        middle_grad = upstream[place, :].astype(F32) + norm_back(
            second_grad * (1.0 + vector(scale_two)), normal, inverted
        )
        kept_middle_grad[place, :] = middle_grad
        branch_grad[place, :] = (vector(gate_one) * middle_grad).astype(BF16)
        terms = (second_grad, second_grad * normal, middle_grad * r.branch[place, :])
        return tuple(total + fold_rows(term) for total, term in zip(carry, terms))

    for index, total in zip(
        (shift_two, scale_two, gate_one), by_rows(rows, second_back, (empty, empty, empty))
    ):
        put_sum(index, total)
    back_first = wires.reserve(3)
    for copy in mixed_sent:
        wires.settle(copy)
    back_all, back_recv = mixed_send, r.back_recv
    for q in range(n.seq):
        back_all[q] = nt(branch_grad[...], w_out(q)).astype(BF16)
    for i in range(3):
        wires.go(back_first + i, back_all.at[order[i]], back_recv.at[s], to_send[i])
    back_recv[s] = back_all[s]
    feed_reduce.to_y()

    out_first = wires.reserve(2)
    second_gather.settle()
    out_parts, quarter = second_all, n.dp * n.half

    def make_out_grad(lanes):
        for q in range(n.seq):
            grad = tn(mixed_recv[q], branch_grad[:, lanes]).astype(BF16)
            for i in range(part // n.half):
                number = q * (part // n.half) + i
                low = (number % 2) * quarter + (number // 2) * n.half
                out_parts[low : low + n.half, lanes] = grad[i * n.half : (i + 1) * n.half]

    by_lanes(width, make_out_grad)

    def out_rows(core):
        return out_parts.at[pl.ds(pl.multiple_of(core * quarter, quarter), quarter)]

    lanes_oy = pl.ds(pl.multiple_of(oy * (width // 2), width // 2), width // 2)

    def out_cores():
        wires.make(out_first, out_rows(oc), r.out_near, at_c).wait_recv()
        mine = out_parts[pl.ds(pl.multiple_of(c * quarter, quarter), quarter), :]
        r.out_near[...] = (r.out_near[...].astype(F32) + mine.astype(F32)).astype(BF16)
        wires.go(out_first + 1, r.out_near.at[:, lanes_oy], r.out_far, at_y)

    def out_sum():
        wires.make(out_first + 1, r.out_near.at[:, lanes_oy], r.out_far, at_y).wait_recv()
        total = (r.out_near[:, lanes_y].astype(F32) + r.out_far[...].astype(F32)).astype(BF16)
        for to in range(n.dp):
            r.proj_grad[to % 2, to // 2] = total[to * n.half : (to + 1) * n.half]
        out_reduce.start()

    dots_t, delta = r.dots_t, r.delta
    pair_grads, query_grads = r.pair_grads, r.query_grads
    bias[...] = jnp.zeros_like(bias)
    crossed, score_grad = r.crossed, inner.at[:, 0:rows]
    crossed[...] = jnp.zeros_like(crossed)
    pair_grads[...] = jnp.zeros_like(pair_grads)
    merged_grads = gate_up_grads

    def take_back(t):
        given_t = back_recv[t].T.astype(F32)
        for h in range(heads):
            scaled = (given_t[h * DH : (h + 1) * DH] * inverse[h, t]).astype(BF16)
            dots_t[h, t] = scaled
            delta[h, t] = jnp.sum(scaled.astype(F32) * outs_t[h, t], axis=0, keepdims=True)

    def attend_back(h, t, first_of):
        place = rows_at(t)
        for q in range(n.seq):
            some = slice(q * rows, (q + 1) * rows)
            raw[some, 0:rows] = nn(values[h, some, :], dots_t[h, t])
        for tile in range(tiles):
            lanes = slice(tile * LANES, (tile + 1) * LANES)
            across = jnp.zeros((8, LANES), F32)
            for keys_of, strip, _, same in tile_parts(t, tile):
                grad = exps[h, t, keys_of, lanes].astype(F32) * (raw[keys_of, lanes] - delta[h, t, :, lanes])
                kept = jnp.where(same, grad, 0.0)
                bias[h, strip, :] = bias[h, strip, :] + kept
                across = across + jnp.sum(eights(grad - kept), axis=0)
                score_grad[keys_of, lanes] = grad.astype(BF16)
            crossed[h] = crossed[h] + jnp.sum(across, axis=0, keepdims=True)
        keys_wide = jnp.concatenate([keys_t[h, q] for q in range(n.seq)], axis=1)
        query_grads[place, :] = (nn(keys_wide, score_grad[...]) * 0.125).T.astype(BF16)
        queries, dots = queries_t[h, t].T, dots_t[h, t].T
        for q in range(n.seq):
            some = slice(q * rows, (q + 1) * rows)
            grad = jnp.concatenate([nn(score_grad[some, :], queries), nn(exps[h, t, some, :], dots)], axis=1)
            pair_grads[some, :] = grad if first_of else pair_grads[some, :] + grad

    def end_head(h):
        for q in range(n.seq):
            some = slice(q * rows, (q + 1) * rows)
            merged_grads[some, h * wide : h * wide + 3 * DH] = jnp.concatenate(
                [query_grads[some, :], pair_grads[some, :].astype(BF16)], axis=1
            )
        merged = merged_grads.at[:, h * wide : h * wide + 3 * DH]
        totals = nn(jnp.ones((16, length), BF16), merged[...])[0:1]
        few = n.dp // 2 * n.shard
        for first_of in range(0, width, few):
            place = slice(first_of, first_of + few)
            scale, shift = 1.0 + r.mod_t[place, 1:2], r.mod_t[place, 0:1]
            weights = w_qkv[place, h * 3 * DH : (h + 1) * 3 * DH].astype(F32)
            product = nn(r.norm_t[place, :], merged[...])
            d_shift = jnp.sum(weights * totals, axis=1, keepdims=True)
            d_scale = jnp.sum(weights * product, axis=1, keepdims=True)
            lane = lax.broadcasted_iota(jnp.int32, (few, LANES), 1)
            both = jnp.where(lane == 0, d_shift, jnp.where(lane == 1, d_scale, 0.0))
            r.first_sums[place, :] = both if h == 0 else r.first_sums[place, :] + both
            grad = (product * scale + totals * shift).astype(BF16)
            for i in range(n.dp // 2):
                to = first_of // n.shard + i
                low = i * n.shard
                qkv_reduces[h].grad[to % 2, to // 2] = jnp.concatenate(
                    [grad[low : low + n.half], grad[low + n.half : low + n.shard]], axis=1
                )
        qkv_reduces[h].start()

    def back_block(i):
        wires.make(back_first + i, back_recv.at[order[i]], back_recv.at[order[i]], to_send[i]).wait_recv()
        take_back(order[i])

    def some_of_head(h, side):
        def one(i, _):
            attend_back(h, side * 2 + lax.rem(c + i, 2), False)
            return 0

        lax.fori_loop(0, 2, one, 0)

    def rest_of_head(h):
        pair_grads[...] = jnp.zeros_like(pair_grads)

        def one(i, _):
            attend_back(h, lax.rem(y + i // 2, 2) * 2 + lax.rem(c + lax.rem(i, 2), 2), False)
            return 0

        lax.fori_loop(0, n.seq, one, 0)

    wires.go(out_first, out_rows(oc), r.out_near, at_c)
    gate_up_reduces[0].along_z(2)
    gate_up_reduces[0].along_z(0)
    gate_up_reduces[1].along_z(3)
    take_back(s)
    back_block(2)
    some_of_head(0, y)
    gate_up_reduces[1].along_z(1)
    out_cores()
    back_block(0)
    back_block(1)
    some_of_head(0, oy)
    end_head(0)
    rest_of_head(1)
    end_head(1)
    down_reduce.merge()
    rest_of_head(2)
    end_head(2)

    second_reduce.settle()
    first_reduce = SeqReduce(r.second_sib, r.second_got, r.second_over, r.second_come)

    def first_part(t, put):
        def by_heads(lanes):
            total = nn(merged_grads[rows_at(t), 0 : 3 * DH], w_qkv_t[0 : 3 * DH, lanes])
            for h in range(1, heads):
                total = total + nn(
                    merged_grads[rows_at(t), h * wide : h * wide + 3 * DH],
                    w_qkv_t[h * 3 * DH : (h + 1) * 3 * DH, lanes],
                )
            put(lanes, total)

        by_lanes(width, by_heads)

    first_part(oy * 2 + oc, first_reduce.put_core(1))
    first_reduce.to_core(1)
    first_reduce.wait_far()
    first_part(oy * 2 + c, first_reduce.put_y())
    first_reduce.to_y()
    first_part(y * 2 + oc, first_reduce.put_core(0))
    first_reduce.to_core(0)
    first_part(s, put_in(r.branch))
    gate_up_reduces[1].along_z(2)
    gate_up_reduces[1].along_z(0)
    for k in (3, 1, 2, 0):
        qkv_reduces[0].along_z(k)
    qkv_reduces[1].along_z(3)
    feed_reduce.wait()

    def make_result(place, total):
        feed = feed_reduce.total(r.feed_own, place)
        r.result[place, :] = (r.middle[place, :] + vector(gate_two) * feed).astype(BF16)
        return total + fold_rows(upstream[place, :].astype(F32) * feed)

    put_sum(gate_two, by_rows(rows, make_result, empty))
    turned = r.first_sums[...].T
    put_sum(shift_one, turned[0:1])
    put_sum(scale_one, turned[1:2])
    sums_first = wires.reserve(3)
    for i, (a, b) in enumerate(seq_peers):
        wires.go(sums_first + i, sums.at[s], sums.at[s], (d, seq_peer(a, b)))
    qkv_reduces[1].along_z(1)
    down_reduce.across()
    qkv_reduces[2].along_z(3)
    qkv_reduces[1].along_z(2)
    qkv_reduces[1].along_z(0)
    out_sum()
    qkv_reduces[2].along_z(1)

    table_sums, table_all = r.table_sums, r.table_all

    def fold(h, _):
        lane = lax.broadcasted_iota(jnp.int32, (1, LANES), 1)
        near = jnp.zeros((LANES, LANES), F32)
        low_end = jnp.zeros((LANES, LANES), F32)
        high_end = jnp.zeros((LANES, LANES), F32)
        for tile in range(2 * n.blocks - 1):
            away = tile - middle_tile
            apart = query_in - key_in - away * LANES
            value = bias[h, tile * LANES : (tile + 1) * LANES]
            if away < -1:
                high_end = high_end + value
            elif away > 1:
                low_end = low_end + value
            else:
                high_end = high_end + jnp.where(apart >= RR, value, 0.0)
                low_end = low_end + jnp.where(apart <= -RR, value, 0.0)
                near = near + jnp.where((apart < RR) & (apart > -RR), value, 0.0)
        line = jnp.sum(skew(near, True), axis=0, keepdims=True)
        for where, array in ((40, low_end), (41, high_end), (42, crossed[h])):
            line = jnp.where(lane == where, jnp.sum(array), line)
        table_sums[d, h] = line
        return 0

    lax.fori_loop(0, heads, fold, 0)
    table_first = wires.reserve(len(dp_peers))
    for i, (k, e) in enumerate(dp_peers):
        wires.go(table_first + i, table_sums.at[d], table_sums.at[d], (dp_peer(k, e)[0], s))

    for i, (a, b) in enumerate(seq_peers):
        place = sums.at[seq_peer(a, b)]
        wires.make(sums_first + i, place, place, (d, seq_peer(a, b))).wait_recv()
    mod_total = sums[0]
    for i in range(1, n.seq):
        mod_total = mod_total + sums[i]
    mod_totals = r.mod_totals
    mod_totals[d] = mod_total
    totals_first = wires.reserve(len(dp_peers))
    for i, (k, e) in enumerate(dp_peers):
        wires.go(totals_first + i, mod_totals.at[d], mod_totals.at[d], (dp_peer(k, e)[0], s))
    qkv_reduces[2].along_z(2)
    qkv_reduces[2].along_z(0)
    gate_up_reduces[0].finish()
    gate_up_reduces[1].finish()
    down_reduce.finish()
    out_reduce.along_z(3)
    first_reduce.wait()

    def first_back(place, _):
        first_grad = first_reduce.total(r.branch, place)
        normal, inverted = layer_norm(r.hidden_own[place, :].astype(F32))
        r.input_grad[place, :] = (
            kept_middle_grad[place, :] + norm_back(first_grad * (1.0 + vector(scale_one)), normal, inverted)
        ).astype(BF16)
        return 0

    by_rows(rows, first_back)
    for k in (1, 2, 0):
        out_reduce.along_z(k)
    for reduce in qkv_reduces:
        reduce.finish()
    for reduce in (*gate_up_reduces, down_reduce):
        reduce.shares.hand_on()
    for i, (k, e) in enumerate(dp_peers):
        place = table_sums.at[dp_peer(k, e)[1]]
        wires.make(table_first + i, place, place, (dp_peer(k, e)[0], s)).wait_recv()
    total = table_sums[0]
    for i in range(1, n.dp):
        total = total + table_sums[i]
    table_all[s] = total
    table_second = wires.reserve(3)
    for i, (a, b) in enumerate(seq_peers):
        wires.go(table_second + i, table_all.at[s], table_all.at[s], (d, seq_peer(a, b)))
    out_reduce.finish()
    for i, (k, e) in enumerate(dp_peers):
        place = mod_totals.at[dp_peer(k, e)[1]]
        wires.make(totals_first + i, place, place, (dp_peer(k, e)[0], s)).wait_recv()
    squashed_rows = r.squashed[pl.ds(pl.multiple_of(d * n.ada_rows, n.ada_rows), n.ada_rows), :]
    ada = squashed_rows[:, 0:1] * mod_totals[0]
    for i in range(1, n.dp):
        ada = ada + squashed_rows[:, i : i + 1] * mod_totals[i]
    r.grad_ada[...] = ada
    for i, (a, b) in enumerate(seq_peers):
        place = table_all.at[seq_peer(a, b)]
        wires.make(table_second + i, place, place, (d, seq_peer(a, b))).wait_recv()
    r.table[...] = table_all[...]
    for reduce in (*qkv_reduces, out_reduce):
        reduce.shares.hand_on()
    for reduce in (*gate_up_reduces, down_reduce, *qkv_reduces, out_reduce):
        reduce.shares.wait()
    wires.finish()


def write_outputs(sizes, inputs, outputs):
    n = sizes
    result, input_grad, grad_ada, table, gate_up0, gate_up1, down, proj, qkv0, qkv1, qkv2 = inputs[:-3]
    pair_embed, pair_gain, pair_weight = inputs[-3:]
    o_result, o_input, o_qkv, o_out, o_gate_up, o_down, o_ada, o_embed, o_gain, o_pair = outputs
    o_result[...] = result[...]
    o_input[...] = input_grad[...]
    o_ada[...] = grad_ada[...]
    everyone = range(n.seq)
    for kind in range(3):
        for side in range(2):
            low = (3 * side + kind) * DH
            o_qkv[side * n.half : (side + 1) * n.half, kind * n.width : (kind + 1) * n.width] = jnp.concatenate(
                [head[q, :, low : low + DH] for q in everyone for head in (qkv0, qkv1, qkv2)], axis=1
            ).astype(F32)
    group = n.seq * n.strip
    for number in range(2 * n.dp):
        side, block = divmod(number % n.dp, n.dp // 2)
        low = (number // n.dp) * (n.hidden // 2) + block * n.strip
        gate_up = (gate_up0, gate_up1)[side]
        o_gate_up[:, number * group : (number + 1) * group] = jnp.concatenate(
            [gate_up[q, :, low : low + n.strip] for q in everyone], axis=1
        ).astype(F32)
    for q in everyone:
        o_down[q * n.strip : (q + 1) * n.strip, :] = down[q].astype(F32)
        side, core = divmod(q, 2)
        lanes = slice(side * (n.width // 2), (side + 1) * (n.width // 2))
        o_out[core * n.half : (core + 1) * n.half, lanes] = proj[q].astype(F32)

    lines = jnp.concatenate([table[q, h] for q in everyone for h in range(n.heads)], axis=0)
    lane = lax.broadcasted_iota(jnp.int32, lines.shape, 1)
    table_t = jnp.where(lane < 2 * RR, pltpu.roll(lines, RR, 1), 0.0)
    for number, at in ((0, 40), (2 * RR, 41), (CLASSES - 1, 42)):
        table_t = jnp.where(lane == number, jnp.broadcast_to(lines[:, at : at + 1], lines.shape), table_t)
    embed = pair_embed[...].astype(F32)
    embed = jnp.concatenate([embed, jnp.zeros((LANES - CLASSES, embed.shape[1]), F32)], axis=0)
    gain = pair_gain[...].astype(F32)
    normal, inverted = layer_norm(embed, 1e-05)

    def exact(a, b):
        return jnp.dot(a, b, precision=HIGHEST, preferred_element_type=F32)

    o_pair[...] = exact(table_t, normal * gain)
    scaled_grad = exact(table_t.T, pair_weight[...].astype(F32))
    o_gain[...] = jnp.sum(scaled_grad * normal, axis=0)
    o_embed[...] = norm_back(scaled_grad * gain, normal, inverted)[0:CLASSES]


def fused_layer(
    sizes, valid_len, chain_break, hidden, out_grad, condition, qkv, out, gate_up, down, ada, embed, gain, weight
):
    n = sizes
    rows, width, length, heads, part, hid = n.rows, n.width, n.length, n.heads, n.part, n.hidden
    any_space, vmem, smem = pl.ANY, pltpu.VMEM, pltpu.SMEM
    inputs = dict(
        valid_len=(valid_len, smem),
        chain_break=(chain_break, smem),
        hidden=(hidden, any_space),
        out_grad=(out_grad, any_space),
        condition=(condition, vmem),
        qkv=(qkv, any_space),
        out=(out, any_space),
        gate_up=(gate_up, any_space),
        down=(down, any_space),
        ada=(ada, vmem),
        pair_embed=(embed, vmem),
        pair_gain=(gain, vmem),
        pair_weight=(weight, vmem),
    )
    modulations = 6 * width

    def reduced(height, columns):
        return (
            ((2, n.far, height, columns), BF16),
            ((n.far, height, columns), BF16),
            ((n.far - 1, height, columns), BF16),
            ((height, columns), BF16),
            ((height, columns), BF16),
        )

    def shares(height, columns):
        return (n.seq, height, columns), BF16, any_space

    sums = ((2, rows, width), BF16), ((2, rows, width), BF16), ((rows, width), BF16), ((rows, width), BF16)
    gate_up_sizes, down_sizes = (n.shard, hid), (n.strip, width)
    proj_sizes, qkv_sizes = (n.half, width // 2), (n.half, 6 * DH)
    outputs = dict(
        result=((rows, width), BF16, vmem),
        input_grad=((rows, width), BF16, vmem),
        grad_ada=((n.ada_rows, modulations), F32, vmem),
        table=((n.seq, heads, 1, LANES), F32, vmem),
        gate_up0_share=shares(*gate_up_sizes),
        gate_up1_share=shares(*gate_up_sizes),
        down_share=shares(*down_sizes),
        proj_share=shares(*proj_sizes),
        qkv0_share=shares(*qkv_sizes),
        qkv1_share=shares(*qkv_sizes),
        qkv2_share=shares(*qkv_sizes),
    )
    scratch = dict(
        w_qkv=((width, 3 * part), BF16),
        w_out=((n.dp, 2, n.half, width), BF16),
        w_gate_up=((width, 2 * hid), BF16),
        w_down=((hid, width), BF16),
        hidden_all=((length, width), BF16),
        grads_all=((length, width), BF16),
        hidden_own=((rows, width), BF16),
        upstream=((rows, width), BF16),
        cond_all=((n.dp, 8, n.conditioning), F32),
        squashed=((n.conditioning, n.dp), F32),
        mod_send=((n.dp, 1, modulations), F32),
        mod_recv=((n.dp, 1, modulations), F32),
        modulation=((1, modulations), F32),
        mod_sums=((n.seq, 1, modulations), F32),
        mod_totals=((n.dp, 1, modulations), F32),
        bias=((heads, (2 * n.blocks - 1) * LANES, LANES), F32),
        crossed=((heads, 1, LANES), F32),
        table_t=((H, LANES), F32),
        table_sums=((n.dp, heads, 1, LANES), F32),
        table_all=((n.seq, heads, 1, LANES), F32),
        keys=((heads, length, DH), BF16),
        keys_t=((heads, n.seq, DH, rows), BF16),
        values_t=((heads, n.seq, DH, rows), BF16),
        queries_t=((heads, n.seq, DH, rows), BF16),
        exps=((heads, n.seq, length, rows), BF16),
        outs_t=((heads, n.seq, DH, rows), F32),
        inverse=((heads, n.seq, 1, rows), F32),
        mixed_send=((n.seq, rows, part), BF16),
        mixed_recv=((n.seq, rows, part), BF16),
        back_recv=((n.seq, rows, part), BF16),
        branch=((rows, width), F32),
        middle=((rows, width), F32),
        feed_own=((rows, width), F32),
        second_own=((rows, width), F32),
        branch_grad=((rows, width), BF16),
        second_all=((length, width), BF16),
        second_t=((width, length), BF16),
        norm_t=((width, length), BF16),
        mod_t=((width, 8), F32),
        first_sums=((width, LANES), F32),
        inner=((length, hid), BF16),
        inner_t=((hid, length), BF16),
        gate_up_grads=((length, 2 * hid), BF16),
        out_near=((n.dp * n.half, width), BF16),
        out_far=((n.dp * n.half, width // 2), BF16),
        raw=((length, hid // 2), F32),
        dots_t=((heads, n.seq, DH, rows), BF16),
        delta=((heads, n.seq, 1, rows), F32),
        pair_grads=((length, 2 * DH), F32),
        query_grads=((length, DH), BF16),
        feed_sib=sums[0],
        feed_got=sums[1],
        feed_over=sums[2],
        feed_come=sums[3],
        second_sib=sums[0],
        second_got=sums[1],
        second_over=sums[2],
        second_come=sums[3],
        gate_up0_grad=reduced(*gate_up_sizes)[0],
        gate_up0_got=reduced(*gate_up_sizes)[1],
        gate_up0_come=reduced(*gate_up_sizes)[2],
        gate_up0_far=reduced(*gate_up_sizes)[3],
        gate_up0_mine=reduced(*gate_up_sizes)[4],
        gate_up1_grad=reduced(*gate_up_sizes)[0],
        gate_up1_got=reduced(*gate_up_sizes)[1],
        gate_up1_come=reduced(*gate_up_sizes)[2],
        gate_up1_far=reduced(*gate_up_sizes)[3],
        gate_up1_mine=reduced(*gate_up_sizes)[4],
        proj_grad=reduced(*proj_sizes)[0],
        proj_got=reduced(*proj_sizes)[1],
        proj_come=reduced(*proj_sizes)[2],
        proj_far=reduced(*proj_sizes)[3],
        proj_mine=reduced(*proj_sizes)[4],
        qkv0_grad=reduced(*qkv_sizes)[0],
        qkv0_got=reduced(*qkv_sizes)[1],
        qkv0_come=reduced(*qkv_sizes)[2],
        qkv0_far=reduced(*qkv_sizes)[3],
        qkv0_mine=reduced(*qkv_sizes)[4],
        qkv1_grad=reduced(*qkv_sizes)[0],
        qkv1_got=reduced(*qkv_sizes)[1],
        qkv1_come=reduced(*qkv_sizes)[2],
        qkv1_far=reduced(*qkv_sizes)[3],
        qkv1_mine=reduced(*qkv_sizes)[4],
        qkv2_grad=reduced(*qkv_sizes)[0],
        qkv2_got=reduced(*qkv_sizes)[1],
        qkv2_come=reduced(*qkv_sizes)[2],
        qkv2_far=reduced(*qkv_sizes)[3],
        qkv2_mine=reduced(*qkv_sizes)[4],
        down_grad=reduced(*down_sizes)[0],
        down_come=((n.far - 1, 2, *down_sizes), BF16),
        down_far=((2, *down_sizes), BF16),
        down_got=(down_sizes, BF16),
        down_mine=(down_sizes, BF16),
    )
    semaphores = dict(send_sem=210, recv_sem=210, local_sem=21)
    names = [*inputs, *outputs, *scratch, *semaphores]
    made = pl.pallas_call(
        functools.partial(layer_kernel, n, names),
        out_shape=[jax.ShapeDtypeStruct(shape, kind) for shape, kind, _ in outputs.values()],
        in_specs=[pl.BlockSpec(memory_space=space) for _, space in inputs.values()],
        out_specs=[pl.BlockSpec(memory_space=space) for _, _, space in outputs.values()],
        scratch_shapes=[pltpu.VMEM(shape, kind) for shape, kind in scratch.values()]
        + [pltpu.SemaphoreType.DMA((count,)) for count in semaphores.values()],
        compiler_params=pltpu.CompilerParams(
            collective_id=0, has_side_effects=True, vmem_limit_bytes=VMEM_LIMIT
        ),
    )(*[array for array, _ in inputs.values()])
    gradients = (
        ((rows, width), BF16),
        ((rows, width), BF16),
        ((n.shard, 3 * width), F32),
        ((n.shard, width), F32),
        ((n.shard, 2 * n.seq * hid), F32),
        ((n.seq * n.strip, width), F32),
        ((n.ada_rows, modulations), F32),
        (embed.shape, F32),
        (gain.shape, F32),
        (weight.shape, F32),
    )
    count = len(made) + 3

    def write(*refs):
        write_outputs(n, refs[:count], refs[count:])

    return pl.pallas_call(
        write,
        out_shape=[jax.ShapeDtypeStruct(shape, kind) for shape, kind in gradients],
        in_specs=[pl.BlockSpec(memory_space=vmem)] * count,
        out_specs=[pl.BlockSpec(memory_space=vmem)] * len(gradients),
        compiler_params=pltpu.CompilerParams(vmem_limit_bytes=VMEM_LIMIT),
    )(*made, embed, gain, weight)


def fused_body(
    hidden_in,
    condition,
    qkv_weight,
    out_weight,
    gate_up_weight,
    down_weight,
    ada_weight,
    pair_embed,
    pair_gain,
    pair_weight,
    valid_len,
    chain_break,
    out_grad,
):
    _, rows, width = hidden_in.shape
    seq = lax.axis_size("seq")
    dp = lax.axis_size("dp")
    shard = qkv_weight.shape[0]
    sizes = Sizes(
        rows, width, seq, dp, shard, down_weight.shape[0], ada_weight.shape[0], condition.shape[1]
    )
    outs = fused_layer(
        sizes,
        valid_len,
        chain_break,
        hidden_in[0],
        out_grad[0],
        condition,
        qkv_weight,
        out_weight,
        gate_up_weight,
        down_weight,
        ada_weight,
        pair_embed,
        pair_gain,
        pair_weight.T,
    )
    result, input_grad, *grads, grad_gain, grad_pair = outs
    return (result[None], input_grad[None], *grads, grad_gain, grad_pair.T)


def body(*arguments):
    hidden_in, _, qkv_weight, _, _, down_weight = arguments[:6]
    seq, dp = lax.axis_size("seq"), lax.axis_size("dp")
    whole_tiles = qkv_weight.shape[0] % 32 == 0 and down_weight.shape[0] % (16 * seq) == 0
    if whole_tiles and hidden_in.shape[0] == 1 and seq == 4 and dp == 8:
        return fused_body(*arguments)
    return plain_body(*arguments)


def solution(mesh):
    rows = P("dp", "seq", None)
    share = P("dp", None)
    return jax.shard_map(
        body,
        mesh=mesh,
        in_specs=(rows, share, share, share, share, share, share, P(), P(), P(), P("dp"), P("dp"), rows),
        out_specs=(rows, rows, share, share, share, share, share, P(), P(), P()),
        check_vma=False,
    )
```

```python
import functools
import types

import jax
import jax.numpy as jnp
from jax import lax
from jax.experimental import pallas as pl
from jax.experimental.pallas import tpu as pltpu
from jax.sharding import PartitionSpec as P

H = 12
DH = 64
RR = 32
CLASSES = 66

HIGHEST = lax.Precision.HIGHEST
F32 = jnp.float32
BF16 = jnp.bfloat16


VMEM_LIMIT = 65400 * 2**10


def layer_norm(values, epsilon=1e-06):
    average = jnp.mean(values, axis=-1, keepdims=True)
    centered = values - average
    inv_std = lax.rsqrt(jnp.mean(centered * centered, axis=-1, keepdims=True) + epsilon)
    return (centered * inv_std, inv_std)


def norm_back(upstream, normal, inv_std):
    return inv_std * (
        upstream
        - jnp.mean(upstream, axis=-1, keepdims=True)
        - normal * jnp.mean(upstream * normal, axis=-1, keepdims=True)
    )


def pair_table(pair_embed, pair_gain, pair_weight):
    average = jnp.mean(pair_embed, axis=-1, keepdims=True)
    centered = pair_embed - average
    normal = centered * lax.rsqrt(jnp.mean(centered * centered, axis=-1, keepdims=True) + 1e-05)
    return jnp.dot(normal * pair_gain, pair_weight, precision=HIGHEST)


def mm(spec, a, b):
    return jnp.einsum(spec, a, b, preferred_element_type=F32)


def plain_body(
    hidden_in,
    condition,
    qkv_weight,
    out_weight,
    gate_up_weight,
    down_weight,
    ada_weight,
    pair_embed,
    pair_gain,
    pair_weight,
    valid_len,
    chain_break,
    out_grad,
):
    items, rows, width = hidden_in.shape
    seq = lax.axis_size("seq")
    dp = lax.axis_size("dp")
    me = lax.axis_index("seq")
    at = lax.axis_index("dp")
    length = rows * seq
    heads = H // seq
    part = heads * DH
    shard = qkv_weight.shape[0]
    strip = down_weight.shape[0] // seq
    hidden_units = dp * strip

    def pick(array, axis):
        return lax.dynamic_index_in_dim(array, me, axis, keepdims=False)

    def gather(array, name, axis):
        return lax.all_gather(array, name, axis=axis, tiled=True)

    def scatter(array, name, axis):
        return lax.psum_scatter(array, name, scatter_dimension=axis, tiled=True)

    conditions = gather(condition, "dp", 0)
    squashed = jax.nn.silu(conditions.astype(F32)).astype(BF16)
    ada_rows = ada_weight.shape[0]
    squashed_part = lax.dynamic_slice_in_dim(squashed, at * ada_rows, ada_rows, 1)
    modulation = scatter(mm("ic,ce->ie", squashed_part, ada_weight), "dp", 0)
    shift_one, scale_one, gate_one, shift_two, scale_two, gate_two = jnp.split(
        modulation[:, None, :], 6, axis=-1
    )
    qkv_w = gather(pick(qkv_weight.reshape(shard, 3, seq, part), 2).reshape(shard, 3 * part), "dp", 0)
    gate_up_w = gather(
        pick(gate_up_weight.reshape(shard, 2, dp, seq, strip), 3).reshape(shard, 2 * hidden_units), "dp", 0
    )
    down_w = gather(pick(down_weight.reshape(seq, strip, width), 0), "dp", 0)
    out_w = gather(gather(pick(out_weight.reshape(shard, seq, width // seq), 1), "dp", 0), "seq", 1)

    table, pair_pull = jax.vjp(
        pair_table, pair_embed.astype(F32), pair_gain.astype(F32), pair_weight.astype(F32)
    )
    my_table = lax.dynamic_slice_in_dim(table, me * heads, heads, 1)
    spread = jnp.arange(2 * length)
    distance = jnp.where(spread < length, -spread, 2 * length - spread)
    line = jnp.take(my_table, jnp.clip(distance, -RR, RR) + RR, axis=0).T
    toeplitz = jnp.tile(line, (1, length))[:, : length * (2 * length - 1)]
    toeplitz = toeplitz.reshape(heads, length, 2 * length - 1)[:, :, :length]
    positions = jnp.arange(length, dtype=jnp.int32)
    side = positions[None] >= chain_break[:, None]
    same = side[:, :, None] == side[:, None, :]
    alive = (positions[None] < valid_len[:, None])[:, None, None, :]

    hidden = gather(hidden_in, "seq", 1).astype(F32)
    upstream = out_grad.astype(F32)
    first_norm, first_inv = layer_norm(hidden)
    first = (first_norm * (1.0 + scale_one) + shift_one).astype(BF16)
    merged = mm("ird,de->ire", first, qkv_w).astype(BF16)
    queries, keys, values = (
        part_of.reshape(items, length, heads, DH) for part_of in jnp.split(merged, 3, axis=-1)
    )
    logits = mm("iqhd,ikhd->ihqk", queries, keys) * 0.125
    logits = logits + jnp.where(same[:, None], toeplitz[None], my_table[CLASSES - 1][None, :, None, None])
    logits = jnp.where(alive, logits, -1e30)
    powers = jnp.exp(logits - jnp.max(logits, axis=-1, keepdims=True))
    probs = powers / jnp.sum(powers, axis=-1, keepdims=True)
    probs_low = probs.astype(BF16)
    mixed_heads = mm("ihqk,ikhd->iqhd", probs_low, values)
    mixed_part = mixed_heads.reshape(items, length, part).astype(BF16)
    mixed_all = gather(mixed_part, "seq", 2)

    def mine(array):
        return lax.dynamic_slice_in_dim(array, me * rows, rows, 1)

    branch = mm("ire,ed->ird", mine(mixed_all), out_w)
    middle = hidden_in.astype(F32) + gate_one * branch
    second_norm, second_inv = layer_norm(middle)
    second = gather((second_norm * (1.0 + scale_two) + shift_two).astype(BF16), "seq", 1)
    gate_up = mm("ird,de->ire", second, gate_up_w)
    gate_part, up_part = jnp.split(gate_up, 2, axis=-1)
    sigmoid_gate = jax.nn.sigmoid(gate_part)
    inner = (gate_part * sigmoid_gate * up_part).astype(BF16)
    feed = scatter(mm("irf,fd->ird", inner, down_w).astype(BF16), "seq", 1).astype(F32)
    result = (middle + gate_two * feed).astype(BF16)

    feed_grad = (gate_two * gather(out_grad, "seq", 1).astype(F32)).astype(BF16)
    d_gate_two = jnp.sum(upstream * feed, axis=1)
    grad_down = mm("irf,ird->fd", inner, feed_grad)
    inner_grad = mm("ird,fd->irf", feed_grad, down_w)
    gate_grad = inner_grad * up_part * sigmoid_gate * (1.0 + gate_part * (1.0 - sigmoid_gate))
    up_grad = inner_grad * gate_part * sigmoid_gate
    gate_up_grad = jnp.concatenate([gate_grad, up_grad], axis=-1).astype(BF16)
    grad_gate_up = mm("ird,ire->de", second, gate_up_grad)
    second_grad = scatter(mm("ire,de->ird", gate_up_grad, gate_up_w).astype(BF16), "seq", 1).astype(F32)
    d_shift_two = jnp.sum(second_grad, axis=1)
    d_scale_two = jnp.sum(second_grad * second_norm, axis=1)
    middle_grad = upstream + norm_back(second_grad * (1.0 + scale_two), second_norm, second_inv)
    branch_grad = (gate_one * middle_grad).astype(BF16)
    d_gate_one = jnp.sum(middle_grad * branch, axis=1)
    branch_grad_all = gather(branch_grad, "seq", 1)
    my_columns = lax.dynamic_slice_in_dim(branch_grad_all, me * part, part, 2)
    grad_out = mm("ire,ird->ed", mixed_all, my_columns)
    out_w_rows = lax.dynamic_slice_in_dim(out_w, me * part, part, 0)
    mixed_grad = mm("ird,ed->ire", branch_grad_all, out_w_rows).astype(BF16).reshape(items, length, heads, DH)

    prob_grad = mm("iqhd,ikhd->ihqk", mixed_grad, values)
    delta = jnp.sum(probs * prob_grad, axis=-1, keepdims=True)
    score_grad = (probs * (prob_grad - delta)).astype(BF16)
    query_grad = mm("ihqk,ikhd->iqhd", score_grad, keys) * 0.125
    key_grad = mm("ihqk,iqhd->ikhd", score_grad, queries) * 0.125
    value_grad = mm("ihqk,iqhd->ikhd", probs_low, mixed_grad)
    merged_grad = jnp.concatenate(
        [term.reshape(items, length, part) for term in (query_grad, key_grad, value_grad)], axis=-1
    ).astype(BF16)
    wide = score_grad.astype(F32)
    kept = jnp.sum(jnp.where(same[:, None], wide, 0.0), axis=0)
    crossed = jnp.sum(jnp.where(same[:, None], 0.0, wide), axis=(0, 2, 3))
    skewed = jnp.pad(kept[:, :, ::-1], ((0, 0), (0, 0), (0, length))).reshape(heads, -1)
    skewed = skewed[:, : length * (2 * length - 1)].reshape(heads, length, 2 * length - 1)
    lines = jnp.sum(skewed, axis=1)
    middle_line = length - 1
    low_end = jnp.sum(lines[:, : middle_line - RR + 1], axis=1)
    high_end = jnp.sum(lines[:, middle_line + RR :], axis=1)
    near = lines[:, middle_line - RR + 1 : middle_line + RR]
    my_table_grad = jnp.concatenate([low_end[:, None], near, high_end[:, None], crossed[:, None]], axis=1).T
    table_grad = lax.psum(
        lax.dynamic_update_slice_in_dim(jnp.zeros((CLASSES, H), F32), my_table_grad, me * heads, 1), ("dp", "seq")
    )
    grad_embed, grad_gain, grad_pair = pair_pull(table_grad)

    grad_qkv = mm("ird,ire->de", first, merged_grad)
    first_grad = scatter(mm("ire,de->ird", merged_grad, qkv_w).astype(BF16), "seq", 1).astype(F32)
    my_norm, my_inv = mine(first_norm), mine(first_inv)
    d_shift_one = jnp.sum(first_grad, axis=1)
    d_scale_one = jnp.sum(first_grad * my_norm, axis=1)
    input_grad = middle_grad + norm_back(first_grad * (1.0 + scale_one), my_norm, my_inv)
    modulation_grad = jnp.concatenate(
        [d_shift_one, d_scale_one, d_gate_one, d_shift_two, d_scale_two, d_gate_two], axis=-1
    )
    modulation_grads = gather(lax.psum(modulation_grad, "seq"), "dp", 0)
    grad_ada = jnp.einsum("ic,ie->ce", squashed_part.astype(F32), modulation_grads, precision=HIGHEST)

    def owned(grad):
        return scatter(grad.astype(BF16), "dp", 0)

    def everyone(grad):
        return lax.all_gather(grad, "seq", axis=0)

    shares_qkv = everyone(owned(grad_qkv)).reshape(seq, shard, 3, part)
    shares_out = everyone(owned(grad_out))
    shares_gate_up = everyone(owned(grad_gate_up)).reshape(seq, shard, 2, dp, strip)
    shares_down = everyone(owned(grad_down))
    return (
        result,
        input_grad.astype(BF16),
        jnp.transpose(shares_qkv, (1, 2, 0, 3)).reshape(shard, -1).astype(F32),
        jnp.transpose(shares_out, (1, 0, 2)).reshape(shard, -1).astype(F32),
        jnp.transpose(shares_gate_up, (1, 2, 3, 0, 4)).reshape(shard, -1).astype(F32),
        shares_down.reshape(seq * strip, width).astype(F32),
        grad_ada,
        grad_embed,
        grad_gain,
        grad_pair,
    )


MESH = pl.DeviceIdType.MESH
LANES = 128


def nn(a, b):
    return jnp.dot(a, b, preferred_element_type=F32)


def nt(a, b):
    return lax.dot_general(a, b, (((1,), (1,)), ((), ())), preferred_element_type=F32)


def tn(a, b):
    return lax.dot_general(a, b, (((0,), (0,)), ((), ())), preferred_element_type=F32)


def skew(tile, back):
    row = lax.broadcasted_iota(jnp.int32, tile.shape, 0)
    for bit in range(7):
        turn = LANES - (1 << bit) if back else 1 << bit
        tile = jnp.where(((row >> bit) & 1) == 1, pltpu.roll(tile, turn, 1), tile)
    return tile


class Sizes:
    def __init__(self, rows, width, seq, dp, shard, down_shard, ada_rows, conditioning):
        self.rows, self.width, self.seq, self.dp = rows, width, seq, dp
        self.shard, self.ada_rows, self.conditioning = shard, ada_rows, conditioning
        self.strip = down_shard // seq
        self.length = rows * seq
        self.heads = H // seq
        self.part = self.heads * DH
        self.hidden = self.strip * dp
        self.far = dp // 2
        self.half = shard // 2
        self.blocks = self.length // LANES


def under(where, work):
    if where is None:
        work()
    else:
        pl.when(where)(work)


class Wires:
    def __init__(self, send, recv):
        self.send, self.recv, self.count, self.started = send, recv, 0, []

    def reserve(self, count=1):
        first = self.count
        self.count += count
        return first

    def make(self, number, source, target, device):
        return pltpu.make_async_remote_copy(
            src_ref=source,
            dst_ref=target,
            send_sem=self.send.at[number],
            recv_sem=self.recv.at[number],
            device_id=device,
            device_id_type=MESH,
        )

    def go(self, number, source, target, device, where=None):
        copy = self.make(number, source, target, device)
        under(where, copy.start)
        self.started.append((copy, where))
        return copy

    def settle(self, copy):
        copy.wait_send()
        self.started = [other for other in self.started if other[0] is not copy]

    def finish(self):
        for copy, where in self.started:
            under(where, copy.wait_send)
        self.started = []


def layer_kernel(sizes, names, *refs):
    r = types.SimpleNamespace(**dict(zip(names, refs, strict=True)))
    n = sizes
    rows, width, part, heads, length, hid = n.rows, n.width, n.part, n.heads, n.length, n.hidden
    half_rows = rows // 2
    d, s = lax.axis_index("dp"), lax.axis_index("seq")
    z, x = d // 2, lax.rem(d, 2)
    y, c = s // 2, lax.rem(s, 2)
    ox, oy, oc = 1 - x, 1 - y, 1 - c
    at_x = (z * 2 + ox, s)
    at_y = (d, oy * 2 + c)
    at_c = (d, y * 2 + oc)

    def z_plus(k):
        return lax.rem(z + k, n.far)

    def at_z(k):
        return (z_plus(k) * 2 + x, s)

    wires = Wires(r.send_sem, r.recv_sem)
    dp_peers = [(k, e) for k in range(n.far) for e in range(2) if k or e]
    seq_peers = [(1, 0), (0, 1), (1, 1)]

    def dp_peer(k, e):
        xx = lax.rem(x + e, 2)
        return z_plus(k) * 2 + xx, lax.rem(z + n.far - k, n.far) * 2 + xx

    def seq_peer(a, b):
        return lax.rem(y + a, 2) * 2 + lax.rem(c + b, 2)

    local_count = [0]

    def local(source, target):
        copy = pltpu.make_async_copy(source, target, r.local_sem.at[local_count[0]])
        local_count[0] += 1
        copy.start()
        return copy

    qkv_stage, gate_up_stage = r.second_t, r.gate_up_grads
    staged = [
        local(r.qkv.at[:, q * width : (q + 1) * width], qkv_stage.at[q * n.shard : (q + 1) * n.shard, 0:width])
        for q in range(3)
    ]
    staged_gate_up = [
        local(r.gate_up.at[:, q * 2 * hid : (q + 1) * 2 * hid], gate_up_stage.at[q * n.shard : (q + 1) * n.shard])
        for q in range(n.seq)
    ]
    own_shard = pl.ds(pl.multiple_of(d * n.shard, n.shard), n.shard)
    r.cond_all[d] = jnp.broadcast_to(r.condition[...].astype(F32), (8, n.conditioning))
    barrier = pltpu.get_barrier_semaphore()
    for k, e in dp_peers:
        pl.semaphore_signal(barrier, inc=1, device_id=(dp_peer(k, e)[0], s), device_id_type=MESH)
    for a, b in seq_peers:
        pl.semaphore_signal(barrier, inc=1, device_id=(d, seq_peer(a, b)), device_id_type=MESH)
    for copy in staged:
        copy.wait()
    for side in range(n.seq):

        @pl.when(s == side)
        def _():
            r.w_qkv[own_shard, :] = jnp.concatenate(
                [
                    qkv_stage[q * n.shard : (q + 1) * n.shard, side * part + h * DH : side * part + (h + 1) * DH]
                    for h in range(heads)
                    for q in range(3)
                ],
                axis=1,
            )

    pl.semaphore_wait(barrier, len(dp_peers) + len(seq_peers))

    class SeqGather:
        def __init__(self, block):
            self.block, self.first = block, wires.reserve(3)
            self.mine, self.from_y, self.from_c, self.from_yc = s, at_y[1], at_c[1], oy * 2 + oc

        def start(self, source=None):
            mine = self.block(self.mine)
            source = mine if source is None else source
            self.sent = [wires.go(self.first, source, mine, at_y), wires.go(self.first + 1, source, mine, at_c)]

        def hand_on(self):
            place = self.block(self.from_y)
            wires.make(self.first, place, place, at_y).wait_recv()
            self.sent.append(wires.go(self.first + 2, place, place, at_c))

        def settle(self):
            for copy in self.sent:
                wires.settle(copy)

        def wait_core(self):
            place = self.block(self.from_c)
            wires.make(self.first + 1, place, place, at_c).wait_recv()

        def wait_last(self):
            place = self.block(self.from_yc)
            wires.make(self.first + 2, place, place, at_c).wait_recv()

        def wait(self):
            self.hand_on()
            self.wait_core()
            self.wait_last()

    last_z = n.far - 1

    class Wave:
        def __init__(self, block, direct=False):
            self.block, self.first, self.direct = block, wires.reserve(4), direct

        def send(self, source=None):
            mine = self.block(z)
            source = mine if source is None else source
            wires.go(self.first + 1, source, mine, at_z(1), None if self.direct else z != last_z)
            wires.go(self.first + 3, source, mine, at_z(3), None if self.direct else z != 0)
            wires.go(self.first + 2, source, mine, at_z(2))

        def relay(self):
            place = self.block(z_plus(2))
            wires.make(self.first + 2, place, place, at_z(2)).wait_recv()
            if not self.direct:
                wires.go(self.first, place, place, at_z(1), z == last_z - 1)
                wires.go(self.first, place, place, at_z(3), z == 1)

        def arrive(self, k):
            place = self.block(z_plus(n.far - k))
            far_end = z == (0 if k == 1 else last_z)
            near = wires.make(self.first + k, place, place, at_z(k))
            if self.direct:
                near.wait_recv()
                return
            far = wires.make(self.first, place, place, at_z(k))
            under(far_end, far.wait_recv)
            under(jnp.logical_not(far_end), near.wait_recv)

    class DpGather:
        def __init__(self, source, place, direct=False):
            self.source, self.place, self.first = source, place, wires.reserve(n.far)
            self.wave = Wave(lambda zz: place(zz * 2 + x), direct)

        def start(self):
            mine = self.place(d)
            self.own = None if self.source is None else local(self.source, mine)
            wires.go(self.first, mine if self.source is None else self.source, mine, at_x)

        def along_z(self):
            self.wave.send(self.source)

        def across(self, k):
            place = self.place(z_plus(n.far - k) * 2 + x)
            wires.go(self.first + k, place, place, at_x)

        def relay(self):
            self.wave.relay()
            self.across(2)

        def hand_on(self):
            for k in (1, 3):
                self.wave.arrive(k)
                self.across(k)

        def wait(self):
            if self.own is not None:
                self.own.wait()
            for k in range(n.far):
                place = self.place(z_plus(n.far - k) * 2 + ox)
                wires.make(self.first + k, place, place, at_x).wait_recv()

    class DpGatherX:
        def __init__(self, source, place):
            self.source, self.place, self.first = source, place, wires.reserve()
            self.waves = Wave(lambda zz: place(zz * 2 + x)), Wave(lambda zz: place(zz * 2 + ox))

        def start(self):
            self.own = local(self.source, self.place(d))
            wires.go(self.first, self.source, self.place(d), at_x)

        def along_z(self):
            self.waves[0].send(self.source)

        def cross(self):
            place = self.place(z * 2 + ox)
            wires.make(self.first, place, place, at_x).wait_recv()
            self.waves[1].send()

        def relay(self, which):
            self.waves[which].relay()

        def wait(self):
            self.own.wait()
            for wave in self.waves:
                wave.arrive(1)
                wave.arrive(3)

    class SeqReduce:
        def __init__(self, sib, got, over, come):
            self.sib, self.got, self.over, self.come = sib, got, over, come
            self.first, self.sent = wires.reserve(3), []

        def put_core(self, index):
            def put(lanes, block):
                self.sib[index, :, lanes] = block.astype(BF16)

            return put

        def to_core(self, index):
            self.sent.append(wires.go(self.first + index, self.sib.at[index], self.got.at[index], at_c))

        def wait_far(self):
            wires.make(self.first + 1, self.sib.at[1], self.got.at[1], at_c).wait_recv()

        def put_y(self):
            def put(lanes, block):
                self.over[:, lanes] = (block + self.got[1, :, lanes].astype(F32)).astype(BF16)

            return put

        def to_y(self):
            self.sent.append(wires.go(self.first + 2, self.over, self.come, at_y))

        def settle(self):
            for copy in self.sent:
                wires.settle(copy)

        def wait(self):
            wires.make(self.first, self.sib.at[0], self.got.at[0], at_c).wait_recv()
            wires.make(self.first + 2, self.over, self.come, at_y).wait_recv()

        def total(self, own, place):
            return own[place, :] + self.got[0, place, :].astype(F32) + self.come[place, :].astype(F32)

    at_end = z * (last_z - z) == 0
    inside = z * (last_z - z) != 0

    def mirror(k):
        return (z, z + 1 - 2 * lax.rem(z, 2), lax.rem(z + 2, n.far), last_z - z)[k]

    def at_mirror(k):
        return (mirror(k) * 2 + x, s)

    def add_up(target, parts):
        def one(q, _):
            place = pl.ds(pl.multiple_of(q * 16, 16), 16)
            total = parts[0][..., place, :].astype(F32)
            for other in parts[1:]:
                total = total + other[..., place, :].astype(F32)
            target[..., place, :] = total.astype(BF16)
            return 0

        lax.fori_loop(0, target.shape[-2] // 16, one, 0)

    class Shares:
        def __init__(self, mine, share):
            self.mine, self.share = mine, share
            self.gather = SeqGather(lambda t: share.at[t])

        def start(self):
            self.own = local(self.mine, self.share.at[s])
            self.gather.start(self.mine)

        def hand_on(self):
            self.gather.hand_on()

        def wait(self):
            self.gather.wait_core()
            self.gather.wait_last()
            self.own.wait()

    class DpReduce:
        def __init__(self, grad, got, come, far, mine, share):
            self.grad, self.got, self.come, self.far, self.mine = grad, got, come, far, mine
            self.first, self.second, self.shares = wires.reserve(n.far), wires.reserve(n.far), Shares(mine, share)

        def start(self):
            for k in (3, 1, 2, 0):
                to = mirror(k)
                wires.go(self.first + k, self.grad.at[ox, to], self.got.at[to], at_x)

        def along_z(self, k):
            to = mirror(k)
            block = self.grad.at[x, to]
            wires.make(self.first + k, self.grad.at[ox, to], self.got.at[to], at_x).wait_recv()
            add_up(block, (block, self.got.at[to]))
            if k == 3:
                wires.go(self.second, block, self.far, at_mirror(1), at_end)
                wires.go(self.second + 3, block, self.come.at[0], at_mirror(3), inside)
            elif k == 1:
                wires.go(self.second + 1, block, self.come.at[2], at_mirror(1))
            elif k == 2:

                @pl.when(inside)
                def _():
                    wires.make(self.second, block, self.far, at_mirror(1)).wait_recv()
                    add_up(block, (block, self.far))

                wires.go(self.second + 2, block, self.come.at[1], at_mirror(2))

        def finish(self):
            for k in (2, 1):
                wires.make(self.second + k, self.mine, self.come.at[3 - k], at_mirror(k)).wait_recv()
            near = self.grad.at[x, z], self.come.at[1], self.come.at[2]

            @pl.when(at_end)
            def _():
                add_up(self.mine, near)

            @pl.when(inside)
            def _():
                wires.make(self.second + 3, self.mine, self.come.at[0], at_mirror(3)).wait_recv()
                add_up(self.mine, (*near, self.come.at[0]))

            self.shares.start()

    class DpReduceZ:
        def __init__(self, grad, come, far, got, mine, share):
            self.grad, self.come, self.far, self.got, self.mine = grad, come, far, got, mine
            self.first, self.cross, self.shares = wires.reserve(4), wires.reserve(), Shares(mine, share)

        def start(self, which):
            ways = (
                (0, self.far, 1, at_end),
                (3, self.come.at[0], 3, inside),
                (1, self.come.at[2], 1, None),
                (2, self.come.at[1], 2, at_end),
            )
            for k, place, to, where in ways[2 * which : 2 * which + 2]:
                block = self.grad.at[:, mirror(k or 3)]
                wires.go(self.first + k, block, place, at_mirror(to), where)

        def merge(self):
            block = self.grad.at[:, mirror(2)]

            @pl.when(inside)
            def _():
                wires.make(self.first, block, self.far, at_mirror(1)).wait_recv()
                add_up(block, (block, self.far))

            wires.go(self.first + 2, block, self.come.at[1], at_mirror(2), inside)

        def across(self):
            block = self.grad.at[:, z]
            for k in (2, 1):
                wires.make(self.first + k, self.far, self.come.at[3 - k], at_mirror(k)).wait_recv()
            near = block, self.come.at[1], self.come.at[2]

            @pl.when(at_end)
            def _():
                add_up(block, near)

            @pl.when(inside)
            def _():
                wires.make(self.first + 3, self.far, self.come.at[0], at_mirror(3)).wait_recv()
                add_up(block, (*near, self.come.at[0]))

            wires.go(self.cross, self.grad.at[ox, z], self.got, at_x)

        def finish(self):
            wires.make(self.cross, self.mine, self.got, at_x).wait_recv()
            add_up(self.mine, (self.grad.at[x, z], self.got))
            self.shares.start()

    step = 64

    def by_rows(count, work, start=0, unroll=2):
        def one(q, carry):
            return work(pl.ds(pl.multiple_of(q * step, step), step), carry)

        return lax.fori_loop(0, count // step, one, start, unroll=unroll)

    wide = 2 * LANES

    def by_lanes(count, work, unroll=True):
        def one(q, _):
            work(pl.ds(pl.multiple_of(q * wide, wide), wide))
            return 0

        lax.fori_loop(0, count // wide, one, 0, unroll=unroll)

    def fold_rows(array):
        return jnp.sum(array.reshape(step // 8, 8, width), axis=0)

    hidden_all, grads_all = r.hidden_all, r.grads_all

    def rows_of(ref):
        return lambda t: ref.at[pl.ds(pl.multiple_of(t * rows, rows), rows)]

    hidden_gather, up_gather = SeqGather(rows_of(hidden_all)), SeqGather(rows_of(grads_all))
    def shard_rows(ref, height, lanes=slice(None)):
        return lambda t: ref.at[pl.ds(pl.multiple_of(t * height, height), height), lanes]

    def lane_half(side):
        return pl.ds(pl.multiple_of(side * (width // 2), width // 2), width // 2)

    lanes_y = lane_half(y)
    qkv_gathers = [
        DpGather(None, shard_rows(r.w_qkv, n.shard, lanes), True)
        for lanes in (slice(0, 2 * LANES), slice(2 * LANES, 3 * part))
    ]
    out_gather = DpGather(
        r.out.at[pl.ds(pl.multiple_of(c * n.half, n.half), n.half), lanes_y],
        lambda t: r.w_out.at[t, c, :, lanes_y],
    )
    half_strip = n.strip // 2

    def down_half(kind, side):
        low = side * half_strip
        return kind(
            r.down.at[pl.ds(pl.multiple_of(s * n.strip + low, half_strip), half_strip)],
            lambda t: r.w_down.at[pl.ds(pl.multiple_of(t * n.strip + low, half_strip), half_strip)],
        )

    down_near, down_gather = down_half(DpGather, 0), down_half(DpGatherX, 1)
    pieces = [
        DpGather(None, shard_rows(r.w_gate_up, n.shard, slice(q * (hid // 2), (q + 1) * (hid // 2))))
        for q in (0, 2, 1, 3)
    ]

    def out_block(t):
        ty, tc = t // 2, lax.rem(t, 2)
        return r.w_out.at[:, tc, :, lane_half(ty)]

    out_share = SeqGather(out_block)

    cond_first, mod_first = wires.reserve(len(dp_peers)), wires.reserve(len(dp_peers))
    cond_all, mod_send, mod_recv = r.cond_all, r.mod_send, r.mod_recv
    for i, (k, e) in enumerate(dp_peers):
        wires.go(cond_first + i, cond_all.at[d], cond_all.at[d], (dp_peer(k, e)[0], s))
    for piece in qkv_gathers:
        piece.along_z()
        piece.start()
    own_hidden = local(r.hidden, hidden_gather.block(s))
    keep_hidden = local(r.hidden, r.hidden_own)
    keep_grads = local(r.out_grad, r.upstream)
    hidden_gather.start(r.hidden)
    own_grads = local(r.out_grad, up_gather.block(s))


    for i, (k, e) in enumerate(dp_peers):
        place = cond_all.at[dp_peer(k, e)[1]]
        wires.make(cond_first + i, place, place, (dp_peer(k, e)[0], s)).wait_recv()
    item_of = lax.broadcasted_iota(jnp.int32, (n.dp, n.conditioning), 0)
    conditions = jnp.where(item_of == 0, cond_all[0], 0.0)
    for i in range(1, n.dp):
        conditions = jnp.where(item_of == i, cond_all[i], conditions)
    squashed = (conditions * (1.0 / (1.0 + jnp.exp(-conditions)))).astype(BF16).astype(F32)
    r.squashed[...] = squashed.T
    squashed_rows = r.squashed[pl.ds(pl.multiple_of(d * n.ada_rows, n.ada_rows), n.ada_rows), :]
    ada_part = tn(squashed_rows.astype(BF16), r.ada[...])
    for i in range(n.dp):
        mod_send[i] = ada_part[i : i + 1]
    mod_recv[d] = mod_send[d]
    for i, (k, e) in enumerate(dp_peers):
        wires.go(mod_first + i, mod_send.at[dp_peer(k, e)[0]], mod_recv.at[d], (dp_peer(k, e)[0], s))
    for copy in staged_gate_up:
        copy.wait()
    group = n.seq * n.strip
    for side in range(n.seq):

        @pl.when(s == side)
        def _():
            strips = []
            for number in range(2 * n.dp):
                block, low = divmod(number * group, 2 * hid)
                low += side * n.strip
                strips.append(gate_up_stage[block * n.shard : (block + 1) * n.shard, low : low + n.strip])
            r.w_gate_up[own_shard, :] = jnp.concatenate(strips, axis=1)

    for piece in (out_gather, *pieces[:2]):
        piece.start()
        piece.along_z()
    down_gather.start()
    down_gather.along_z()
    down_near.start()
    down_near.along_z()
    for piece in pieces[2:]:
        piece.start()
    hidden_gather.hand_on()
    up_gather.start(r.out_grad)
    for piece in qkv_gathers:
        piece.relay()
        piece.hand_on()

    bias, table_t = r.bias, r.table_t
    embed = r.pair_embed[...].astype(F32)
    normal, _ = layer_norm(embed, 1e-05)
    scaled = normal * r.pair_gain[...].astype(F32)
    scaled = jnp.concatenate([scaled, jnp.zeros((LANES - CLASSES, scaled.shape[1]), F32)], axis=0)
    table_t[...] = lax.dot_general(
        r.pair_weight[...].astype(F32),
        scaled,
        (((1,), (1,)), ((), ())),
        precision=HIGHEST,
        preferred_element_type=F32,
    )

    def table_line(h):
        return table_t[pl.ds(s * heads + h, 1), :]

    key_in = lax.broadcasted_iota(jnp.int32, (LANES, LANES), 0)
    query_in = lax.broadcasted_iota(jnp.int32, (LANES, LANES), 1)
    middle_tile = n.blocks - 1

    def build_bias(h, _):
        line = table_line(h)
        near = skew(jnp.broadcast_to(pltpu.roll(line, LANES - RR, 1), (LANES, LANES)), False)
        low_end = jnp.broadcast_to(line[:, 0:1], (LANES, LANES))
        high_end = jnp.broadcast_to(line[:, 2 * RR : 2 * RR + 1], (LANES, LANES))
        for tile in range(2 * n.blocks - 1):
            away = tile - middle_tile
            apart = query_in - key_in - away * LANES
            if away < -1:
                value = high_end
            elif away > 1:
                value = low_end
            else:
                value = jnp.where(apart >= RR, high_end, jnp.where(apart <= -RR, low_end, near))
            bias[h, tile * LANES : (tile + 1) * LANES] = value
        return 0

    lax.fori_loop(0, heads, build_bias, 0)

    own_hidden.wait()
    hidden_gather.wait_core()
    hidden_gather.wait_last()
    for i, (k, e) in enumerate(dp_peers):
        place = mod_recv.at[dp_peer(k, e)[1]]
        wires.make(mod_first + i, mod_send.at[d], place, (dp_peer(k, e)[0], s)).wait_recv()
    modulation = mod_recv[0]
    for i in range(1, n.dp):
        modulation = modulation + mod_recv[i]
    r.modulation[...] = modulation

    def vector(index):
        return r.modulation[:, index * width : (index + 1) * width]

    shift_one, scale_one, gate_one, shift_two, scale_two, gate_two = range(6)
    first = hidden_all
    hidden_gather.settle()

    def make_first(t, _):
        place = pl.ds(pl.multiple_of(t * LANES, LANES), LANES)
        normal, _ = layer_norm(hidden_all[place, :].astype(F32))
        first[place, :] = (normal * (1.0 + vector(scale_one)) + vector(shift_one)).astype(BF16)
        r.norm_t[:, place] = normal.astype(BF16).T
        return 0

    lax.fori_loop(0, n.blocks, make_first, 0)
    few_rows = jnp.concatenate([vector(q) for q in range(6)] + [vector(0)] * 2, axis=0)
    r.mod_t[...] = few_rows.T
    out_gather.relay()
    out_gather.hand_on()
    pieces[0].relay()

    for piece in qkv_gathers:
        piece.wait()
    w_qkv = r.w_qkv
    keys = r.keys
    keys_t, values_t, queries_t = r.keys_t, r.values_t, r.queries_t
    w_qkv_t = r.inner_t

    def turn_weight(q, _):
        place = pl.ds(pl.multiple_of(q * 2 * LANES, 2 * LANES), 2 * LANES)
        w_qkv_t[0 : 3 * part, place] = w_qkv[place, :].T
        return 0

    lax.fori_loop(0, width // (2 * LANES), turn_weight, 0)

    def project(t, _):
        place = pl.ds(pl.multiple_of(t * rows, rows), rows)
        block = first[place, :]
        for low in range(0, 3 * part, wide):
            merged = nn(block, w_qkv[:, low : min(low + wide, 3 * part)]).astype(BF16)
            for q in range(merged.shape[1] // DH):
                h, kind = divmod(low // DH + q, 3)
                if kind == 1:
                    keys[h, place, :] = merged[:, q * DH : (q + 1) * DH]
        for h in range(heads):
            merged_t = nt(w_qkv_t[h * 3 * DH : (h + 1) * 3 * DH, 0:width], block).astype(BF16)
            queries_t[h, t] = (merged_t[:DH].astype(F32) * 0.125).astype(BF16)
            keys_t[h, t] = merged_t[DH : 2 * DH]
            values_t[h, t] = merged_t[2 * DH :]
        return 0

    lax.fori_loop(0, n.seq, project, 0)
    pieces[0].hand_on()
    down_gather.cross()
    for piece in pieces[2:]:
        piece.along_z()
    pieces[1].relay()

    valid, broken = r.valid_len[0], r.chain_break[0]
    exps, outs_t, inverse = r.exps, r.outs_t, r.inverse
    tiles = rows // LANES
    order = [oy * 2 + c, oy * 2 + oc, y * 2 + oc, s]

    raw = r.raw

    def tile_parts(t, tile):
        number = t * tiles + tile
        query_side = number * LANES + lax.broadcasted_iota(jnp.int32, (1, LANES), 1) >= broken
        for q in range(n.blocks):
            key_pos = q * LANES + lax.broadcasted_iota(jnp.int32, (LANES, LANES), 0)
            strip = pl.ds(pl.multiple_of((n.blocks - 1 + q - number) * LANES, LANES), LANES)
            yield slice(q * LANES, (q + 1) * LANES), strip, key_pos, (key_pos >= broken) == query_side

    def eights(array):
        return array.reshape(LANES // 8, 8, LANES)

    def attend(t):
        def one_head(h, _):
            for q in range(n.seq):
                place = slice(q * rows, (q + 1) * rows)
                raw[place, 0:rows] = nn(keys[h, place, :], queries_t[h, t])
            for tile in range(tiles):
                lanes = slice(tile * LANES, (tile + 1) * LANES)
                far_side = jnp.broadcast_to(table_line(h)[:, CLASSES - 1 : CLASSES], (1, LANES))
                top = jnp.full((8, LANES), -1e30, F32)
                for place, strip, key_pos, same in tile_parts(t, tile):
                    logits = raw[place, lanes] + jnp.where(same, bias[h, strip, :], far_side)
                    logits = jnp.where(key_pos < valid, logits, -1e30)
                    raw[place, lanes] = logits
                    top = jnp.maximum(top, jnp.max(eights(logits), axis=0))
                top = jnp.max(top, axis=0, keepdims=True)
                total = jnp.zeros((8, LANES), F32)
                for q in range(n.blocks):
                    place = slice(q * LANES, (q + 1) * LANES)
                    powers = jnp.exp(raw[place, lanes] - top)
                    total = total + jnp.sum(eights(powers), axis=0)
                    exps[h, t, place, lanes] = powers.astype(BF16)
                inverse[h, t, :, lanes] = 1.0 / jnp.sum(total, axis=0, keepdims=True)
            values_wide = jnp.concatenate([values_t[h, q] for q in range(n.seq)], axis=1)
            outs_t[h, t] = nn(values_wide, exps[h, t]) * inverse[h, t]
            return 0

        lax.fori_loop(0, heads, one_head, 0)

    mixed_first = wires.reserve(3)
    mixed_send, mixed_recv = r.mixed_send, r.mixed_recv
    mixed_sent = []
    to_send = [at_y, (d, oy * 2 + oc), at_c]
    out_gather.wait()
    out_share.start()

    def mixed_block(t):
        return jnp.concatenate([outs_t[h, t] for h in range(heads)], axis=0).T.astype(BF16)

    def send_mixed(i):
        mixed_sent.append(wires.go(mixed_first + i, mixed_send.at[i], mixed_recv.at[s], to_send[i]))

    def far_blocks(i, _):
        t = oy * 2 + lax.rem(c + i, 2)
        attend(t)
        mixed_send[i] = mixed_block(t)
        return 0

    lax.fori_loop(0, 2, far_blocks, 0)
    send_mixed(0)
    send_mixed(1)
    up_gather.hand_on()
    pieces[1].hand_on()
    down_gather.relay(0)
    out_share.hand_on()
    attend(order[2])
    mixed_send[2] = mixed_block(order[2])
    send_mixed(2)
    down_near.relay()
    attend(s)
    mixed_recv[s] = mixed_block(s)
    down_near.hand_on()

    out_share.wait_core()
    out_share.wait_last()

    def w_out(q, lanes=slice(None)):
        shards = part // n.shard
        block = r.w_out[q * shards : (q + 1) * shards, :, :, lanes]
        return block.reshape(part, block.shape[-1])

    for i in range(3):
        place = mixed_recv.at[order[i]]
        wires.make(mixed_first + i, mixed_send.at[i], place, to_send[i]).wait_recv()
    keep_hidden.wait()

    def make_branch(lanes):
        branch = nn(mixed_recv[0], w_out(0, lanes))
        for q in range(1, n.seq):
            branch = branch + nn(mixed_recv[q], w_out(q, lanes))
        r.branch[:, lanes] = branch

    by_lanes(width, make_branch)
    second_all = r.second_all
    second_gather = SeqGather(rows_of(second_all))

    def make_second(place, _):
        middle = r.hidden_own[place, :].astype(F32) + vector(gate_one) * r.branch[place, :]
        r.middle[place, :] = middle
        normal, _ = layer_norm(middle)
        r.branch_grad[place, :] = (normal * (1.0 + vector(scale_two)) + vector(shift_two)).astype(BF16)
        return 0

    by_rows(rows, make_second)
    second_all[pl.ds(pl.multiple_of(s * rows, rows), rows), :] = r.branch_grad[...]
    second_gather.start()

    own_grads.wait()
    up_gather.wait_core()
    up_gather.wait_last()
    up_gather.settle()
    feed_grads = grads_all

    def make_feed_grads(place, _):
        feed_grads[place, :] = (vector(gate_two) * grads_all[place, :].astype(F32)).astype(BF16)
        return 0

    by_rows(length, make_feed_grads)
    down_gather.relay(1)
    for piece in (pieces[0], pieces[1], down_near, down_gather):
        piece.wait()
    w_gate_up, w_down = r.w_gate_up, r.w_down
    inner, inner_t, gate_up_grads, second_t = r.inner, r.inner_t, r.gate_up_grads, r.second_t
    feed_places = (r.feed_sib, r.feed_got, r.feed_over, r.feed_come)
    feed_reduce = SeqReduce(*feed_places)
    second_reduce = SeqReduce(r.second_sib, r.second_got, r.second_over, r.second_come)
    half_hid = hid // 2

    def rows_at(t):
        return pl.ds(pl.multiple_of(t * rows, rows), rows)

    def units(t, side):
        place, low = rows_at(t), side * half_hid
        block, given = second_all[place, :], feed_grads[place, :]
        gates, ups, inner_grads = (raw.at[i * rows : (i + 1) * rows] for i in range(3))
        gates[...] = nn(block, w_gate_up[:, low : low + half_hid])
        ups[...] = nn(block, w_gate_up[:, hid + low : hid + low + half_hid])
        inner_grads[...] = nt(given, w_down[low : low + half_hid, :])
        for first_row in range(0, rows, step):
            few = slice(first_row, first_row + step)
            gate, up, inner_grad = gates[few, :], ups[few, :], inner_grads[few, :]
            sigmoid = 1.0 / (1.0 + jnp.exp(-gate))
            silu = gate * sigmoid
            to = pl.ds(pl.multiple_of(t * rows + first_row, step), step)
            inner[to, low : low + half_hid] = (silu * up).astype(BF16)
            gate_up_grads[to, low : low + half_hid] = (
                inner_grad * up * sigmoid * (1.0 + gate * (1.0 - sigmoid))
            ).astype(BF16)
            gate_up_grads[to, hid + low : hid + low + half_hid] = (inner_grad * silu).astype(BF16)

    def second_part(t, put):
        by_lanes(width, lambda lanes: put(lanes, nt(gate_up_grads[rows_at(t), :], w_gate_up[lanes, :])))

    def feed_part(t, put):
        by_lanes(width, lambda lanes: put(lanes, nn(inner[rows_at(t), :], w_down[:, lanes])), False)

    def put_in(ref):
        def put(lanes, block):
            ref[:, lanes] = block.astype(ref.dtype)

        return put

    def units_of(side):
        def one(i, _):
            units(side * 2 + lax.rem(c + i, 2), 0)
            return 0

        lax.fori_loop(0, 2, one, 0)

    second_gather.wait_core()
    units_of(y)
    second_gather.hand_on()
    pieces[2].relay()
    second_gather.wait_last()
    pieces[2].hand_on()
    pieces[3].relay()
    units_of(oy)
    pieces[3].hand_on()

    gate_up_reduces = (
        DpReduce(r.gate_up0_grad, r.gate_up0_got, r.gate_up0_come, r.gate_up0_far, r.gate_up0_mine, r.gate_up0_share),
        DpReduce(r.gate_up1_grad, r.gate_up1_got, r.gate_up1_come, r.gate_up1_far, r.gate_up1_mine, r.gate_up1_share),
    )
    down_reduce = DpReduceZ(r.down_grad, r.down_come, r.down_far, r.down_got, r.down_mine, r.down_share)
    out_reduce = DpReduce(r.proj_grad, r.proj_got, r.proj_come, r.proj_far, r.proj_mine, r.proj_share)
    qkv_reduces = (
        DpReduce(r.qkv0_grad, r.qkv0_got, r.qkv0_come, r.qkv0_far, r.qkv0_mine, r.qkv0_share),
        DpReduce(r.qkv1_grad, r.qkv1_got, r.qkv1_come, r.qkv1_far, r.qkv1_mine, r.qkv1_share),
        DpReduce(r.qkv2_grad, r.qkv2_got, r.qkv2_come, r.qkv2_far, r.qkv2_mine, r.qkv2_share),
    )

    def turn_rows(source, target):
        def turn(t, _):
            target[:, rows_at(t)] = source[rows_at(t), :].T
            return 0

        lax.fori_loop(0, n.seq, turn, 0)

    def weight_grad(left_t, right, reduce, lows):
        height, few = reduce.grad.shape[2], n.dp // 2
        columns = reduce.grad.shape[3] // len(lows)
        for at, low in enumerate(lows):
            for first_of in range(0, n.dp, few):
                grad = nn(
                    left_t[first_of * height : (first_of + few) * height, :], right[:, low : low + columns]
                ).astype(BF16)
                for i in range(few):
                    to = first_of + i
                    reduce.grad[to % 2, to // 2, :, at * columns : (at + 1) * columns] = grad[
                        i * height : (i + 1) * height
                    ]

    turn_rows(second_all, second_t)
    weight_grad(second_t, gate_up_grads, gate_up_reduces[0], (0, hid))
    gate_up_reduces[0].start()
    pieces[2].wait()
    pieces[3].wait()
    far, over, near = oy * 2 + oc, oy * 2 + c, y * 2 + oc
    units(far, 1)
    second_part(far, second_reduce.put_core(1))
    second_reduce.to_core(1)
    units(over, 1)
    second_reduce.wait_far()
    second_part(over, second_reduce.put_y())
    second_reduce.to_y()
    units(near, 1)
    second_part(near, second_reduce.put_core(0))
    second_reduce.to_core(0)
    units(s, 1)
    second_part(s, put_in(r.second_own))

    weight_grad(second_t, gate_up_grads, gate_up_reduces[1], (half_hid, hid + half_hid))
    gate_up_reduces[1].start()
    gate_up_reduces[0].along_z(3)
    turn_rows(inner, inner_t)
    weight_grad(inner_t, feed_grads, down_reduce, (0, half_hid))
    down_reduce.start(0)
    gate_up_reduces[0].along_z(1)
    down_reduce.start(1)
    feed_part(far, feed_reduce.put_core(1))
    feed_reduce.to_core(1)
    feed_part(near, feed_reduce.put_core(0))
    feed_reduce.to_core(0)
    feed_reduce.wait_far()
    feed_part(over, feed_reduce.put_y())
    feed_part(s, put_in(r.feed_own))
    lax.fori_loop(0, width // (2 * LANES), turn_weight, 0)
    values = keys

    def turn_values(t, _):
        for h in range(heads):
            values[h, rows_at(t), :] = values_t[h, t].T
        return 0

    lax.fori_loop(0, n.seq, turn_values, 0)

    sums = r.mod_sums

    upstream = r.upstream
    keep_grads.wait()
    second_reduce.wait()
    kept_middle_grad, branch_grad = r.second_own, r.branch_grad
    empty = jnp.zeros((8, width), F32)

    def put_sum(index, array):
        sums[s, :, index * width : (index + 1) * width] = jnp.sum(array, axis=0, keepdims=True)

    def second_back(place, carry):
        second_grad = second_reduce.total(r.second_own, place)
        normal, inverted = layer_norm(r.middle[place, :])
        middle_grad = upstream[place, :].astype(F32) + norm_back(
            second_grad * (1.0 + vector(scale_two)), normal, inverted
        )
        kept_middle_grad[place, :] = middle_grad
        branch_grad[place, :] = (vector(gate_one) * middle_grad).astype(BF16)
        terms = (second_grad, second_grad * normal, middle_grad * r.branch[place, :])
        return tuple(total + fold_rows(term) for total, term in zip(carry, terms))

    for index, total in zip(
        (shift_two, scale_two, gate_one), by_rows(rows, second_back, (empty, empty, empty))
    ):
        put_sum(index, total)
    back_first = wires.reserve(3)
    for copy in mixed_sent:
        wires.settle(copy)
    back_all, back_recv = mixed_send, r.back_recv
    for q in range(n.seq):
        back_all[q] = nt(branch_grad[...], w_out(q)).astype(BF16)
    for i in range(3):
        wires.go(back_first + i, back_all.at[order[i]], back_recv.at[s], to_send[i])
    back_recv[s] = back_all[s]
    feed_reduce.to_y()

    out_first = wires.reserve(2)
    second_gather.settle()
    out_parts, quarter = second_all, n.dp * n.half

    def make_out_grad(lanes):
        for q in range(n.seq):
            grad = tn(mixed_recv[q], branch_grad[:, lanes]).astype(BF16)
            for i in range(part // n.half):
                number = q * (part // n.half) + i
                low = (number % 2) * quarter + (number // 2) * n.half
                out_parts[low : low + n.half, lanes] = grad[i * n.half : (i + 1) * n.half]

    by_lanes(width, make_out_grad)

    def out_rows(core):
        return out_parts.at[pl.ds(pl.multiple_of(core * quarter, quarter), quarter)]

    lanes_oy = pl.ds(pl.multiple_of(oy * (width // 2), width // 2), width // 2)

    def out_cores():
        wires.make(out_first, out_rows(oc), r.out_near, at_c).wait_recv()
        mine = out_parts[pl.ds(pl.multiple_of(c * quarter, quarter), quarter), :]
        r.out_near[...] = (r.out_near[...].astype(F32) + mine.astype(F32)).astype(BF16)
        wires.go(out_first + 1, r.out_near.at[:, lanes_oy], r.out_far, at_y)

    def out_sum():
        wires.make(out_first + 1, r.out_near.at[:, lanes_oy], r.out_far, at_y).wait_recv()
        total = (r.out_near[:, lanes_y].astype(F32) + r.out_far[...].astype(F32)).astype(BF16)
        for to in range(n.dp):
            r.proj_grad[to % 2, to // 2] = total[to * n.half : (to + 1) * n.half]
        out_reduce.start()

    dots_t, delta = r.dots_t, r.delta
    pair_grads, query_grads = r.pair_grads, r.query_grads
    bias[...] = jnp.zeros_like(bias)
    crossed, score_grad = r.crossed, inner.at[:, 0:rows]
    crossed[...] = jnp.zeros_like(crossed)
    pair_grads[...] = jnp.zeros_like(pair_grads)
    merged_grads = gate_up_grads

    def take_back(t):
        given_t = back_recv[t].T.astype(F32)
        for h in range(heads):
            scaled = (given_t[h * DH : (h + 1) * DH] * inverse[h, t]).astype(BF16)
            dots_t[h, t] = scaled
            delta[h, t] = jnp.sum(scaled.astype(F32) * outs_t[h, t], axis=0, keepdims=True)

    def attend_back(h, t, first_of):
        place = rows_at(t)
        for q in range(n.seq):
            some = slice(q * rows, (q + 1) * rows)
            raw[some, 0:rows] = nn(values[h, some, :], dots_t[h, t])
        for tile in range(tiles):
            lanes = slice(tile * LANES, (tile + 1) * LANES)
            across = jnp.zeros((8, LANES), F32)
            for keys_of, strip, _, same in tile_parts(t, tile):
                grad = exps[h, t, keys_of, lanes].astype(F32) * (raw[keys_of, lanes] - delta[h, t, :, lanes])
                kept = jnp.where(same, grad, 0.0)
                bias[h, strip, :] = bias[h, strip, :] + kept
                across = across + jnp.sum(eights(grad - kept), axis=0)
                score_grad[keys_of, lanes] = grad.astype(BF16)
            crossed[h] = crossed[h] + jnp.sum(across, axis=0, keepdims=True)
        keys_wide = jnp.concatenate([keys_t[h, q] for q in range(n.seq)], axis=1)
        query_grads[place, :] = (nn(keys_wide, score_grad[...]) * 0.125).T.astype(BF16)
        queries, dots = queries_t[h, t].T, dots_t[h, t].T
        for q in range(n.seq):
            some = slice(q * rows, (q + 1) * rows)
            grad = jnp.concatenate([nn(score_grad[some, :], queries), nn(exps[h, t, some, :], dots)], axis=1)
            pair_grads[some, :] = grad if first_of else pair_grads[some, :] + grad

    def end_head(h):
        for q in range(n.seq):
            some = slice(q * rows, (q + 1) * rows)
            merged_grads[some, h * wide : h * wide + 3 * DH] = jnp.concatenate(
                [query_grads[some, :], pair_grads[some, :].astype(BF16)], axis=1
            )
        merged = merged_grads.at[:, h * wide : h * wide + 3 * DH]
        totals = nn(jnp.ones((16, length), BF16), merged[...])[0:1]
        few = n.dp // 2 * n.shard
        for first_of in range(0, width, few):
            place = slice(first_of, first_of + few)
            scale, shift = 1.0 + r.mod_t[place, 1:2], r.mod_t[place, 0:1]
            weights = w_qkv[place, h * 3 * DH : (h + 1) * 3 * DH].astype(F32)
            product = nn(r.norm_t[place, :], merged[...])
            d_shift = jnp.sum(weights * totals, axis=1, keepdims=True)
            d_scale = jnp.sum(weights * product, axis=1, keepdims=True)
            lane = lax.broadcasted_iota(jnp.int32, (few, LANES), 1)
            both = jnp.where(lane == 0, d_shift, jnp.where(lane == 1, d_scale, 0.0))
            r.first_sums[place, :] = both if h == 0 else r.first_sums[place, :] + both
            grad = (product * scale + totals * shift).astype(BF16)
            for i in range(n.dp // 2):
                to = first_of // n.shard + i
                low = i * n.shard
                qkv_reduces[h].grad[to % 2, to // 2] = jnp.concatenate(
                    [grad[low : low + n.half], grad[low + n.half : low + n.shard]], axis=1
                )
        qkv_reduces[h].start()

    def back_block(i):
        wires.make(back_first + i, back_recv.at[order[i]], back_recv.at[order[i]], to_send[i]).wait_recv()
        take_back(order[i])

    def some_of_head(h, side):
        def one(i, _):
            attend_back(h, side * 2 + lax.rem(c + i, 2), False)
            return 0

        lax.fori_loop(0, 2, one, 0)

    def rest_of_head(h):
        pair_grads[...] = jnp.zeros_like(pair_grads)

        def one(i, _):
            attend_back(h, lax.rem(y + i // 2, 2) * 2 + lax.rem(c + lax.rem(i, 2), 2), False)
            return 0

        lax.fori_loop(0, n.seq, one, 0)

    wires.go(out_first, out_rows(oc), r.out_near, at_c)
    gate_up_reduces[0].along_z(0)
    gate_up_reduces[1].along_z(3)
    take_back(s)
    back_block(2)
    some_of_head(0, y)
    gate_up_reduces[0].along_z(2)
    out_cores()
    back_block(0)
    back_block(1)
    some_of_head(0, oy)
    end_head(0)
    gate_up_reduces[1].along_z(1)
    rest_of_head(1)
    end_head(1)
    down_reduce.merge()
    rest_of_head(2)
    end_head(2)

    second_reduce.settle()
    first_reduce = SeqReduce(r.second_sib, r.second_got, r.second_over, r.second_come)

    def first_part(t, put):
        def by_heads(lanes):
            total = nn(merged_grads[rows_at(t), 0 : 3 * DH], w_qkv_t[0 : 3 * DH, lanes])
            for h in range(1, heads):
                total = total + nn(
                    merged_grads[rows_at(t), h * wide : h * wide + 3 * DH],
                    w_qkv_t[h * 3 * DH : (h + 1) * 3 * DH, lanes],
                )
            put(lanes, total)

        by_lanes(width, by_heads)

    first_part(oy * 2 + oc, first_reduce.put_core(1))
    first_reduce.to_core(1)
    first_reduce.wait_far()
    first_part(oy * 2 + c, first_reduce.put_y())
    first_reduce.to_y()
    first_part(y * 2 + oc, first_reduce.put_core(0))
    first_reduce.to_core(0)
    first_part(s, put_in(r.branch))
    gate_up_reduces[1].along_z(2)
    gate_up_reduces[1].along_z(0)
    for k in (3, 1, 2, 0):
        qkv_reduces[0].along_z(k)
    qkv_reduces[1].along_z(3)
    feed_reduce.wait()

    def make_result(place, total):
        feed = feed_reduce.total(r.feed_own, place)
        r.result[place, :] = (r.middle[place, :] + vector(gate_two) * feed).astype(BF16)
        return total + fold_rows(upstream[place, :].astype(F32) * feed)

    put_sum(gate_two, by_rows(rows, make_result, empty))
    turned = r.first_sums[...].T
    put_sum(shift_one, turned[0:1])
    put_sum(scale_one, turned[1:2])
    sums_first = wires.reserve(3)
    for i, (a, b) in enumerate(seq_peers):
        wires.go(sums_first + i, sums.at[s], sums.at[s], (d, seq_peer(a, b)))
    qkv_reduces[1].along_z(1)
    down_reduce.across()
    qkv_reduces[2].along_z(3)
    qkv_reduces[1].along_z(2)
    qkv_reduces[1].along_z(0)
    out_sum()
    qkv_reduces[2].along_z(1)

    table_sums, table_all = r.table_sums, r.table_all

    def fold(h, _):
        lane = lax.broadcasted_iota(jnp.int32, (1, LANES), 1)
        near = jnp.zeros((LANES, LANES), F32)
        low_end = jnp.zeros((LANES, LANES), F32)
        high_end = jnp.zeros((LANES, LANES), F32)
        for tile in range(2 * n.blocks - 1):
            away = tile - middle_tile
            apart = query_in - key_in - away * LANES
            value = bias[h, tile * LANES : (tile + 1) * LANES]
            if away < -1:
                high_end = high_end + value
            elif away > 1:
                low_end = low_end + value
            else:
                high_end = high_end + jnp.where(apart >= RR, value, 0.0)
                low_end = low_end + jnp.where(apart <= -RR, value, 0.0)
                near = near + jnp.where((apart < RR) & (apart > -RR), value, 0.0)
        line = jnp.sum(skew(near, True), axis=0, keepdims=True)
        for where, array in ((40, low_end), (41, high_end), (42, crossed[h])):
            line = jnp.where(lane == where, jnp.sum(array), line)
        table_sums[d, h] = line
        return 0

    lax.fori_loop(0, heads, fold, 0)
    table_first = wires.reserve(len(dp_peers))
    for i, (k, e) in enumerate(dp_peers):
        wires.go(table_first + i, table_sums.at[d], table_sums.at[d], (dp_peer(k, e)[0], s))

    for i, (a, b) in enumerate(seq_peers):
        place = sums.at[seq_peer(a, b)]
        wires.make(sums_first + i, place, place, (d, seq_peer(a, b))).wait_recv()
    mod_total = sums[0]
    for i in range(1, n.seq):
        mod_total = mod_total + sums[i]
    mod_totals = r.mod_totals
    mod_totals[d] = mod_total
    totals_first = wires.reserve(len(dp_peers))
    for i, (k, e) in enumerate(dp_peers):
        wires.go(totals_first + i, mod_totals.at[d], mod_totals.at[d], (dp_peer(k, e)[0], s))
    qkv_reduces[2].along_z(2)
    qkv_reduces[2].along_z(0)
    gate_up_reduces[0].finish()
    gate_up_reduces[1].finish()
    down_reduce.finish()
    out_reduce.along_z(3)
    first_reduce.wait()

    def first_back(place, _):
        first_grad = first_reduce.total(r.branch, place)
        normal, inverted = layer_norm(r.hidden_own[place, :].astype(F32))
        r.input_grad[place, :] = (
            kept_middle_grad[place, :] + norm_back(first_grad * (1.0 + vector(scale_one)), normal, inverted)
        ).astype(BF16)
        return 0

    by_rows(rows, first_back)
    for k in (1, 2, 0):
        out_reduce.along_z(k)
    for reduce in qkv_reduces:
        reduce.finish()
    for reduce in (*gate_up_reduces, down_reduce):
        reduce.shares.hand_on()
    for i, (k, e) in enumerate(dp_peers):
        place = table_sums.at[dp_peer(k, e)[1]]
        wires.make(table_first + i, place, place, (dp_peer(k, e)[0], s)).wait_recv()
    total = table_sums[0]
    for i in range(1, n.dp):
        total = total + table_sums[i]
    table_all[s] = total
    table_second = wires.reserve(3)
    for i, (a, b) in enumerate(seq_peers):
        wires.go(table_second + i, table_all.at[s], table_all.at[s], (d, seq_peer(a, b)))
    out_reduce.finish()
    for i, (k, e) in enumerate(dp_peers):
        place = mod_totals.at[dp_peer(k, e)[1]]
        wires.make(totals_first + i, place, place, (dp_peer(k, e)[0], s)).wait_recv()
    squashed_rows = r.squashed[pl.ds(pl.multiple_of(d * n.ada_rows, n.ada_rows), n.ada_rows), :]
    ada = squashed_rows[:, 0:1] * mod_totals[0]
    for i in range(1, n.dp):
        ada = ada + squashed_rows[:, i : i + 1] * mod_totals[i]
    r.grad_ada[...] = ada
    for i, (a, b) in enumerate(seq_peers):
        place = table_all.at[seq_peer(a, b)]
        wires.make(table_second + i, place, place, (d, seq_peer(a, b))).wait_recv()
    r.table[...] = table_all[...]
    for reduce in (*qkv_reduces, out_reduce):
        reduce.shares.hand_on()
    for reduce in (*gate_up_reduces, down_reduce, *qkv_reduces, out_reduce):
        reduce.shares.wait()
    wires.finish()


def write_outputs(sizes, inputs, outputs):
    n = sizes
    result, input_grad, grad_ada, table, gate_up0, gate_up1, down, proj, qkv0, qkv1, qkv2 = inputs[:-3]
    pair_embed, pair_gain, pair_weight = inputs[-3:]
    o_result, o_input, o_qkv, o_out, o_gate_up, o_down, o_ada, o_embed, o_gain, o_pair = outputs
    o_result[...] = result[...]
    o_input[...] = input_grad[...]
    o_ada[...] = grad_ada[...]
    everyone = range(n.seq)
    for kind in range(3):
        for side in range(2):
            low = (3 * side + kind) * DH
            o_qkv[side * n.half : (side + 1) * n.half, kind * n.width : (kind + 1) * n.width] = jnp.concatenate(
                [head[q, :, low : low + DH] for q in everyone for head in (qkv0, qkv1, qkv2)], axis=1
            ).astype(F32)
    group = n.seq * n.strip
    for number in range(2 * n.dp):
        side, block = divmod(number % n.dp, n.dp // 2)
        low = (number // n.dp) * (n.hidden // 2) + block * n.strip
        gate_up = (gate_up0, gate_up1)[side]
        o_gate_up[:, number * group : (number + 1) * group] = jnp.concatenate(
            [gate_up[q, :, low : low + n.strip] for q in everyone], axis=1
        ).astype(F32)
    for q in everyone:
        o_down[q * n.strip : (q + 1) * n.strip, :] = down[q].astype(F32)
        side, core = divmod(q, 2)
        lanes = slice(side * (n.width // 2), (side + 1) * (n.width // 2))
        o_out[core * n.half : (core + 1) * n.half, lanes] = proj[q].astype(F32)

    lines = jnp.concatenate([table[q, h] for q in everyone for h in range(n.heads)], axis=0)
    lane = lax.broadcasted_iota(jnp.int32, lines.shape, 1)
    table_t = jnp.where(lane < 2 * RR, pltpu.roll(lines, RR, 1), 0.0)
    for number, at in ((0, 40), (2 * RR, 41), (CLASSES - 1, 42)):
        table_t = jnp.where(lane == number, jnp.broadcast_to(lines[:, at : at + 1], lines.shape), table_t)
    embed = pair_embed[...].astype(F32)
    embed = jnp.concatenate([embed, jnp.zeros((LANES - CLASSES, embed.shape[1]), F32)], axis=0)
    gain = pair_gain[...].astype(F32)
    normal, inverted = layer_norm(embed, 1e-05)

    def exact(a, b):
        return jnp.dot(a, b, precision=HIGHEST, preferred_element_type=F32)

    o_pair[...] = exact(table_t, normal * gain)
    scaled_grad = exact(table_t.T, pair_weight[...].astype(F32))
    o_gain[...] = jnp.sum(scaled_grad * normal, axis=0)
    o_embed[...] = norm_back(scaled_grad * gain, normal, inverted)[0:CLASSES]


def fused_layer(
    sizes, valid_len, chain_break, hidden, out_grad, condition, qkv, out, gate_up, down, ada, embed, gain, weight
):
    n = sizes
    rows, width, length, heads, part, hid = n.rows, n.width, n.length, n.heads, n.part, n.hidden
    any_space, vmem, smem = pl.ANY, pltpu.VMEM, pltpu.SMEM
    inputs = dict(
        valid_len=(valid_len, smem),
        chain_break=(chain_break, smem),
        hidden=(hidden, any_space),
        out_grad=(out_grad, any_space),
        condition=(condition, vmem),
        qkv=(qkv, any_space),
        out=(out, any_space),
        gate_up=(gate_up, any_space),
        down=(down, any_space),
        ada=(ada, vmem),
        pair_embed=(embed, vmem),
        pair_gain=(gain, vmem),
        pair_weight=(weight, vmem),
    )
    modulations = 6 * width

    def reduced(height, columns):
        return (
            ((2, n.far, height, columns), BF16),
            ((n.far, height, columns), BF16),
            ((n.far - 1, height, columns), BF16),
            ((height, columns), BF16),
            ((height, columns), BF16),
        )

    def shares(height, columns):
        return (n.seq, height, columns), BF16, any_space

    sums = ((2, rows, width), BF16), ((2, rows, width), BF16), ((rows, width), BF16), ((rows, width), BF16)
    gate_up_sizes, down_sizes = (n.shard, hid), (n.strip, width)
    proj_sizes, qkv_sizes = (n.half, width // 2), (n.half, 6 * DH)
    outputs = dict(
        result=((rows, width), BF16, vmem),
        input_grad=((rows, width), BF16, vmem),
        grad_ada=((n.ada_rows, modulations), F32, vmem),
        table=((n.seq, heads, 1, LANES), F32, vmem),
        gate_up0_share=shares(*gate_up_sizes),
        gate_up1_share=shares(*gate_up_sizes),
        down_share=shares(*down_sizes),
        proj_share=shares(*proj_sizes),
        qkv0_share=shares(*qkv_sizes),
        qkv1_share=shares(*qkv_sizes),
        qkv2_share=shares(*qkv_sizes),
    )
    scratch = dict(
        w_qkv=((width, 3 * part), BF16),
        w_out=((n.dp, 2, n.half, width), BF16),
        w_gate_up=((width, 2 * hid), BF16),
        w_down=((hid, width), BF16),
        hidden_all=((length, width), BF16),
        grads_all=((length, width), BF16),
        hidden_own=((rows, width), BF16),
        upstream=((rows, width), BF16),
        cond_all=((n.dp, 8, n.conditioning), F32),
        squashed=((n.conditioning, n.dp), F32),
        mod_send=((n.dp, 1, modulations), F32),
        mod_recv=((n.dp, 1, modulations), F32),
        modulation=((1, modulations), F32),
        mod_sums=((n.seq, 1, modulations), F32),
        mod_totals=((n.dp, 1, modulations), F32),
        bias=((heads, (2 * n.blocks - 1) * LANES, LANES), F32),
        crossed=((heads, 1, LANES), F32),
        table_t=((H, LANES), F32),
        table_sums=((n.dp, heads, 1, LANES), F32),
        table_all=((n.seq, heads, 1, LANES), F32),
        keys=((heads, length, DH), BF16),
        keys_t=((heads, n.seq, DH, rows), BF16),
        values_t=((heads, n.seq, DH, rows), BF16),
        queries_t=((heads, n.seq, DH, rows), BF16),
        exps=((heads, n.seq, length, rows), BF16),
        outs_t=((heads, n.seq, DH, rows), F32),
        inverse=((heads, n.seq, 1, rows), F32),
        mixed_send=((n.seq, rows, part), BF16),
        mixed_recv=((n.seq, rows, part), BF16),
        back_recv=((n.seq, rows, part), BF16),
        branch=((rows, width), F32),
        middle=((rows, width), F32),
        feed_own=((rows, width), F32),
        second_own=((rows, width), F32),
        branch_grad=((rows, width), BF16),
        second_all=((length, width), BF16),
        second_t=((width, length), BF16),
        norm_t=((width, length), BF16),
        mod_t=((width, 8), F32),
        first_sums=((width, LANES), F32),
        inner=((length, hid), BF16),
        inner_t=((hid, length), BF16),
        gate_up_grads=((length, 2 * hid), BF16),
        out_near=((n.dp * n.half, width), BF16),
        out_far=((n.dp * n.half, width // 2), BF16),
        raw=((length, hid // 2), F32),
        dots_t=((heads, n.seq, DH, rows), BF16),
        delta=((heads, n.seq, 1, rows), F32),
        pair_grads=((length, 2 * DH), F32),
        query_grads=((length, DH), BF16),
        feed_sib=sums[0],
        feed_got=sums[1],
        feed_over=sums[2],
        feed_come=sums[3],
        second_sib=sums[0],
        second_got=sums[1],
        second_over=sums[2],
        second_come=sums[3],
        gate_up0_grad=reduced(*gate_up_sizes)[0],
        gate_up0_got=reduced(*gate_up_sizes)[1],
        gate_up0_come=reduced(*gate_up_sizes)[2],
        gate_up0_far=reduced(*gate_up_sizes)[3],
        gate_up0_mine=reduced(*gate_up_sizes)[4],
        gate_up1_grad=reduced(*gate_up_sizes)[0],
        gate_up1_got=reduced(*gate_up_sizes)[1],
        gate_up1_come=reduced(*gate_up_sizes)[2],
        gate_up1_far=reduced(*gate_up_sizes)[3],
        gate_up1_mine=reduced(*gate_up_sizes)[4],
        proj_grad=reduced(*proj_sizes)[0],
        proj_got=reduced(*proj_sizes)[1],
        proj_come=reduced(*proj_sizes)[2],
        proj_far=reduced(*proj_sizes)[3],
        proj_mine=reduced(*proj_sizes)[4],
        qkv0_grad=reduced(*qkv_sizes)[0],
        qkv0_got=reduced(*qkv_sizes)[1],
        qkv0_come=reduced(*qkv_sizes)[2],
        qkv0_far=reduced(*qkv_sizes)[3],
        qkv0_mine=reduced(*qkv_sizes)[4],
        qkv1_grad=reduced(*qkv_sizes)[0],
        qkv1_got=reduced(*qkv_sizes)[1],
        qkv1_come=reduced(*qkv_sizes)[2],
        qkv1_far=reduced(*qkv_sizes)[3],
        qkv1_mine=reduced(*qkv_sizes)[4],
        qkv2_grad=reduced(*qkv_sizes)[0],
        qkv2_got=reduced(*qkv_sizes)[1],
        qkv2_come=reduced(*qkv_sizes)[2],
        qkv2_far=reduced(*qkv_sizes)[3],
        qkv2_mine=reduced(*qkv_sizes)[4],
        down_grad=reduced(*down_sizes)[0],
        down_come=((n.far - 1, 2, *down_sizes), BF16),
        down_far=((2, *down_sizes), BF16),
        down_got=(down_sizes, BF16),
        down_mine=(down_sizes, BF16),
    )
    semaphores = dict(send_sem=210, recv_sem=210, local_sem=21)
    names = [*inputs, *outputs, *scratch, *semaphores]
    made = pl.pallas_call(
        functools.partial(layer_kernel, n, names),
        out_shape=[jax.ShapeDtypeStruct(shape, kind) for shape, kind, _ in outputs.values()],
        in_specs=[pl.BlockSpec(memory_space=space) for _, space in inputs.values()],
        out_specs=[pl.BlockSpec(memory_space=space) for _, _, space in outputs.values()],
        scratch_shapes=[pltpu.VMEM(shape, kind) for shape, kind in scratch.values()]
        + [pltpu.SemaphoreType.DMA((count,)) for count in semaphores.values()],
        compiler_params=pltpu.CompilerParams(
            collective_id=0, has_side_effects=True, vmem_limit_bytes=VMEM_LIMIT
        ),
    )(*[array for array, _ in inputs.values()])
    gradients = (
        ((rows, width), BF16),
        ((rows, width), BF16),
        ((n.shard, 3 * width), F32),
        ((n.shard, width), F32),
        ((n.shard, 2 * n.seq * hid), F32),
        ((n.seq * n.strip, width), F32),
        ((n.ada_rows, modulations), F32),
        (embed.shape, F32),
        (gain.shape, F32),
        (weight.shape, F32),
    )
    count = len(made) + 3

    def write(*refs):
        write_outputs(n, refs[:count], refs[count:])

    return pl.pallas_call(
        write,
        out_shape=[jax.ShapeDtypeStruct(shape, kind) for shape, kind in gradients],
        in_specs=[pl.BlockSpec(memory_space=vmem)] * count,
        out_specs=[pl.BlockSpec(memory_space=vmem)] * len(gradients),
        compiler_params=pltpu.CompilerParams(vmem_limit_bytes=VMEM_LIMIT),
    )(*made, embed, gain, weight)


def fused_body(
    hidden_in,
    condition,
    qkv_weight,
    out_weight,
    gate_up_weight,
    down_weight,
    ada_weight,
    pair_embed,
    pair_gain,
    pair_weight,
    valid_len,
    chain_break,
    out_grad,
):
    _, rows, width = hidden_in.shape
    seq = lax.axis_size("seq")
    dp = lax.axis_size("dp")
    shard = qkv_weight.shape[0]
    sizes = Sizes(
        rows, width, seq, dp, shard, down_weight.shape[0], ada_weight.shape[0], condition.shape[1]
    )
    outs = fused_layer(
        sizes,
        valid_len,
        chain_break,
        hidden_in[0],
        out_grad[0],
        condition,
        qkv_weight,
        out_weight,
        gate_up_weight,
        down_weight,
        ada_weight,
        pair_embed,
        pair_gain,
        pair_weight.T,
    )
    result, input_grad, *grads, grad_gain, grad_pair = outs
    return (result[None], input_grad[None], *grads, grad_gain, grad_pair.T)


def body(*arguments):
    hidden_in, _, qkv_weight, _, _, down_weight = arguments[:6]
    seq, dp = lax.axis_size("seq"), lax.axis_size("dp")
    whole_tiles = qkv_weight.shape[0] % 32 == 0 and down_weight.shape[0] % (16 * seq) == 0
    if whole_tiles and hidden_in.shape[0] == 1 and seq == 4 and dp == 8:
        return fused_body(*arguments)
    return plain_body(*arguments)


def solution(mesh):
    rows = P("dp", "seq", None)
    share = P("dp", None)
    return jax.shard_map(
        body,
        mesh=mesh,
        in_specs=(rows, share, share, share, share, share, share, P(), P(), P(), P("dp"), P("dp"), rows),
        out_specs=(rows, rows, share, share, share, share, share, P(), P(), P()),
        check_vma=False,
    )
```
